32 devices in a mesh: dp: 4 (over y, core), seq: 8 (over z, x).
Axes of the slice: x: 2, y: 2, z: 4, core: 2. Of those that a mesh axis runs over, the one named last changes fastest.
Arguments:
- stream: bfloat16 [48, 1024, 512], P('dp', 'seq'), may hold values from -6 to 6
- encoder: bfloat16 [48, 1024, 512], P('dp', 'seq'), may hold values from -6 to 6
- cotangent: bfloat16 [48, 1024, 512], P('dp', 'seq'), may hold values from -6 to 6
- self_qkv: bfloat16 [512, 1536], replicated, may hold values from -0.25 to 0.25
- self_out: bfloat16 [512, 512], replicated, may hold values from -1 to 1
- cross_q: bfloat16 [512, 512], replicated, may hold values from -0.25 to 0.25
- cross_kv: bfloat16 [512, 1024], replicated, may hold values from -0.25 to 0.25
- cross_out: bfloat16 [512, 512], replicated, may hold values from -1 to 1
- ffn_in: bfloat16 [512, 2048], P(None, 'seq'), may hold values from -0.25 to 0.25
- ffn_out: bfloat16 [2048, 512], P('seq'), may hold values from -0.125 to 0.125
- norm_gain: float32 [3, 512], replicated, may hold values from 0.25 to 1.75
- norm_bias: float32 [3, 512], replicated, may hold values from -0.5 to 0.5
- lengths: int32 [48, 128], P('dp'), may hold values from 0 to 1024, as said below
- enc_lengths: int32 [48, 128], P('dp'), may hold values from 0 to 1024, as said below
- ranks: int32 [48, 1024], P('dp', 'seq'), may hold values from 0 to 15
- cuts: int32 [48, 1024], P('dp', 'seq'), may hold values from 1 to 16
Outputs:
- output: bfloat16 [48, 1024, 512], P('dp', 'seq')
- stream_grad: float32 [48, 1024, 512], P('dp', 'seq')
- encoder_grad: float32 [48, 1024, 512], P('dp', 'seq')
- self_qkv_grad: float32 [512, 1536], replicated
- self_out_grad: float32 [512, 512], replicated
- cross_q_grad: float32 [512, 512], replicated
- cross_kv_grad: float32 [512, 1024], replicated
- cross_out_grad: float32 [512, 512], replicated
- ffn_in_grad: float32 [512, 2048], P(None, 'seq')
- ffn_out_grad: float32 [2048, 512], P('seq')
- gain_grad: float32 [3, 512], replicated
- bias_grad: float32 [3, 512], replicated
The draws below stay inside these ranges and needn't reach their ends.
Inputs may be any that keep to these rules, and one draw needn't show every extreme that they name: `lengths`: each row sums to 1024; entries after a row's last document are 0; in each aligned block of 12 rows one row is a single document of 1024 tokens; documents of the other rows have at most max(512, 55) tokens. `enc_lengths`: entry k is 0 where lengths' entry k is 0, else between 1 and lengths' entry k and at least three quarters of it, rounded down; a single document of 1024 tokens has a source of 1024 tokens.
All inputs are finite; a program needn't handle non-finite values.
Results may differ from the reference program's by a relative error of at most 0.02.
Values may be sent and summed in bfloat16 or wider, within the bound.
A program may use at most 448 MiB of HBM per device.

```python
import jax
import jax.numpy as jnp
from jax import lax

D = 512
HEADS = 8
HEAD = 64
FF = 2048
LINE = 1024
LINES = 12
ROWS = 48
DOCS = 128


def target_lengths(key):
    raw_key, first_key, whole_key = jax.random.split(key, 3)
    raw = jax.random.randint(raw_key, (ROWS, DOCS), 8, 56)
    opening = jax.random.randint(first_key, (ROWS, 1), LINE // 8, LINE // 2 + 1)
    column = jnp.arange(DOCS, dtype=jnp.int32)[None, :]
    raw = jnp.where(column == 0, opening, raw)
    before = jnp.cumsum(raw, axis=1) - raw
    trimmed = jnp.clip(LINE - before, 0, raw)
    chosen = jax.random.randint(whole_key, (ROWS // LINES, 1), 0, LINES)
    within = (jnp.arange(ROWS, dtype=jnp.int32) % LINES).reshape(ROWS // LINES, LINES)
    whole = (within == chosen).reshape(ROWS, 1)
    single = jnp.where(column == 0, LINE, 0)
    return jnp.where(whole, single, trimmed).astype(jnp.int32)


def draw_lengths(key, part):
    shared = target_lengths(key)
    return shared


def draw_enc_lengths(key, part):
    shared = target_lengths(key)
    key = jax.random.fold_in(key, 7)
    shave = jax.random.randint(key, shared.shape, 0, shared // 4 + 1)
    whole = shared[:, :1] == LINE
    source = jnp.where(shared > 0, jnp.maximum(1, shared - shave), 0)
    return jnp.where(whole, shared, source).astype(jnp.int32)


def set_ends(array, key, smallest, top_value):
    extent = array.shape
    place = [jax.random.randint(jax.random.fold_in(key, axis), (), 0, extent[axis]) for axis in range(len(extent))]
    array = array.at[tuple(place)].set(smallest)
    longest = extent.index(max(extent))
    place[longest] = (place[longest] + 1) % extent[longest]
    return array.at[tuple(place)].set(top_value)


def levels(own_key, shape, pieces, least, top_value):
    gain, own = 1.0, jax.random.fold_in(own_key, 6)
    for position, parts in pieces:
        heights = jnp.exp(jax.random.uniform(jax.random.fold_in(own, position), (parts,), jnp.float32, least / len(pieces), top_value / len(pieces)))
        gain = gain * jnp.repeat(heights, shape[position] // parts).reshape([-1 if axis == position else 1 for axis in range(len(shape))])
    return gain


def gaussian(stream_key, extent, deviation, limit, cuts=(), kind=jnp.bfloat16):
    values = jax.random.normal(stream_key, extent, jnp.float32) * deviation
    if len(cuts) > 0:
        values = levels(stream_key, extent, cuts, -0.22, 0.18) * values
    return jnp.clip(values, min=-limit, max=limit).astype(kind)


def setup_inputs(seed: int = 0) -> dict:
    keys = jax.random.split(jax.random.key(seed), 17)
    stream = gaussian(keys[0], (ROWS, LINE, D), 1.0, 6.0, ((0, 4), (1, 8)))
    encoder = gaussian(keys[1], (ROWS, LINE, D), 1.0, 6.0, ((0, 4), (1, 8)))
    cotangent = gaussian(keys[2], (ROWS, LINE, D), 1.0, 6.0, ((0, 4), (1, 8)))
    self_qkv = gaussian(keys[3], (D, 3 * D), D ** -0.5, 0.25)
    self_out = gaussian(keys[4], (D, D), (D // 16) ** -0.5, 1.0)
    cross_q = gaussian(keys[5], (D, D), D ** -0.5, 0.25)
    cross_kv = gaussian(keys[6], (D, 2 * D), D ** -0.5, 0.25)
    cross_out = gaussian(keys[7], (D, D), (D // 16) ** -0.5, 1.0)
    ffn_in = gaussian(keys[8], (D, FF), D ** -0.5, 0.25, ((1, 8),))
    ffn_out = gaussian(keys[9], (FF, D), FF ** -0.5, 0.125, ((0, 8),))
    norm_gain = jnp.clip(1.0 + 0.15 * jax.random.normal(keys[10], (3, D), jnp.float32), 0.25, 1.75)
    norm_bias = jnp.clip(jax.random.uniform(keys[11], (3, D), jnp.float32, -0.5, 0.5), -0.5, 0.5)
    lengths = draw_lengths(jax.random.fold_in(keys[16], 71), 0)
    enc_lengths = draw_enc_lengths(jax.random.fold_in(keys[16], 71), 0)
    ranks = set_ends(jax.random.randint(keys[14], (ROWS, LINE), 0, 16), jax.random.fold_in(keys[14], 1), 0, 15).astype(jnp.int32)
    cuts = set_ends(jax.random.randint(keys[15], (ROWS, LINE), 1, 17), jax.random.fold_in(keys[15], 1), 1, 16).astype(jnp.int32)
    return {"stream": stream, "encoder": encoder, "cotangent": cotangent, "self_qkv": self_qkv, "self_out": self_out, "cross_q": cross_q, "cross_kv": cross_kv, "cross_out": cross_out, "ffn_in": ffn_in, "ffn_out": ffn_out, "norm_gain": norm_gain, "norm_bias": norm_bias, "lengths": lengths, "enc_lengths": enc_lengths, "ranks": ranks, "cuts": cuts}


@jax.custom_vjp
def low(v):
    return lax.optimization_barrier(v.astype(jnp.bfloat16)).astype(jnp.float32)

@jax.custom_vjp
def low_back(v):
    return v

def low_keep(v):
    return (low(v), None)

def low_pass(kept, grad):
    return (grad,)

def back_keep(v):
    return (v, None)

def back_low(kept, grad):
    return (low(grad),)
low.defvjp(low_keep, low_pass)
low_back.defvjp(back_keep, back_low)
HIGHEST_PRECISION = lax.Precision.HIGHEST
NEGATIVE_FILL = -1e+30
EPSILON = 1e-05

def product(left, right):
    return jnp.dot(left, right, precision=HIGHEST_PRECISION)

def layer_norm(tensor, gain_row, bias_row):
    centred = tensor - lax.optimization_barrier(jnp.mean(tensor, axis=-1, keepdims=True))
    variance = lax.optimization_barrier(jnp.mean(centred * centred, axis=-1, keepdims=True))
    return centred * lax.rsqrt(variance + EPSILON) * gain_row + bias_row

def doc_numbers(lengths):
    bounds = jnp.cumsum(lengths)
    places = jnp.arange(LINE, dtype=jnp.int32)
    return lax.optimization_barrier(jnp.sum((bounds[None, :] <= places[:, None]).astype(jnp.int32), axis=1))

def to_heads(tensor):
    return tensor.reshape(LINE, HEADS, HEAD).transpose(1, 0, 2)

def attend(queries, keys_part, values, allowed):
    raw = jnp.einsum('hqd,hkd->hqk', to_heads(queries), to_heads(keys_part), precision=HIGHEST_PRECISION)
    scores = low_back(raw * HEAD ** (-0.5))
    scores = jnp.where(allowed[None], scores, NEGATIVE_FILL)
    probabilities = low(jax.nn.softmax(scores, axis=-1))
    mixed = jnp.einsum('hqk,hkd->hqd', probabilities, to_heads(values), precision=HIGHEST_PRECISION)
    return mixed.transpose(1, 0, 2).reshape(LINE, D)

def line_layer(stream_line, encoder_line, length_line, source_line, rank_line, cut_line, params):
    self_qkv, self_out, cross_q, cross_kv, cross_out, ffn_in, ffn_out, norm_gain, norm_bias = params
    doc_ids = doc_numbers(length_line)
    source_ids = doc_numbers(source_line)
    places = jnp.arange(LINE, dtype=jnp.int32)
    self_allowed = (doc_ids[:, None] == doc_ids[None, :]) & ((rank_line[None, :] < cut_line[:, None]) | (places[:, None] == places[None, :]))
    cross_allowed = doc_ids[:, None] == source_ids[None, :]
    projected = low(low_back(product(stream_line, self_qkv)))
    attended = low(low_back(attend(projected[:, :D], projected[:, D:2 * D], projected[:, 2 * D:], self_allowed)))
    first_out = layer_norm(stream_line + low_back(product(attended, self_out)), norm_gain[0], norm_bias[0])
    cross_queries = low(low_back(product(low(first_out), cross_q)))
    memory = low(low_back(product(encoder_line, cross_kv)))
    cross_att = low(low_back(attend(cross_queries, memory[:, :D], memory[:, D:], cross_allowed)))
    second = layer_norm(first_out + low_back(product(cross_att, cross_out)), norm_gain[1], norm_bias[1])
    pre_act = low_back(product(low(second), ffn_in))
    hidden = low(jax.nn.gelu(pre_act))
    return layer_norm(second + low_back(product(hidden, ffn_out)), norm_gain[2], norm_bias[2])

def reference(stream, encoder, cotangent, self_qkv, self_out, cross_q, cross_kv, cross_out, ffn_in, ffn_out, norm_gain, norm_bias, lengths, enc_lengths, ranks, cuts):
    params = tuple((item.astype(jnp.float32) for item in (self_qkv, self_out, cross_q, cross_kv, cross_out, ffn_in, ffn_out, norm_gain, norm_bias)))

    def grouped(tensor):
        return tensor.reshape((ROWS // 2, 2) + tensor.shape[1:])

    def step(totals, items):
        stream_pair, encoder_pair, cot_pair, length_pair, source_pair, rank_pair, cut_pair = items

        def run(stream_float, encoder_float, weights):

            def one_line(stream_one, encoder_one, length_one, source_one, rank_one, cut_one):
                return line_layer(stream_one, encoder_one, length_one, source_one, rank_one, cut_one, weights)
            return jax.vmap(one_line)(stream_float, encoder_float, length_pair, source_pair, rank_pair, cut_pair)
        result, pull_back = jax.vjp(run, stream_pair.astype(jnp.float32), encoder_pair.astype(jnp.float32), params)
        stream_back, encoder_back, weight_back = pull_back(cot_pair.astype(jnp.float32))
        return (jax.tree.map(jnp.add, totals, weight_back), (result.astype(jnp.bfloat16), stream_back, encoder_back))
    start = jax.tree.map(jnp.zeros_like, params)
    items = (grouped(stream), grouped(encoder), grouped(cotangent), grouped(lengths), grouped(enc_lengths), grouped(ranks), grouped(cuts))
    totals, (outputs, stream_grads, encoder_grads) = lax.scan(step, start, items)
    return (outputs.reshape(ROWS, LINE, D), stream_grads.reshape(ROWS, LINE, D), encoder_grads.reshape(ROWS, LINE, D), totals[0], totals[1], totals[2], totals[3], totals[4], totals[5], totals[6], totals[7], totals[8])
```

```python
import functools
import math

import jax
import jax.numpy as jnp
from jax import lax
from jax.experimental import pallas as pl
from jax.experimental.pallas import tpu as pltpu
from jax.sharding import PartitionSpec as P

D = 512
HEADS = 8
HEAD = 64
PAIR = 2 * HEAD
NEGATIVE_FILL = -1e30
EPSILON = 1e-05
SCALE = HEAD ** (-0.5)
BLOCK = 256
SUB = 128
BF = jnp.bfloat16
F32 = jnp.float32
NT = (((1,), (1,)), ((), ()))
GELU_C = math.sqrt(2.0 / math.pi)
VMEM = 60 * 1024 * 1024


def mm(left, right):
    return jnp.dot(left, right, preferred_element_type=F32)


def mm_nt(left, right):
    return lax.dot_general(left, right, NT, preferred_element_type=F32)


def plan(lines, n):
    whole = lines // n
    rest = lines - whole * n
    groups = math.gcd(rest, n) if rest else n
    return whole, n // groups, rest // groups


def widths_for(line_len):
    return tuple(w for w in (256, 384, 512, 768) if w < line_len) + (line_len,)


def norm_stats(r):
    centred = r - jnp.mean(r, axis=-1, keepdims=True)
    inv = lax.rsqrt(jnp.mean(centred * centred, axis=-1, keepdims=True) + EPSILON)
    return centred * inv, inv


def norm_back(dy, normed, inv, gain):
    scaled = dy * gain
    inner = (
        scaled
        - jnp.mean(scaled, axis=-1, keepdims=True)
        - normed * jnp.mean(scaled * normed, axis=-1, keepdims=True)
    )
    return inner * inv


def fold8(t):
    return jnp.sum(t.reshape(t.shape[0] // 8, 8, t.shape[1]), axis=0)


def head_lanes(half):
    lane = lax.broadcasted_iota(jnp.int32, (1, PAIR), 1)
    return (lane < HEAD) if half == 0 else (lane >= HEAD)


def query_meta(mk, at):
    return mk[0, :, pl.ds(at, SUB)].T


def self_mask(mk, meta, at, ks, wd):
    doc = mk[0, 0:1, pl.ds(ks, wd)] == meta[:, 0:1]
    low = mk[0, 1:2, pl.ds(ks, wd)] < meta[:, 2:3]
    key = lax.broadcasted_iota(jnp.int32, (SUB, wd), 1) + ks
    query = lax.broadcasted_iota(jnp.int32, (SUB, wd), 0) + at
    return doc & (low | (key == query))


def cross_mask(mk, meta, at, ks, wd):
    return mk[0, 3:4, pl.ds(ks, wd)] == meta[:, 0:1]


def by_width(var, ks, widths, run):
    for index, wd in enumerate(widths):

        @pl.when(var == index)
        def _(wd=wd):
            run(pl.multiple_of(ks, SUB), wd)


def attend(q, kv, mask, ks, wd, put_out, put_prob, put_lse):
    lane = lax.broadcasted_iota(jnp.int32, (SUB, 128), 1)
    lse = jnp.zeros((SUB, 128), F32)
    for pair in range(HEADS // 2):
        cols = slice(pair * PAIR, (pair + 1) * PAIR)
        keys = kv[pl.ds(ks, wd), cols]
        vals = kv[pl.ds(ks, wd), D + pair * PAIR : D + (pair + 1) * PAIR]
        outs = []
        for half in range(2):
            head = 2 * pair + half
            qm = jnp.where(head_lanes(half), q[:, cols], jnp.zeros((), BF))
            s = jnp.where(mask, mm_nt(qm, keys), NEGATIVE_FILL)
            top = jnp.max(s, axis=-1, keepdims=True)
            e = jnp.exp(s - top)
            total = jnp.sum(e, axis=-1, keepdims=True)
            prob = (e * (1.0 / total)).astype(BF)
            if put_prob is not None:
                put_prob(head, prob)
            if put_lse is not None:
                lse = jnp.where(lane == head, top + jnp.log(total), lse)
            outs.append(mm(prob, vals))
        put_out(cols, jnp.where(head_lanes(0), outs[0], outs[1]).astype(BF))
    if put_lse is not None:
        put_lse(lse)


def attend_back(q, g, kv, get_prob, ks, wd, acc, put_dq):
    qt, gt = q.T, g.T
    for pair in range(HEADS // 2):
        cols = slice(pair * PAIR, (pair + 1) * PAIR)
        keys = kv[pl.ds(ks, wd), cols]
        vals = kv[pl.ds(ks, wd), D + pair * PAIR : D + (pair + 1) * PAIR]
        outs = []
        for half in range(2):
            head = 2 * pair + half
            rows = slice(head * HEAD, (head + 1) * HEAD)
            gm = jnp.where(head_lanes(half), g[:, cols], jnp.zeros((), BF))
            dp = mm_nt(gm, vals)
            prob, low = get_prob(head, half, cols, keys)
            ds = (prob * (dp - jnp.sum(prob * dp, axis=-1, keepdims=True))).astype(BF)
            outs.append(mm(ds, keys))
            acc[rows, pl.ds(ks, wd)] += mm(qt[rows, :], ds)
            vrows = slice(D + head * HEAD, D + (head + 1) * HEAD)
            acc[vrows, pl.ds(ks, wd)] += mm(gt[rows, :], low)
        put_dq(cols, (jnp.where(head_lanes(0), outs[0], outs[1]) * SCALE).astype(BF))


def self_forward(widths, tab, xs, mk, wqkv, wso, kv, q_out, att_out, n0_out, s0_out, lse_out):
    b = pl.program_id(0)
    row0 = pl.multiple_of(tab[1, b], SUB)

    @pl.when(tab[2, b] == 1)
    def _():
        @pl.loop(0, kv.shape[1] // BLOCK)
        def _(i):
            rows = pl.ds(pl.multiple_of(i * BLOCK, BLOCK), BLOCK)
            kv[0, rows, :] = mm(xs[0, rows, :], wqkv[:, D:]).astype(BF)

    x = xs[0, pl.ds(row0, BLOCK), :]
    q_out[...] = mm(x, wqkv[:, :D]).astype(BF) * jnp.asarray(SCALE, BF)
    for sub in range(BLOCK // SUB):
        at = pl.multiple_of(row0 + sub * SUB, SUB)
        here = slice(sub * SUB, (sub + 1) * SUB)
        meta = query_meta(mk, at)

        def put_out(cols, value, here=here):
            att_out[here, cols] = value

        def put_lse(value, here=here):
            lse_out[here, :] = value

        def run(ks, wd, meta=meta, at=at, here=here, put_out=put_out, put_lse=put_lse):
            mask = self_mask(mk, meta, at, ks, wd)
            attend(q_out[here, :], kv.at[0], mask, ks, wd, put_out, None, put_lse)

        by_width(tab[5, 2 * b + sub], tab[4, 2 * b + sub], widths, run)
    r = x.astype(F32) + mm(att_out[...], wso[...])
    normed, inv = norm_stats(r)
    n0_out[...] = normed
    s0_out[...] = jnp.broadcast_to(inv, s0_out.shape)


def middle(
    widths, ff, tab, es, mk, n0, s0, att, cot, wckv, wso, wcq, wco, w1, w2, gains, biases,
    out, gfirst, gself, dkv, dw1, dw2t, dwco, dwcq, dwso, gb,
    mkv, acc, probs, catt, cq_scr, gatt, dq_scr, hid, gprime,
):
    b = pl.program_id(0)
    row0 = pl.multiple_of(tab[1, b], SUB)

    @pl.when(b == 0)
    def _():
        for ref in (dw1, dw2t, dwco, dwcq, dwso, gb):
            ref[...] = jnp.zeros_like(ref)

    @pl.when(tab[2, b] == 1)
    def _():
        acc[...] = jnp.zeros_like(acc)

        @pl.loop(0, mkv.shape[0] // BLOCK)
        def _(i):
            rows = pl.ds(pl.multiple_of(i * BLOCK, BLOCK), BLOCK)
            mkv[rows, :] = mm(es[0, rows, :], wckv[...]).astype(BF)

    first = n0[...] * gains[0:1, :] + biases[0:1, :]
    first_low = first.astype(BF)
    cq_scr[...] = mm(first_low, wcq[...]).astype(BF) * jnp.asarray(SCALE, BF)
    for sub in range(BLOCK // SUB):
        at = pl.multiple_of(row0 + sub * SUB, SUB)
        here = slice(sub * SUB, (sub + 1) * SUB)
        meta = query_meta(mk, at)

        def run(ks, wd, meta=meta, at=at, here=here, sub=sub):
            def put_out(cols, value):
                catt[here, cols] = value

            def put_prob(head, value):
                probs[sub, head, :, :wd] = value

            mask = cross_mask(mk, meta, at, ks, wd)
            attend(cq_scr[here, :], mkv, mask, ks, wd, put_out, put_prob, None)

        by_width(tab[7, 2 * b + sub], tab[6, 2 * b + sub], widths, run)

    n1, s1 = norm_stats(first + mm(catt[...], wco[...]))
    second = n1 * gains[1:2, :] + biases[1:2, :]
    second_low = second.astype(BF)
    chunk = D
    total = second
    for c in range(ff // chunk):
        cols = slice(c * chunk, (c + 1) * chunk)
        v = mm(second_low, w1[:, cols])
        v2 = v * v
        t = jnp.tanh(GELU_C * (v + 0.044715 * (v2 * v)))
        half = 0.5 * (1.0 + t)
        h = (v * half).astype(BF)
        hid[:, cols] = h
        gprime[:, cols] = half + (0.5 * v) * (1.0 - t * t) * (GELU_C + (3 * 0.044715 * GELU_C) * v2)
        total = total + mm(h, w2[cols, :])
    n2, s2 = norm_stats(total)
    out[...] = (n2 * gains[2:3, :] + biases[2:3, :]).astype(BF)
    dy = cot[...].astype(F32)
    gb[2] += fold8(dy * n2)
    gb[5] += fold8(dy)
    gthird = norm_back(dy, n2, s2, gains[2:3, :])
    fg = gthird.astype(BF)
    fgt, sect = fg.T, second_low.T
    back = gthird
    for c in range(ff // chunk):
        cols = slice(c * chunk, (c + 1) * chunk)
        pg = (mm_nt(fg, w2[cols, :]) * gprime[:, cols]).astype(BF)
        dw2t[:, cols] += mm(fgt, hid[:, cols])
        dw1[:, cols] += mm(sect, pg)
        back = back + mm_nt(pg, w1[:, cols])
    gb[1] += fold8(back * n1)
    gb[4] += fold8(back)
    gsecond = norm_back(back, n1, s1, gains[1:2, :])
    cg = gsecond.astype(BF)
    dwco[...] += mm(catt[...].T, cg)
    gatt[...] = mm_nt(cg, wco[...]).astype(BF)
    for sub in range(BLOCK // SUB):
        here = slice(sub * SUB, (sub + 1) * SUB)

        def run_back(ks, wd, here=here, sub=sub):
            def get_prob(head, half, cols, keys):
                low = probs[sub, head, :, :wd]
                return low.astype(F32), low

            def put_dq(cols, value):
                dq_scr[here, cols] = value

            attend_back(cq_scr[here, :], gatt[here, :], mkv, get_prob, ks, wd, acc, put_dq)

        by_width(tab[7, 2 * b + sub], tab[6, 2 * b + sub], widths, run_back)

    dq = dq_scr[...]
    dwcq[...] += mm(first_low.T, dq)
    gf = gsecond + mm_nt(dq, wcq[...])
    gb[0] += fold8(gf * n0[...])
    gb[3] += fold8(gf)
    gf = norm_back(gf, n0[...], s0[:, 0:1], gains[0:1, :])
    gfirst[...] = gf
    sg = gf.astype(BF)
    dwso[...] += mm(att[...].T, sg)
    gself[...] = mm_nt(sg, wso[...]).astype(BF)

    @pl.when(tab[3, b] == 1)
    def _():
        dkv[0] = acc[...].astype(BF)


def self_backward(widths, tab, q, g, lse, kv, mk, dq, dkv, acc):
    b = pl.program_id(0)
    row0 = pl.multiple_of(tab[1, b], SUB)

    @pl.when(tab[2, b] == 1)
    def _():
        acc[...] = jnp.zeros_like(acc)

    for sub in range(BLOCK // SUB):
        at = pl.multiple_of(row0 + sub * SUB, SUB)
        here = slice(sub * SUB, (sub + 1) * SUB)
        meta = query_meta(mk, at)

        def run(ks, wd, meta=meta, at=at, here=here):
            mask = self_mask(mk, meta, at, ks, wd)
            qs = q[here, :]
            logs = lse[here, :]

            def get_prob(head, half, cols, keys):
                qm = jnp.where(head_lanes(half), qs[:, cols], jnp.zeros((), BF))
                s = jnp.where(mask, mm_nt(qm, keys), NEGATIVE_FILL)
                prob = jnp.exp(s - logs[:, head : head + 1])
                return prob, prob.astype(BF)

            def put_dq(cols, value):
                dq[here, cols] = value

            attend_back(qs, g[here, :], kv.at[0], get_prob, ks, wd, acc, put_dq)

        by_width(tab[5, 2 * b + sub], tab[4, 2 * b + sub], widths, run)

    @pl.when(tab[3, b] == 1)
    def _():
        dkv[0] = acc[...].astype(BF)


def const_spec(shape):
    return pl.BlockSpec(shape, lambda b, t: (0,) * len(shape), pipeline_mode=pl.Buffered(1))


def row_spec(cols):
    return pl.BlockSpec((BLOCK, cols), lambda b, t: (b, 0))


def line_spec(shape):
    return pl.BlockSpec((1,) + shape, lambda b, t: (t[0, b],) + (0,) * len(shape))


def sds(shape, dtype):
    return jax.ShapeDtypeStruct(shape, dtype)


def doc_numbers(bounds, places):
    return jnp.sum((bounds[:, None, :] <= places[None, :, None]).astype(jnp.int32), axis=2)


def body(
    stream, encoder, cotangent, self_qkv, self_out, cross_q, cross_kv, cross_out, ffn_in, ffn_out,
    norm_gain, norm_bias, lengths, enc_lengths, ranks, cuts,
):
    n = lax.axis_size("seq")
    me = lax.axis_index("seq")
    lines, piece = stream.shape[0], stream.shape[1]
    line_len = piece * n
    whole, p, k = plan(lines, n)
    groups = n // p
    slots = k + whole
    part_len = line_len // p
    chunks = n // p
    rows_p, rows_w = k * part_len, whole * line_len
    rows_all = rows_p + rows_w
    ff = ffn_in.shape[1] * n
    group, part = me // p, me % p
    widths = widths_for(line_len)
    i32 = jnp.int32

    cost = jnp.sum(lengths * lengths, axis=1)
    order = jnp.arange(lines, dtype=i32)
    lighter = (cost[None, :] < cost[:, None]) | (
        (cost[None, :] == cost[:, None]) & (order[None, :] < order[:, None])
    )
    rank = jnp.sum(lighter.astype(i32), axis=1)
    slot_of = jnp.where(rank < whole * n, rank, whole * n + lines - 1 - rank)
    line_of = jnp.sum(jnp.where(slot_of[None, :] == order[:, None], order[None, :], 0), axis=1)

    def slots_of(device):
        shared = whole * n + (device // p)[..., None] * k + jnp.arange(k)
        own = device[..., None] * whole + jnp.arange(whole)
        return jnp.concatenate([shared, own], axis=-1).astype(i32)

    targets = (me + jnp.arange(n)) % n
    target_lines = line_of[slots_of(targets)]

    def ring(t):
        return [(i, (i + t) % n) for i in range(n)]

    def exchange_in(x):
        send = x[target_lines]
        got = [send[0]] + [lax.ppermute(send[t], "seq", ring(t)) for t in range(1, n)]
        rel = jnp.stack(got)
        full = rel[(me - jnp.arange(n)) % n]
        return jnp.moveaxis(full, 0, 1).reshape((slots, line_len) + x.shape[2:])

    def own_rows_in(x):
        pieces = []
        if k:
            got = []
            mine = me // chunks
            for u in range(groups):
                perm = [
                    (pt * chunks + (g + u) % chunks, g * p + pt)
                    for g in range(groups)
                    for pt in range(p)
                ]
                to_group = (me % chunks - u) % groups
                pick = line_of[whole * n + to_group * k + jnp.arange(k)]
                got.append(lax.ppermute(x[pick], "seq", perm))
            rel = jnp.stack(got)
            full = rel[(jnp.arange(chunks) - group) % chunks]
            pieces.append(jnp.moveaxis(full, 0, 1).reshape(rows_p, x.shape[-1]))
        if whole:
            send = x[target_lines[:, k:]]
            got = [send[0]] + [lax.ppermute(send[t], "seq", ring(t)) for t in range(1, n)]
            full = jnp.stack(got)[(me - jnp.arange(n)) % n]
            pieces.append(jnp.moveaxis(full, 0, 1).reshape(rows_w, x.shape[-1]))
        return jnp.concatenate(pieces)

    def own_rows_out(y):
        got, base = [], []
        if k:
            parts = y[:rows_p].reshape(k, chunks, piece, D)
            for u in range(groups):
                perm = [
                    (g * p + pt, pt * chunks + (g + u) % chunks)
                    for g in range(groups)
                    for pt in range(p)
                ]
                send = lax.dynamic_index_in_dim(parts, (group + u) % chunks, 1, keepdims=False)
                got.append(lax.ppermute(send, "seq", perm))
        if whole:
            wholes = y[rows_p:].reshape(whole, n, piece, D)
            for t in range(n):
                send = lax.dynamic_index_in_dim(wholes, (me + t) % n, 1, keepdims=False)
                got.append(lax.ppermute(send, "seq", ring(t)) if t else send)
        rel = jnp.concatenate(got)
        slot = slot_of
        shared = slot - whole * n
        u = (me % chunks - shared // max(k, 1)) % groups
        at_shared = u * k + shared % max(k, 1)
        t = (me - slot // max(whole, 1)) % n
        at_whole = groups * k + t * whole + slot % max(whole, 1)
        return rel[jnp.where(slot >= whole * n, at_shared, at_whole)]

    xs = exchange_in(stream)
    rc = exchange_in(ranks * 32 + cuts)
    enc_src, cot_src = lax.optimization_barrier((encoder, cotangent, xs))[:2]
    es = exchange_in(enc_src)
    cot_src = lax.optimization_barrier((cot_src, es))[0]
    cot = own_rows_in(cot_src)
    w1 = lax.all_gather(ffn_in, "seq", axis=1, tiled=True)
    w2 = lax.all_gather(ffn_out, "seq", axis=0, tiled=True)

    mine = target_lines[0]
    cum_t = jnp.cumsum(lengths[mine], axis=1)
    cum_e = jnp.cumsum(enc_lengths[mine], axis=1)
    places = jnp.arange(line_len, dtype=i32)
    doc = doc_numbers(cum_t, places)
    src = doc_numbers(cum_e, places)
    zero = jnp.zeros_like(rc)
    mk = jnp.stack([doc, rc // 32, rc % 32, src, zero, zero, zero, zero], axis=1).astype(F32)

    block_line = [j for j in range(k) for _ in range(part_len // BLOCK)]
    block_line += [k + j for j in range(whole) for _ in range(line_len // BLOCK)]
    block_row = [r * BLOCK for j in range(k) for r in range(part_len // BLOCK)]
    block_row += [r * BLOCK for j in range(whole) for r in range(line_len // BLOCK)]
    blocks = len(block_line)
    begin = [int(i == 0 or block_line[i] != block_line[i - 1]) for i in range(blocks)]
    end = [int(i == blocks - 1 or block_line[i] != block_line[i + 1]) for i in range(blocks)]
    per = BLOCK // SUB
    bl = jnp.asarray(block_line, i32)
    br = jnp.asarray(block_row, i32) + jnp.where(bl < k, part * part_len, 0)
    sub_line = jnp.repeat(bl, per)
    sub_row = jnp.repeat(br, per) + jnp.tile(jnp.arange(per, dtype=i32) * SUB, blocks)
    ct, ce = cum_t[sub_line], cum_e[sub_line]
    before = ct <= sub_row[:, None]
    after = ct > sub_row[:, None] + (SUB - 1)

    def key_range(bounds):
        start = jnp.max(jnp.where(before, bounds, 0), axis=1)
        stop = jnp.min(jnp.where(after, bounds, line_len), axis=1)
        ks = start // SUB * SUB
        table = jnp.asarray(widths, i32)
        var = jnp.sum((stop - ks)[:, None] > table[None, :], axis=1).astype(i32)
        wd = jnp.sum(jnp.where(var[:, None] == jnp.arange(len(widths)), table[None, :], 0), axis=1)
        return jnp.minimum(ks, line_len - wd), var

    sks, svar = key_range(ct)
    cks, cvar = key_range(ce)
    pad = jnp.zeros((blocks * (per - 1),), i32)
    wide = lambda v: jnp.concatenate([jnp.asarray(v, i32), pad])
    tab = jnp.stack([wide(bl), wide(br), wide(begin), wide(end), sks, svar, cks, cvar])

    params = pltpu.CompilerParams(vmem_limit_bytes=VMEM, dimension_semantics=("arbitrary",))

    def call(kernel, name, ins, in_specs, outs, out_specs, scratch, flops):
        return pl.pallas_call(
            kernel,
            name=name,
            grid_spec=pltpu.PrefetchScalarGridSpec(
                num_scalar_prefetch=1,
                grid=(blocks,),
                in_specs=in_specs,
                out_specs=out_specs,
                scratch_shapes=scratch,
            ),
            out_shape=outs,
            compiler_params=params,
            cost_estimate=pl.CostEstimate(
                flops=int(flops), bytes_accessed=16 << 20, transcendentals=1 << 20
            ),
        )(tab, *ins)

    line2 = (line_len, 2 * D)
    kv, q, att, n0, s0, lse = call(
        functools.partial(self_forward, widths),
        "self_forward",
        (xs, mk, self_qkv, self_out),
        [line_spec((line_len, D)), line_spec((8, line_len)), const_spec((D, 3 * D)), const_spec((D, D))],
        (
            sds((slots,) + line2, BF),
            sds((rows_all, D), BF),
            sds((rows_all, D), BF),
            sds((rows_all, D), F32),
            sds((rows_all, 128), F32),
            sds((rows_all, 128), F32),
        ),
        (line_spec(line2), row_spec(D), row_spec(D), row_spec(D), row_spec(128), row_spec(128)),
        [],
        2e10,
    )

    out, gfirst, gself, dmkv, dw1, dw2t, dwco, dwcq, dwso, gb = call(
        functools.partial(middle, widths, ff),
        "middle",
        (es, mk, n0, s0, att, cot, cross_kv, self_out, cross_q, cross_out, w1, w2, norm_gain, norm_bias),
        [
            line_spec((line_len, D)), line_spec((8, line_len)), row_spec(D), row_spec(128), row_spec(D),
            row_spec(D), const_spec((D, 2 * D)), const_spec((D, D)), const_spec((D, D)),
            const_spec((D, D)), const_spec((D, ff)), const_spec((ff, D)), const_spec((3, D)),
            const_spec((3, D)),
        ],
        (
            sds((rows_all, D), BF),
            sds((rows_all, D), F32),
            sds((rows_all, D), BF),
            sds((slots, 2 * D, line_len), BF),
            sds((D, ff), F32),
            sds((D, ff), F32),
            sds((D, D), F32),
            sds((D, D), F32),
            sds((D, D), F32),
            sds((6, 8, D), F32),
        ),
        (
            row_spec(D), row_spec(D), row_spec(D), line_spec((2 * D, line_len)), const_spec((D, ff)),
            const_spec((D, ff)), const_spec((D, D)), const_spec((D, D)), const_spec((D, D)),
            const_spec((6, 8, D)),
        ),
        [
            pltpu.VMEM(line2, BF),
            pltpu.VMEM((2 * D, line_len), F32),
            pltpu.VMEM((per, HEADS, SUB, line_len), BF),
            pltpu.VMEM((BLOCK, D), BF),
            pltpu.VMEM((BLOCK, D), BF),
            pltpu.VMEM((BLOCK, D), BF),
            pltpu.VMEM((BLOCK, D), BF),
            pltpu.VMEM((BLOCK, ff), BF),
            pltpu.VMEM((BLOCK, ff), F32),
        ],
        8e10,
    )

    dq, dkv = call(
        functools.partial(self_backward, widths),
        "self_backward",
        (q, gself, lse, kv, mk),
        [row_spec(D), row_spec(D), row_spec(128), line_spec(line2), line_spec((8, line_len))],
        (sds((rows_all, D), BF), sds((slots, 2 * D, line_len), BF)),
        (row_spec(D), line_spec((2 * D, line_len))),
        [pltpu.VMEM((2 * D, line_len), F32)],
        3e10,
    )

    def own_rows(tensor):
        pieces = []
        if k:
            own = lax.dynamic_slice_in_dim(tensor[:k], part * part_len, part_len, 1)
            pieces.append(own.reshape(rows_p, tensor.shape[-1]))
        if whole:
            pieces.append(tensor[k:].reshape(rows_w, tensor.shape[-1]))
        return jnp.concatenate(pieces)

    def share_parts(tensor):
        pieces = []
        if k:
            own = lax.dynamic_slice_in_dim(tensor[:k], part * part_len, part_len, 1)
            for t in range(1, p):
                perm = [(g * p + i, g * p + (i + t) % p) for g in range(groups) for i in range(p)]
                to = (part + t) % p
                send = lax.dynamic_slice_in_dim(tensor[:k], to * part_len, part_len, 1)
                own = own + lax.ppermute(send.astype(BF), "seq", perm).astype(F32)
            pieces.append(own.reshape(rows_p, D))
        if whole:
            pieces.append(tensor[k:].reshape(rows_w, D))
        return jnp.concatenate(pieces)

    def to_lines(grads, weight):
        return jnp.einsum("wdk,cd->wkc", grads, weight, preferred_element_type=F32)

    def to_weight(inputs, grads):
        return jnp.einsum("wkc,wdk->cd", inputs, grads, preferred_element_type=F32)

    output = own_rows_out(out)
    cross_kv_grad = to_weight(es, dmkv)
    encoder_grad = own_rows_out(share_parts(to_lines(dmkv, cross_kv)).astype(BF)).astype(F32)

    from_kv = share_parts(to_lines(dkv, self_qkv[:, D:]))
    stream_rows = gfirst + mm_nt(dq, self_qkv[:, :D]) + from_kv
    stream_grad = own_rows_out(stream_rows.astype(BF)).astype(F32)
    q_grad = lax.dot_general(own_rows(xs), dq, (((0,), (0,)), ((), ())), preferred_element_type=F32)
    self_qkv_grad = jnp.concatenate([q_grad, to_weight(xs, dkv)], axis=1)

    def total(tensor):
        return lax.psum(tensor.astype(BF), ("dp", "seq")).astype(F32)

    ffn = lax.psum_scatter(jnp.stack([dw1, dw2t]).astype(BF), "seq", scatter_dimension=2, tiled=True)
    ffn = lax.psum(ffn, "dp").astype(F32)
    early = total(jnp.concatenate([dwso, dwcq, cross_kv_grad, dwco], axis=1))
    late = total(self_qkv_grad)
    norms = lax.psum(jnp.sum(gb, axis=1), ("dp", "seq"))
    return (
        output,
        stream_grad,
        encoder_grad,
        late,
        early[:, :D],
        early[:, D : 2 * D],
        early[:, 2 * D : 4 * D],
        early[:, 4 * D :],
        ffn[0],
        ffn[1].T,
        norms[:3],
        norms[3:],
    )


def solution(mesh):
    lines = P("dp", "seq", None)
    in_specs = (
        lines, lines, lines, P(), P(), P(), P(), P(), P(None, "seq"), P("seq", None), P(), P(),
        P("dp", None), P("dp", None), P("dp", "seq"), P("dp", "seq"),
    )
    out_specs = (
        lines, lines, lines, P(), P(), P(), P(), P(), P(None, "seq"), P("seq", None), P(), P(),
    )
    return jax.shard_map(body, mesh=mesh, in_specs=in_specs, out_specs=out_specs, check_vma=False)
```

```python
import functools
import math

import jax
import jax.numpy as jnp
from jax import lax
from jax.experimental import pallas as pl
from jax.experimental.pallas import tpu as pltpu
from jax.sharding import PartitionSpec as P

D = 512
HEADS = 8
HEAD = 64
PAIR = 2 * HEAD
PAIRS = HEADS // 2
NEGATIVE_FILL = -1e30
EPSILON = 1e-05
SCALE = HEAD ** (-0.5)
BLOCK = 256
SUB = 128
BF = jnp.bfloat16
F32 = jnp.float32
NT = (((1,), (1,)), ((), ()))
GELU_C = math.sqrt(2.0 / math.pi)
VMEM = 60 * 1024 * 1024


def mm(left, right):
    return jnp.dot(left, right, preferred_element_type=F32)


def mm_nt(left, right):
    return lax.dot_general(left, right, NT, preferred_element_type=F32)


def plan(lines, n):
    whole = lines // n
    rest = lines - whole * n
    groups = math.gcd(rest, n) if rest else n
    return whole, n // groups, rest // groups


def widths_for(line_len):
    some = ((256, True), (384, True), (640, False))
    return tuple(w for w in some if w[0] < line_len) + ((line_len, False),)


def norm_stats(r):
    centred = r - jnp.mean(r, axis=-1, keepdims=True)
    inv = lax.rsqrt(jnp.mean(centred * centred, axis=-1, keepdims=True) + EPSILON)
    return centred * inv, inv


def norm_back(dy, normed, inv, gain):
    scaled = dy * gain
    inner = (
        scaled
        - jnp.mean(scaled, axis=-1, keepdims=True)
        - normed * jnp.mean(scaled * normed, axis=-1, keepdims=True)
    )
    return inner * inv


def fold8(t):
    return jnp.sum(t.reshape(t.shape[0] // 8, 8, t.shape[1]), axis=0)


def head_lanes(half):
    lane = lax.broadcasted_iota(jnp.int32, (1, PAIR), 1)
    return (lane < HEAD) if half == 0 else (lane >= HEAD)


def query_meta(mk, at):
    return mk[0, :, pl.ds(at, SUB)].T


def self_mask(mk, meta, at, ks, wd):
    doc = mk[0, 0:1, pl.ds(ks, wd)] == meta[:, 0:1]
    low = mk[0, 1:2, pl.ds(ks, wd)] < meta[:, 2:3]
    key = lax.broadcasted_iota(jnp.int32, (SUB, wd), 1) + ks
    query = lax.broadcasted_iota(jnp.int32, (SUB, wd), 0) + at
    return doc & (low | (key == query))


def cross_mask(mk, meta, at, ks, wd):
    return mk[0, 3:4, pl.ds(ks, wd)] == meta[:, 0:1]


def by_width(var, ks, widths, run):
    ks = pl.multiple_of(ks, SUB)
    for index, (wd, together) in enumerate(widths):

        @pl.when(var == index)
        def _(wd=wd, together=together):
            if together:
                run(tuple(range(PAIRS)), ks, wd)
            else:

                @pl.loop(0, PAIRS)
                def _(pair):
                    run((pair,), ks, wd)


def stacked(t):
    zero = jnp.zeros((), t.dtype)
    return jnp.concatenate([jnp.where(head_lanes(half), t, zero) for half in range(2)])


def unstacked(t):
    return jnp.where(head_lanes(0), t[:SUB], t[SUB:])


def pair_cols(pair, base=0):
    if isinstance(pair, int):
        return slice(base + pair * PAIR, base + (pair + 1) * PAIR)
    return pl.ds(pl.multiple_of(base + pair * PAIR, PAIR), PAIR)


def head_col(values, pair):
    if isinstance(pair, int):
        return jnp.concatenate([values[:, 2 * pair : 2 * pair + 1], values[:, 2 * pair + 1 : 2 * pair + 2]])
    lane = lax.broadcasted_iota(jnp.int32, values.shape, 1)
    pick = lambda head: jnp.sum(jnp.where(lane == head, values, 0.0), axis=-1, keepdims=True)
    return jnp.concatenate([pick(2 * pair), pick(2 * pair + 1)])


def attend(pairs, q, rows, kv, mask, ks, wd, out, lse):
    mask = jnp.concatenate([mask, mask])
    keys = pl.ds(ks, wd)
    lane = lax.broadcasted_iota(jnp.int32, (SUB, 128), 1)
    scores = [mm_nt(stacked(q[rows, pair_cols(i)]), kv[keys, pair_cols(i)]) for i in pairs]
    scores = [jnp.where(mask, s, NEGATIVE_FILL) for s in scores]
    tops = [jnp.max(s, axis=-1, keepdims=True) for s in scores]
    exps = [jnp.exp(s - top) for s, top in zip(scores, tops)]
    sums = [jnp.sum(e, axis=-1, keepdims=True) for e in exps]
    probs = [(e * (1.0 / total)).astype(BF) for e, total in zip(exps, sums)]
    outs = [mm(prob, kv[keys, pair_cols(i, D)]) for prob, i in zip(probs, pairs)]
    logs_all = lse[rows, :]
    for i, o, top, total in zip(pairs, outs, tops, sums):
        out[rows, pair_cols(i)] = unstacked(o).astype(BF)
        logs = top + jnp.log(total)
        logs_all = jnp.where(lane == 2 * i, logs[:SUB], logs_all)
        logs_all = jnp.where(lane == 2 * i + 1, logs[SUB:], logs_all)
    lse[rows, :] = logs_all


def attend_back(pairs, q, g, lse, rows, kv, mask, ks, wd, acc, dq):
    mask = jnp.concatenate([mask, mask])
    keys = pl.ds(ks, wd)
    logs = lse[rows, :]
    qs = [stacked(q[rows, pair_cols(i)]) for i in pairs]
    gs = [stacked(g[rows, pair_cols(i)]) for i in pairs]
    scores = [mm_nt(qi, kv[keys, pair_cols(i)]) for qi, i in zip(qs, pairs)]
    dps = [mm_nt(gi, kv[keys, pair_cols(i, D)]) for gi, i in zip(gs, pairs)]
    probs = [jnp.exp(jnp.where(mask, s, NEGATIVE_FILL) - head_col(logs, i)) for s, i in zip(scores, pairs)]
    sums = [jnp.sum(prob * dp, axis=-1, keepdims=True) for prob, dp in zip(probs, dps)]
    dss = [(prob * (dp - total)).astype(BF) for prob, dp, total in zip(probs, dps, sums)]
    for i, gi, prob in zip(pairs, gs, probs):
        acc[pair_cols(i, D), keys] += mm(gi.T, prob.astype(BF))
    for i, qi, ds in zip(pairs, qs, dss):
        acc[pair_cols(i), keys] += mm(qi.T, ds)
    for i, ds in zip(pairs, dss):
        dq[rows, pair_cols(i)] = (unstacked(mm(ds, kv[keys, pair_cols(i)])) * SCALE).astype(BF)


def each_sub(row0, body):
    @pl.loop(0, BLOCK // SUB)
    def _(sub):
        body(sub, pl.ds(pl.multiple_of(sub * SUB, SUB), SUB), pl.multiple_of(row0 + sub * SUB, SUB))


def self_forward(widths, tab, xs, mk, wqkv, wso, kv, q_out, att_out, n0_out, s0_out, lse_out):
    b = pl.program_id(0)
    row0 = pl.multiple_of(tab[1, b], SUB)

    @pl.when(tab[2, b] == 1)
    def _():
        @pl.loop(0, kv.shape[1] // BLOCK)
        def _(i):
            rows = pl.ds(pl.multiple_of(i * BLOCK, BLOCK), BLOCK)
            kv[0, rows, :] = mm(xs[0, rows, :], wqkv[:, D:]).astype(BF)

    x = xs[0, pl.ds(row0, BLOCK), :]
    q_out[...] = mm(x, wqkv[:, :D]).astype(BF) * jnp.asarray(SCALE, BF)
    lse_out[...] = jnp.zeros_like(lse_out)

    def sub_block(sub, rows, at):
        meta = query_meta(mk, at)

        def run(pairs, ks, wd):
            mask = self_mask(mk, meta, at, ks, wd)
            attend(pairs, q_out, rows, kv.at[0], mask, ks, wd, att_out, lse_out)

        by_width(tab[5, 2 * b + sub], tab[4, 2 * b + sub], widths, run)

    each_sub(row0, sub_block)
    r = x.astype(F32) + mm(att_out[...], wso[...])
    normed, inv = norm_stats(r)
    n0_out[...] = normed
    s0_out[...] = jnp.broadcast_to(inv, s0_out.shape)


def middle(
    widths, ff, tab, es, mk, n0, s0, att, cot, wckv, wso, wcq, wco, w1, w2, gains, biases,
    out, gfirst, gself, dkv, dw1, dw2t, dwco, dwcq, dwso, gb,
    mkv, acc, clse, catt, cq_scr, gatt, dq_scr, hid, gprime,
):
    b = pl.program_id(0)
    row0 = pl.multiple_of(tab[1, b], SUB)

    @pl.when(b == 0)
    def _():
        for ref in (dw1, dw2t, dwco, dwcq, dwso, gb):
            ref[...] = jnp.zeros_like(ref)

    @pl.when(tab[2, b] == 1)
    def _():
        acc[...] = jnp.zeros_like(acc)

        @pl.loop(0, mkv.shape[0] // BLOCK)
        def _(i):
            rows = pl.ds(pl.multiple_of(i * BLOCK, BLOCK), BLOCK)
            mkv[rows, :] = mm(es[0, rows, :], wckv[...]).astype(BF)

    first = n0[...] * gains[0:1, :] + biases[0:1, :]
    first_low = first.astype(BF)
    cq_scr[...] = mm(first_low, wcq[...]).astype(BF) * jnp.asarray(SCALE, BF)
    clse[...] = jnp.zeros_like(clse)

    def sub_block(sub, rows, at):
        meta = query_meta(mk, at)

        def run(pairs, ks, wd):
            mask = cross_mask(mk, meta, at, ks, wd)
            attend(pairs, cq_scr, rows, mkv, mask, ks, wd, catt, clse)

        by_width(tab[7, 2 * b + sub], tab[6, 2 * b + sub], widths, run)

    each_sub(row0, sub_block)
    n1, s1 = norm_stats(first + mm(catt[...], wco[...]))
    second = n1 * gains[1:2, :] + biases[1:2, :]
    second_low = second.astype(BF)
    chunk = D
    total = second
    for c in range(ff // chunk):
        cols = slice(c * chunk, (c + 1) * chunk)
        v = mm(second_low, w1[:, cols])
        v2 = v * v
        t = jnp.tanh(GELU_C * (v + 0.044715 * (v2 * v)))
        half = 0.5 * (1.0 + t)
        h = (v * half).astype(BF)
        hid[:, cols] = h
        gprime[:, cols] = half + (0.5 * v) * (1.0 - t * t) * (GELU_C + (3 * 0.044715 * GELU_C) * v2)
        total = total + mm(h, w2[cols, :])
    n2, s2 = norm_stats(total)
    out[...] = (n2 * gains[2:3, :] + biases[2:3, :]).astype(BF)
    dy = cot[...].astype(F32)
    gb[2] += fold8(dy * n2)
    gb[5] += fold8(dy)
    gthird = norm_back(dy, n2, s2, gains[2:3, :])
    fg = gthird.astype(BF)
    fgt, sect = fg.T, second_low.T
    back = gthird
    for c in range(ff // chunk):
        cols = slice(c * chunk, (c + 1) * chunk)
        pg = (mm_nt(fg, w2[cols, :]) * gprime[:, cols]).astype(BF)
        dw2t[:, cols] += mm(fgt, hid[:, cols])
        dw1[:, cols] += mm(sect, pg)
        back = back + mm_nt(pg, w1[:, cols])
    gb[1] += fold8(back * n1)
    gb[4] += fold8(back)
    gsecond = norm_back(back, n1, s1, gains[1:2, :])
    cg = gsecond.astype(BF)
    dwco[...] += mm(catt[...].T, cg)
    gatt[...] = mm_nt(cg, wco[...]).astype(BF)

    def sub_block_back(sub, rows, at):
        meta = query_meta(mk, at)

        def run(pairs, ks, wd):
            mask = cross_mask(mk, meta, at, ks, wd)
            attend_back(pairs, cq_scr, gatt, clse, rows, mkv, mask, ks, wd, acc, dq_scr)

        by_width(tab[7, 2 * b + sub], tab[6, 2 * b + sub], widths, run)

    each_sub(row0, sub_block_back)
    dq = dq_scr[...]
    dwcq[...] += mm(first_low.T, dq)
    gf = gsecond + mm_nt(dq, wcq[...])
    gb[0] += fold8(gf * n0[...])
    gb[3] += fold8(gf)
    gf = norm_back(gf, n0[...], s0[:, 0:1], gains[0:1, :])
    gfirst[...] = gf
    sg = gf.astype(BF)
    dwso[...] += mm(att[...].T, sg)
    gself[...] = mm_nt(sg, wso[...]).astype(BF)

    @pl.when(tab[3, b] == 1)
    def _():
        dkv[0] = acc[...].astype(BF)


def self_backward(widths, tab, q, g, lse, kv, mk, dq, dkv, acc):
    b = pl.program_id(0)
    row0 = pl.multiple_of(tab[1, b], SUB)

    @pl.when(tab[2, b] == 1)
    def _():
        acc[...] = jnp.zeros_like(acc)

    def sub_block(sub, rows, at):
        meta = query_meta(mk, at)

        def run(pairs, ks, wd):
            mask = self_mask(mk, meta, at, ks, wd)
            attend_back(pairs, q, g, lse, rows, kv.at[0], mask, ks, wd, acc, dq)

        by_width(tab[5, 2 * b + sub], tab[4, 2 * b + sub], widths, run)

    each_sub(row0, sub_block)

    @pl.when(tab[3, b] == 1)
    def _():
        dkv[0] = acc[...].astype(BF)


def const_spec(shape):
    return pl.BlockSpec(shape, lambda b, t: (0,) * len(shape), pipeline_mode=pl.Buffered(1))


def row_spec(cols):
    return pl.BlockSpec((BLOCK, cols), lambda b, t: (b, 0))


def line_spec(shape):
    return pl.BlockSpec((1,) + shape, lambda b, t: (t[0, b],) + (0,) * len(shape))


def sds(shape, dtype):
    return jax.ShapeDtypeStruct(shape, dtype)


def kernels(
    tab, xs, es, cot, mk, self_qkv, self_out, cross_q, cross_kv, cross_out, w1, w2, norm_gain, norm_bias
):
    slots, line_len = xs.shape[0], xs.shape[1]
    rows_all, ff = cot.shape[0], w1.shape[1]
    per, blocks = BLOCK // SUB, rows_all // BLOCK
    widths = widths_for(line_len)
    params = pltpu.CompilerParams(vmem_limit_bytes=VMEM, dimension_semantics=("arbitrary",))

    def call(kernel, name, ins, in_specs, outs, out_specs, scratch, flops):
        return pl.pallas_call(
            kernel,
            name=name,
            grid_spec=pltpu.PrefetchScalarGridSpec(
                num_scalar_prefetch=1,
                grid=(blocks,),
                in_specs=in_specs,
                out_specs=out_specs,
                scratch_shapes=scratch,
            ),
            out_shape=outs,
            compiler_params=params,
            cost_estimate=pl.CostEstimate(
                flops=int(flops), bytes_accessed=16 << 20, transcendentals=1 << 20
            ),
        )(tab, *ins)

    line2 = (line_len, 2 * D)
    kv, q, att, n0, s0, lse = call(
        functools.partial(self_forward, widths),
        "self_forward",
        (xs, mk, self_qkv, self_out),
        [line_spec((line_len, D)), line_spec((8, line_len)), const_spec((D, 3 * D)), const_spec((D, D))],
        (
            sds((slots,) + line2, BF),
            sds((rows_all, D), BF),
            sds((rows_all, D), BF),
            sds((rows_all, D), F32),
            sds((rows_all, 128), F32),
            sds((rows_all, 128), F32),
        ),
        (line_spec(line2), row_spec(D), row_spec(D), row_spec(D), row_spec(128), row_spec(128)),
        [],
        2e10,
    )

    out, gfirst, gself, dmkv, dw1, dw2t, dwco, dwcq, dwso, gb = call(
        functools.partial(middle, widths, ff),
        "middle",
        (es, mk, n0, s0, att, cot, cross_kv, self_out, cross_q, cross_out, w1, w2, norm_gain, norm_bias),
        [
            line_spec((line_len, D)), line_spec((8, line_len)), row_spec(D), row_spec(128), row_spec(D),
            row_spec(D), const_spec((D, 2 * D)), const_spec((D, D)), const_spec((D, D)),
            const_spec((D, D)), const_spec((D, ff)), const_spec((ff, D)), const_spec((3, D)),
            const_spec((3, D)),
        ],
        (
            sds((rows_all, D), BF),
            sds((rows_all, D), F32),
            sds((rows_all, D), BF),
            sds((slots, 2 * D, line_len), BF),
            sds((D, ff), F32),
            sds((D, ff), F32),
            sds((D, D), F32),
            sds((D, D), F32),
            sds((D, D), F32),
            sds((6, 8, D), F32),
        ),
        (
            row_spec(D), row_spec(D), row_spec(D), line_spec((2 * D, line_len)), const_spec((D, ff)),
            const_spec((D, ff)), const_spec((D, D)), const_spec((D, D)), const_spec((D, D)),
            const_spec((6, 8, D)),
        ),
        [
            pltpu.VMEM(line2, BF),
            pltpu.VMEM((2 * D, line_len), F32),
            pltpu.VMEM((BLOCK, 128), F32),
            pltpu.VMEM((BLOCK, D), BF),
            pltpu.VMEM((BLOCK, D), BF),
            pltpu.VMEM((BLOCK, D), BF),
            pltpu.VMEM((BLOCK, D), BF),
            pltpu.VMEM((BLOCK, ff), BF),
            pltpu.VMEM((BLOCK, ff), F32),
        ],
        8e10,
    )

    dq, dkv = call(
        functools.partial(self_backward, widths),
        "self_backward",
        (q, gself, lse, kv, mk),
        [row_spec(D), row_spec(D), row_spec(128), line_spec(line2), line_spec((8, line_len))],
        (sds((rows_all, D), BF), sds((slots, 2 * D, line_len), BF)),
        (row_spec(D), line_spec((2 * D, line_len))),
        [pltpu.VMEM((2 * D, line_len), F32)],
        3e10,
    )
    return out, gfirst, dmkv, dw1, dw2t, dwco, dwcq, dwso, gb, dq, dkv


def doc_numbers(bounds, places):
    return jnp.sum((bounds[:, None, :] <= places[None, :, None]).astype(jnp.int32), axis=2)


def body(
    stream, encoder, cotangent, self_qkv, self_out, cross_q, cross_kv, cross_out, ffn_in, ffn_out,
    norm_gain, norm_bias, lengths, enc_lengths, ranks, cuts,
):
    n = lax.axis_size("seq")
    me = lax.axis_index("seq")
    lines, piece = stream.shape[0], stream.shape[1]
    line_len = piece * n
    whole, p, k = plan(lines, n)
    groups = n // p
    slots = k + whole
    part_len = line_len // p
    chunks = n // p
    rows_p, rows_w = k * part_len, whole * line_len
    rows_all = rows_p + rows_w
    ff = ffn_in.shape[1] * n
    group, part = me // p, me % p
    widths = widths_for(line_len)
    i32 = jnp.int32

    cost = jnp.sum(lengths * lengths, axis=1)
    order = jnp.arange(lines, dtype=i32)
    lighter = (cost[None, :] < cost[:, None]) | (
        (cost[None, :] == cost[:, None]) & (order[None, :] < order[:, None])
    )
    rank = jnp.sum(lighter.astype(i32), axis=1)
    slot_of = jnp.where(rank < whole * n, rank, whole * n + lines - 1 - rank)
    line_of = jnp.sum(jnp.where(slot_of[None, :] == order[:, None], order[None, :], 0), axis=1)

    def slots_of(device):
        shared = whole * n + (device // p)[..., None] * k + jnp.arange(k)
        own = device[..., None] * whole + jnp.arange(whole)
        return jnp.concatenate([shared, own], axis=-1).astype(i32)

    targets = (me + jnp.arange(n)) % n
    target_lines = line_of[slots_of(targets)]

    def ring(t):
        return [(i, (i + t) % n) for i in range(n)]

    def exchange_in(x):
        send = x[target_lines]
        got = [send[0]] + [lax.ppermute(send[t], "seq", ring(t)) for t in range(1, n)]
        rel = jnp.stack(got)
        full = rel[(me - jnp.arange(n)) % n]
        return jnp.moveaxis(full, 0, 1).reshape((slots, line_len) + x.shape[2:])

    def own_rows_in(x):
        pieces = []
        if k:
            got = []
            mine = me // chunks
            for u in range(groups):
                perm = [
                    (pt * chunks + (g + u) % chunks, g * p + pt)
                    for g in range(groups)
                    for pt in range(p)
                ]
                to_group = (me % chunks - u) % groups
                pick = line_of[whole * n + to_group * k + jnp.arange(k)]
                got.append(lax.ppermute(x[pick], "seq", perm))
            rel = jnp.stack(got)
            full = rel[(jnp.arange(chunks) - group) % chunks]
            pieces.append(jnp.moveaxis(full, 0, 1).reshape(rows_p, x.shape[-1]))
        if whole:
            send = x[target_lines[:, k:]]
            got = [send[0]] + [lax.ppermute(send[t], "seq", ring(t)) for t in range(1, n)]
            full = jnp.stack(got)[(me - jnp.arange(n)) % n]
            pieces.append(jnp.moveaxis(full, 0, 1).reshape(rows_w, x.shape[-1]))
        return jnp.concatenate(pieces)

    def own_rows_out(y):
        got, base = [], []
        if k:
            parts = y[:rows_p].reshape(k, chunks, piece, D)
            for u in range(groups):
                perm = [
                    (g * p + pt, pt * chunks + (g + u) % chunks)
                    for g in range(groups)
                    for pt in range(p)
                ]
                send = lax.dynamic_index_in_dim(parts, (group + u) % chunks, 1, keepdims=False)
                got.append(lax.ppermute(send, "seq", perm))
        if whole:
            wholes = y[rows_p:].reshape(whole, n, piece, D)
            for t in range(n):
                send = lax.dynamic_index_in_dim(wholes, (me + t) % n, 1, keepdims=False)
                got.append(lax.ppermute(send, "seq", ring(t)) if t else send)
        rel = jnp.concatenate(got)
        slot = slot_of
        shared = slot - whole * n
        u = (me % chunks - shared // max(k, 1)) % groups
        at_shared = u * k + shared % max(k, 1)
        t = (me - slot // max(whole, 1)) % n
        at_whole = groups * k + t * whole + slot % max(whole, 1)
        return rel[jnp.where(slot >= whole * n, at_shared, at_whole)]

    xs = exchange_in(stream)
    rc = exchange_in(ranks * 32 + cuts)
    enc_src, cot_src = lax.optimization_barrier((encoder, cotangent, xs))[:2]
    es = exchange_in(enc_src)
    cot_src = lax.optimization_barrier((cot_src, es))[0]
    cot = own_rows_in(cot_src)
    w1 = lax.all_gather(ffn_in, "seq", axis=1, tiled=True)
    w2 = lax.all_gather(ffn_out, "seq", axis=0, tiled=True)

    mine = target_lines[0]
    cum_t = jnp.cumsum(lengths[mine], axis=1)
    cum_e = jnp.cumsum(enc_lengths[mine], axis=1)
    places = jnp.arange(line_len, dtype=i32)
    doc = doc_numbers(cum_t, places)
    src = doc_numbers(cum_e, places)
    zero = jnp.zeros_like(rc)
    mk = jnp.stack([doc, rc // 32, rc % 32, src, zero, zero, zero, zero], axis=1).astype(F32)

    block_line = [j for j in range(k) for _ in range(part_len // BLOCK)]
    block_line += [k + j for j in range(whole) for _ in range(line_len // BLOCK)]
    block_row = [r * BLOCK for j in range(k) for r in range(part_len // BLOCK)]
    block_row += [r * BLOCK for j in range(whole) for r in range(line_len // BLOCK)]
    blocks = len(block_line)
    begin = [int(i == 0 or block_line[i] != block_line[i - 1]) for i in range(blocks)]
    end = [int(i == blocks - 1 or block_line[i] != block_line[i + 1]) for i in range(blocks)]
    per = BLOCK // SUB
    bl = jnp.asarray(block_line, i32)
    br = jnp.asarray(block_row, i32) + jnp.where(bl < k, part * part_len, 0)
    sub_line = jnp.repeat(bl, per)
    sub_row = jnp.repeat(br, per) + jnp.tile(jnp.arange(per, dtype=i32) * SUB, blocks)
    ct, ce = cum_t[sub_line], cum_e[sub_line]
    before = ct <= sub_row[:, None]
    after = ct > sub_row[:, None] + (SUB - 1)

    def key_range(bounds):
        start = jnp.max(jnp.where(before, bounds, 0), axis=1)
        stop = jnp.min(jnp.where(after, bounds, line_len), axis=1)
        ks = start // SUB * SUB
        table = jnp.asarray([wd for wd, _ in widths], i32)
        var = jnp.sum((stop - ks)[:, None] > table[None, :], axis=1).astype(i32)
        wd = jnp.sum(jnp.where(var[:, None] == jnp.arange(len(widths)), table[None, :], 0), axis=1)
        return jnp.minimum(ks, line_len - wd), var

    sks, svar = key_range(ct)
    cks, cvar = key_range(ce)
    pad = jnp.zeros((blocks * (per - 1),), i32)
    wide = lambda v: jnp.concatenate([jnp.asarray(v, i32), pad])
    tab = jnp.stack([wide(bl), wide(br), wide(begin), wide(end), sks, svar, cks, cvar])

    out, gfirst, dmkv, dw1, dw2t, dwco, dwcq, dwso, gb, dq, dkv = kernels(
        tab, xs, es, cot, mk, self_qkv, self_out, cross_q, cross_kv, cross_out, w1, w2, norm_gain, norm_bias
    )

    def own_rows(tensor):
        pieces = []
        if k:
            own = lax.dynamic_slice_in_dim(tensor[:k], part * part_len, part_len, 1)
            pieces.append(own.reshape(rows_p, tensor.shape[-1]))
        if whole:
            pieces.append(tensor[k:].reshape(rows_w, tensor.shape[-1]))
        return jnp.concatenate(pieces)

    def share_parts(tensor):
        pieces = []
        if k:
            own = lax.dynamic_slice_in_dim(tensor[:k], part * part_len, part_len, 1)
            for t in range(1, p):
                perm = [(g * p + i, g * p + (i + t) % p) for g in range(groups) for i in range(p)]
                to = (part + t) % p
                send = lax.dynamic_slice_in_dim(tensor[:k], to * part_len, part_len, 1)
                own = own + lax.ppermute(send.astype(BF), "seq", perm).astype(F32)
            pieces.append(own.reshape(rows_p, D))
        if whole:
            pieces.append(tensor[k:].reshape(rows_w, D))
        return jnp.concatenate(pieces)

    def to_lines(grads, weight):
        return jnp.einsum("wdk,cd->wkc", grads, weight, preferred_element_type=F32)

    def to_weight(inputs, grads):
        return jnp.einsum("wkc,wdk->cd", inputs, grads, preferred_element_type=F32)

    output = own_rows_out(out)
    cross_kv_grad = to_weight(es, dmkv)
    encoder_grad = own_rows_out(share_parts(to_lines(dmkv, cross_kv)).astype(BF)).astype(F32)

    from_kv = share_parts(to_lines(dkv, self_qkv[:, D:]))
    stream_rows = gfirst + mm_nt(dq, self_qkv[:, :D]) + from_kv
    stream_grad = own_rows_out(stream_rows.astype(BF)).astype(F32)
    q_grad = lax.dot_general(own_rows(xs), dq, (((0,), (0,)), ((), ())), preferred_element_type=F32)
    self_qkv_grad = jnp.concatenate([q_grad, to_weight(xs, dkv)], axis=1)

    def total(tensor):
        return lax.psum(tensor.astype(BF), ("dp", "seq")).astype(F32)

    ffn = lax.psum_scatter(jnp.stack([dw1, dw2t]).astype(BF), "seq", scatter_dimension=2, tiled=True)
    ffn = lax.psum(ffn, "dp").astype(F32)
    early = total(jnp.concatenate([dwso, dwcq, cross_kv_grad, dwco], axis=1))
    late = total(self_qkv_grad)
    norms = lax.psum(jnp.sum(gb, axis=1), ("dp", "seq"))
    return (
        output,
        stream_grad,
        encoder_grad,
        late,
        early[:, :D],
        early[:, D : 2 * D],
        early[:, 2 * D : 4 * D],
        early[:, 4 * D :],
        ffn[0],
        ffn[1].T,
        norms[:3],
        norms[3:],
    )


def solution(mesh):
    lines = P("dp", "seq", None)
    in_specs = (
        lines, lines, lines, P(), P(), P(), P(), P(), P(None, "seq"), P("seq", None), P(), P(),
        P("dp", None), P("dp", None), P("dp", "seq"), P("dp", "seq"),
    )
    out_specs = (
        lines, lines, lines, P(), P(), P(), P(), P(), P(None, "seq"), P("seq", None), P(), P(),
    )
    return jax.shard_map(body, mesh=mesh, in_specs=in_specs, out_specs=out_specs, check_vma=False)
```

```python
import functools
import math

import jax
import jax.numpy as jnp
from jax import lax
from jax.experimental import pallas as pl
from jax.experimental.pallas import tpu as pltpu
from jax.sharding import PartitionSpec as P

D = 512
HEADS = 8
HEAD = 64
PAIR = 2 * HEAD
PAIRS = HEADS // 2
NEGATIVE_FILL = -1e30
EPSILON = 1e-05
SCALE = HEAD ** (-0.5)
BLOCK = 256
SUB = 128
BF = jnp.bfloat16
F32 = jnp.float32
NT = (((1,), (1,)), ((), ()))
GELU_C = math.sqrt(2.0 / math.pi)
VMEM = 60 * 1024 * 1024


def mm(left, right):
    return jnp.dot(left, right, preferred_element_type=F32)


def mm_nt(left, right):
    return lax.dot_general(left, right, NT, preferred_element_type=F32)


def plan(lines, n):
    whole = lines // n
    rest = lines - whole * n
    groups = math.gcd(rest, n) if rest else n
    return whole, n // groups, rest // groups


def widths_for(line_len):
    some = ((256, True), (384, True), (640, False))
    return tuple(w for w in some if w[0] < line_len) + ((line_len, False),)


def norm_stats(r):
    centred = r - jnp.mean(r, axis=-1, keepdims=True)
    inv = lax.rsqrt(jnp.mean(centred * centred, axis=-1, keepdims=True) + EPSILON)
    return centred * inv, inv


def norm_back(dy, normed, inv, gain):
    scaled = dy * gain
    inner = (
        scaled
        - jnp.mean(scaled, axis=-1, keepdims=True)
        - normed * jnp.mean(scaled * normed, axis=-1, keepdims=True)
    )
    return inner * inv


def fold8(t):
    return jnp.sum(t.reshape(t.shape[0] // 8, 8, t.shape[1]), axis=0)


def head_lanes(half):
    lane = lax.broadcasted_iota(jnp.int32, (1, PAIR), 1)
    return (lane < HEAD) if half == 0 else (lane >= HEAD)


def query_meta(mk, at):
    return mk[0, :, pl.ds(at, SUB)].T


def self_mask(mk, meta, at, ks, wd):
    doc = mk[0, 0:1, pl.ds(ks, wd)] == meta[:, 0:1]
    low = mk[0, 1:2, pl.ds(ks, wd)] < meta[:, 2:3]
    key = lax.broadcasted_iota(jnp.int32, (SUB, wd), 1) + ks
    query = lax.broadcasted_iota(jnp.int32, (SUB, wd), 0) + at
    return doc & (low | (key == query))


def cross_mask(mk, meta, at, ks, wd):
    return mk[0, 3:4, pl.ds(ks, wd)] == meta[:, 0:1]


def by_width(var, ks, widths, run):
    ks = pl.multiple_of(ks, SUB)
    for index, (wd, together) in enumerate(widths):

        @pl.when(var == index)
        def _(wd=wd, together=together):
            if together:
                run(tuple(range(PAIRS)), ks, wd)
            else:

                @pl.loop(0, PAIRS)
                def _(pair):
                    run((pair,), ks, wd)


def stacked(t):
    zero = jnp.zeros((), t.dtype)
    return jnp.concatenate([jnp.where(head_lanes(half), t, zero) for half in range(2)])


def unstacked(t):
    return jnp.where(head_lanes(0), t[:SUB], t[SUB:])


def pair_cols(pair, base=0):
    if isinstance(pair, int):
        return slice(base + pair * PAIR, base + (pair + 1) * PAIR)
    return pl.ds(pl.multiple_of(base + pair * PAIR, PAIR), PAIR)


def head_col(values, pair):
    if isinstance(pair, int):
        return jnp.concatenate([values[:, 2 * pair : 2 * pair + 1], values[:, 2 * pair + 1 : 2 * pair + 2]])
    lane = lax.broadcasted_iota(jnp.int32, values.shape, 1)
    pick = lambda head: jnp.sum(jnp.where(lane == head, values, 0.0), axis=-1, keepdims=True)
    return jnp.concatenate([pick(2 * pair), pick(2 * pair + 1)])


def attend(pairs, q, rows, kv, mask, ks, wd, out, lse):
    mask = jnp.concatenate([mask, mask])
    keys = pl.ds(ks, wd)
    lane = lax.broadcasted_iota(jnp.int32, (SUB, 128), 1)
    scores = [mm_nt(stacked(q[rows, pair_cols(i)]), kv[keys, pair_cols(i)]) for i in pairs]
    scores = [jnp.where(mask, s, NEGATIVE_FILL) for s in scores]
    tops = [jnp.max(s, axis=-1, keepdims=True) for s in scores]
    exps = [jnp.exp(s - top) for s, top in zip(scores, tops)]
    sums = [jnp.sum(e, axis=-1, keepdims=True) for e in exps]
    probs = [(e * (1.0 / total)).astype(BF) for e, total in zip(exps, sums)]
    outs = [mm(prob, kv[keys, pair_cols(i, D)]) for prob, i in zip(probs, pairs)]
    logs_all = lse[rows, :]
    for i, o, top, total in zip(pairs, outs, tops, sums):
        out[rows, pair_cols(i)] = unstacked(o).astype(BF)
        logs = top + jnp.log(total)
        logs_all = jnp.where(lane == 2 * i, logs[:SUB], logs_all)
        logs_all = jnp.where(lane == 2 * i + 1, logs[SUB:], logs_all)
    lse[rows, :] = logs_all


def attend_back(pairs, q, g, lse, rows, kv, mask, ks, wd, acc, dq):
    mask = jnp.concatenate([mask, mask])
    keys = pl.ds(ks, wd)
    logs = lse[rows, :]
    qs = [stacked(q[rows, pair_cols(i)]) for i in pairs]
    gs = [stacked(g[rows, pair_cols(i)]) for i in pairs]
    scores = [mm_nt(qi, kv[keys, pair_cols(i)]) for qi, i in zip(qs, pairs)]
    dps = [mm_nt(gi, kv[keys, pair_cols(i, D)]) for gi, i in zip(gs, pairs)]
    probs = [jnp.exp(jnp.where(mask, s, NEGATIVE_FILL) - head_col(logs, i)) for s, i in zip(scores, pairs)]
    sums = [jnp.sum(prob * dp, axis=-1, keepdims=True) for prob, dp in zip(probs, dps)]
    dss = [(prob * (dp - total)).astype(BF) for prob, dp, total in zip(probs, dps, sums)]
    for i, gi, prob in zip(pairs, gs, probs):
        acc[pair_cols(i, D), keys] += mm(gi.T, prob.astype(BF))
    for i, qi, ds in zip(pairs, qs, dss):
        acc[pair_cols(i), keys] += mm(qi.T, ds)
    for i, ds in zip(pairs, dss):
        dq[rows, pair_cols(i)] = (unstacked(mm(ds, kv[keys, pair_cols(i)])) * SCALE).astype(BF)


def each_sub(row0, body):
    @pl.loop(0, BLOCK // SUB)
    def _(sub):
        body(sub, pl.ds(pl.multiple_of(sub * SUB, SUB), SUB), pl.multiple_of(row0 + sub * SUB, SUB))


def self_forward(widths, tab, xs, mk, wqkv, wso, kv, q_out, att_out, n0_out, s0_out, lse_out):
    b = pl.program_id(0)
    row0 = pl.multiple_of(tab[1, b], SUB)

    @pl.when(tab[2, b] == 1)
    def _():
        @pl.loop(0, kv.shape[1] // BLOCK)
        def _(i):
            rows = pl.ds(pl.multiple_of(i * BLOCK, BLOCK), BLOCK)
            kv[0, rows, :] = mm(xs[0, rows, :], wqkv[:, D:]).astype(BF)

    x = xs[0, pl.ds(row0, BLOCK), :]
    q_out[...] = mm(x, wqkv[:, :D]).astype(BF) * jnp.asarray(SCALE, BF)
    lse_out[...] = jnp.zeros_like(lse_out)

    def sub_block(sub, rows, at):
        meta = query_meta(mk, at)

        def run(pairs, ks, wd):
            mask = self_mask(mk, meta, at, ks, wd)
            attend(pairs, q_out, rows, kv.at[0], mask, ks, wd, att_out, lse_out)

        by_width(tab[5, 2 * b + sub], tab[4, 2 * b + sub], widths, run)

    each_sub(row0, sub_block)
    r = x.astype(F32) + mm(att_out[...], wso[...])
    normed, inv = norm_stats(r)
    n0_out[...] = normed
    s0_out[...] = jnp.broadcast_to(inv, s0_out.shape)


def middle(
    widths, ff, tab, es, mk, n0, s0, att, cot, wckv, wso, wcq, wco, w1, w2, gains, biases,
    out, gfirst, gself, gline, ffn_grad, att_grad, norm_grad,
    mkv, acc, clse, catt, cq_scr, gatt, dq_scr, hid, gprime, dwckvt, dw1, dw2t, dwco, dwcq, dwso, gb,
):
    b = pl.program_id(0)
    row0 = pl.multiple_of(tab[1, b], SUB)

    @pl.when(b == 0)
    def _():
        for ref in (dwckvt, dw1, dw2t, dwco, dwcq, dwso, gb):
            ref[...] = jnp.zeros_like(ref)

    @pl.when(tab[2, b] == 1)
    def _():
        acc[...] = jnp.zeros_like(acc)

        @pl.loop(0, mkv.shape[0] // BLOCK)
        def _(i):
            rows = pl.ds(pl.multiple_of(i * BLOCK, BLOCK), BLOCK)
            mkv[rows, :] = mm(es[0, rows, :], wckv[...]).astype(BF)

    first = n0[...] * gains[0:1, :] + biases[0:1, :]
    first_low = first.astype(BF)
    cq_scr[...] = mm(first_low, wcq[...]).astype(BF) * jnp.asarray(SCALE, BF)
    clse[...] = jnp.zeros_like(clse)

    def sub_block(sub, rows, at):
        meta = query_meta(mk, at)

        def run(pairs, ks, wd):
            mask = cross_mask(mk, meta, at, ks, wd)
            attend(pairs, cq_scr, rows, mkv, mask, ks, wd, catt, clse)

        by_width(tab[7, 2 * b + sub], tab[6, 2 * b + sub], widths, run)

    each_sub(row0, sub_block)
    n1, s1 = norm_stats(first + mm(catt[...], wco[...]))
    second = n1 * gains[1:2, :] + biases[1:2, :]
    second_low = second.astype(BF)
    chunk = D
    total = second
    for c in range(ff // chunk):
        cols = slice(c * chunk, (c + 1) * chunk)
        v = mm(second_low, w1[:, cols])
        v2 = v * v
        t = jnp.tanh(GELU_C * (v + 0.044715 * (v2 * v)))
        half = 0.5 * (1.0 + t)
        h = (v * half).astype(BF)
        hid[:, cols] = h
        gprime[:, cols] = half + (0.5 * v) * (1.0 - t * t) * (GELU_C + (3 * 0.044715 * GELU_C) * v2)
        total = total + mm(h, w2[cols, :])
    n2, s2 = norm_stats(total)
    out[...] = (n2 * gains[2:3, :] + biases[2:3, :]).astype(BF)
    dy = cot[...].astype(F32)
    gb[2] += fold8(dy * n2)
    gb[5] += fold8(dy)
    gthird = norm_back(dy, n2, s2, gains[2:3, :])
    fg = gthird.astype(BF)
    fgt, sect = fg.T, second_low.T
    back = gthird
    for c in range(ff // chunk):
        cols = slice(c * chunk, (c + 1) * chunk)
        pg = (mm_nt(fg, w2[cols, :]) * gprime[:, cols]).astype(BF)
        dw2t[:, cols] += mm(fgt, hid[:, cols])
        dw1[:, cols] += mm(sect, pg)
        back = back + mm_nt(pg, w1[:, cols])
    gb[1] += fold8(back * n1)
    gb[4] += fold8(back)
    gsecond = norm_back(back, n1, s1, gains[1:2, :])
    cg = gsecond.astype(BF)
    dwco[...] += mm(catt[...].T, cg)
    gatt[...] = mm_nt(cg, wco[...]).astype(BF)

    def sub_block_back(sub, rows, at):
        meta = query_meta(mk, at)

        def run(pairs, ks, wd):
            mask = cross_mask(mk, meta, at, ks, wd)
            attend_back(pairs, cq_scr, gatt, clse, rows, mkv, mask, ks, wd, acc, dq_scr)

        by_width(tab[7, 2 * b + sub], tab[6, 2 * b + sub], widths, run)

    each_sub(row0, sub_block_back)
    dq = dq_scr[...]
    dwcq[...] += mm(first_low.T, dq)
    gf = gsecond + mm_nt(dq, wcq[...])
    gb[0] += fold8(gf * n0[...])
    gb[3] += fold8(gf)
    gf = norm_back(gf, n0[...], s0[:, 0:1], gains[0:1, :])
    gfirst[...] = gf
    sg = gf.astype(BF)
    dwso[...] += mm(att[...].T, sg)
    gself[...] = mm_nt(sg, wso[...]).astype(BF)

    @pl.when(tab[3, b] == 1)
    def _():
        line_end(acc, es, wckv, 0, None, gline, dwckvt)

    @pl.when(b == pl.num_programs(0) - 1)
    def _():
        cols = ffn_grad.shape[2]
        for i in range(ffn_grad.shape[0]):
            ffn_grad[i, :D, :] = dw1[:, i * cols : (i + 1) * cols].astype(BF)
            ffn_grad[i, D:, :] = dw2t[:, i * cols : (i + 1) * cols].astype(BF)
        att_grad[: 2 * D, :] = dwckvt[...].astype(BF)
        for i, ref in enumerate((dwso, dwcq, dwco)):
            att_grad[(2 + i) * D : (3 + i) * D, :] = ref[...].astype(BF)
        norm_grad[...] = jnp.concatenate([jnp.sum(gb[...], axis=1), jnp.zeros((2, D), F32)])


def line_end(acc, inputs, weight, base, rows, gline, dwt):
    columns = 256

    @pl.loop(0, acc.shape[1] // columns)
    def _(i):
        cols = pl.ds(pl.multiple_of(i * columns, columns), columns)
        low = acc[:, cols].astype(BF)
        back = mm(weight[:, base:], low).T
        if rows is not None:
            back = back + rows[cols, :]
        gline[0, cols, :] = back.astype(BF)
        dwt[...] += mm(low, inputs[0, cols, :])


def self_backward(widths, tab, q, g, gf, lse, kv, mk, xs, wqkv, gline, qkv_grad, dq, acc, rows, dwq, dwkvt):
    b = pl.program_id(0)
    row0 = pl.multiple_of(tab[1, b], SUB)

    @pl.when(b == 0)
    def _():
        dwq[...] = jnp.zeros_like(dwq)
        dwkvt[...] = jnp.zeros_like(dwkvt)

    @pl.when(tab[2, b] == 1)
    def _():
        acc[...] = jnp.zeros_like(acc)
        rows[...] = jnp.zeros_like(rows)

    def sub_block(sub, here, at):
        meta = query_meta(mk, at)

        def run(pairs, ks, wd):
            mask = self_mask(mk, meta, at, ks, wd)
            attend_back(pairs, q, g, lse, here, kv.at[0], mask, ks, wd, acc, dq)

        by_width(tab[5, 2 * b + sub], tab[4, 2 * b + sub], widths, run)

    each_sub(row0, sub_block)

    x = xs[0, pl.ds(row0, BLOCK), :]
    dwq[...] += mm(x.T, dq[...])
    rows[pl.ds(row0, BLOCK), :] = gf[...] + mm_nt(dq[...], wqkv[:, :D])

    @pl.when(tab[3, b] == 1)
    def _():
        line_end(acc, xs, wqkv, D, rows, gline, dwkvt)

    @pl.when(b == pl.num_programs(0) - 1)
    def _():
        qkv_grad[:D, :] = dwq[...].astype(BF)
        qkv_grad[D:, :] = dwkvt[...].astype(BF)


def const_spec(shape):
    return pl.BlockSpec(shape, lambda b, t: (0,) * len(shape), pipeline_mode=pl.Buffered(1))


def row_spec(cols):
    return pl.BlockSpec((BLOCK, cols), lambda b, t: (b, 0))


def line_spec(shape):
    return pl.BlockSpec((1,) + shape, lambda b, t: (t[0, b],) + (0,) * len(shape))


def sds(shape, dtype):
    return jax.ShapeDtypeStruct(shape, dtype)


def kernels(
    n, tab, xs, es, cot, mk, self_qkv, self_out, cross_q, cross_kv, cross_out, w1, w2, norm_gain, norm_bias
):
    slots, line_len = xs.shape[0], xs.shape[1]
    rows_all, ff = cot.shape[0], w1.shape[1]
    per, blocks = BLOCK // SUB, rows_all // BLOCK
    widths = widths_for(line_len)
    params = pltpu.CompilerParams(vmem_limit_bytes=VMEM, dimension_semantics=("arbitrary",))

    def call(kernel, name, ins, in_specs, outs, out_specs, scratch, flops):
        return pl.pallas_call(
            kernel,
            name=name,
            grid_spec=pltpu.PrefetchScalarGridSpec(
                num_scalar_prefetch=1,
                grid=(blocks,),
                in_specs=in_specs,
                out_specs=out_specs,
                scratch_shapes=scratch,
            ),
            out_shape=outs,
            compiler_params=params,
            cost_estimate=pl.CostEstimate(
                flops=int(flops), bytes_accessed=16 << 20, transcendentals=1 << 20
            ),
        )(tab, *ins)

    line2 = (line_len, 2 * D)
    kv, q, att, n0, s0, lse = call(
        functools.partial(self_forward, widths),
        "self_forward",
        (xs, mk, self_qkv, self_out),
        [line_spec((line_len, D)), line_spec((8, line_len)), const_spec((D, 3 * D)), const_spec((D, D))],
        (
            sds((slots,) + line2, BF),
            sds((rows_all, D), BF),
            sds((rows_all, D), BF),
            sds((rows_all, D), F32),
            sds((rows_all, 128), F32),
            sds((rows_all, 128), F32),
        ),
        (line_spec(line2), row_spec(D), row_spec(D), row_spec(D), row_spec(128), row_spec(128)),
        [],
        2e10,
    )

    out, gfirst, gself, enc_line, ffn_grad, att_grad, norm_grad = call(
        functools.partial(middle, widths, ff),
        "middle",
        (es, mk, n0, s0, att, cot, cross_kv, self_out, cross_q, cross_out, w1, w2, norm_gain, norm_bias),
        [
            line_spec((line_len, D)), line_spec((8, line_len)), row_spec(D), row_spec(128), row_spec(D),
            row_spec(D), const_spec((D, 2 * D)), const_spec((D, D)), const_spec((D, D)),
            const_spec((D, D)), const_spec((D, ff)), const_spec((ff, D)), const_spec((3, D)),
            const_spec((3, D)),
        ],
        (
            sds((rows_all, D), BF),
            sds((rows_all, D), F32),
            sds((rows_all, D), BF),
            sds((slots, line_len, D), BF),
            sds((n, 2 * D, ff // n), BF),
            sds((5 * D, D), BF),
            sds((8, D), F32),
        ),
        (
            row_spec(D), row_spec(D), row_spec(D), line_spec((line_len, D)), const_spec((n, 2 * D, ff // n)),
            const_spec((5 * D, D)), const_spec((8, D)),
        ),
        [
            pltpu.VMEM(line2, BF),
            pltpu.VMEM((2 * D, line_len), F32),
            pltpu.VMEM((BLOCK, 128), F32),
            pltpu.VMEM((BLOCK, D), BF),
            pltpu.VMEM((BLOCK, D), BF),
            pltpu.VMEM((BLOCK, D), BF),
            pltpu.VMEM((BLOCK, D), BF),
            pltpu.VMEM((BLOCK, ff), BF),
            pltpu.VMEM((BLOCK, ff), F32),
            pltpu.VMEM((2 * D, D), F32),
            pltpu.VMEM((D, ff), F32),
            pltpu.VMEM((D, ff), F32),
            pltpu.VMEM((D, D), F32),
            pltpu.VMEM((D, D), F32),
            pltpu.VMEM((D, D), F32),
            pltpu.VMEM((6, 8, D), F32),
        ],
        8e10,
    )

    stream_line, qkv_grad = call(
        functools.partial(self_backward, widths),
        "self_backward",
        (q, gself, gfirst, lse, kv, mk, xs, self_qkv),
        [
            row_spec(D), row_spec(D), row_spec(D), row_spec(128), line_spec(line2), line_spec((8, line_len)),
            line_spec((line_len, D)), const_spec((D, 3 * D)),
        ],
        (sds((slots, line_len, D), BF), sds((3 * D, D), BF)),
        (line_spec((line_len, D)), const_spec((3 * D, D))),
        [
            pltpu.VMEM((BLOCK, D), BF),
            pltpu.VMEM((2 * D, line_len), F32),
            pltpu.VMEM((line_len, D), F32),
            pltpu.VMEM((D, D), F32),
            pltpu.VMEM((2 * D, D), F32),
        ],
        3e10,
    )
    return out, enc_line, stream_line, ffn_grad, att_grad, qkv_grad, norm_grad


def seq_barrier(n, me):
    barrier = pltpu.get_barrier_semaphore()
    for o in range(1, n):
        pl.semaphore_signal(
            barrier, inc=1, device_id={"seq": (me + o) % n}, device_id_type=pl.DeviceIdType.MESH
        )
    pl.semaphore_wait(barrier, n - 1)


def remote(src, dst, send, recv, device):
    return pltpu.make_async_remote_copy(
        src_ref=src, dst_ref=dst, send_sem=send, recv_sem=recv, device_id={"seq": device},
        device_id_type=pl.DeviceIdType.MESH,
    )


def part_of(device, p):
    return (device % p + device // p) % p


class Exchange:
    def __init__(self, lines, n, line_len):
        self.n, self.piece = n, line_len // n
        self.whole, self.p, self.k = plan(lines, n)
        self.groups = n // self.p
        self.chunks = n // self.p
        self.part_len = line_len // self.p
        self.line_len = line_len
        self.shared0 = self.whole * n
        self.rows_p = self.k * self.part_len
        self.me = lax.axis_index("seq")
        self.group = self.me // self.p
        self.part = part_of(self.me, self.p)
        self.pos_part, self.pos_chunk = self.me // self.chunks, self.me % self.chunks

    def owner(self, group):
        return group * self.p + (self.pos_part + self.p * self.groups - group) % self.p


def in_kernel(ex, x_ref, rc_ref, e_ref, c_ref, xs, rc, es, cot, sem_w, sem_p, sem_f, sem_l):
    n, piece, w, k, me = ex.n, ex.piece, ex.whole, ex.k, ex.me
    seq_barrier(n, me)
    spans = pl.ds(pl.multiple_of(me * piece, piece), piece)
    names = (x_ref, rc_ref, e_ref, c_ref)

    def line_dst(out, slots):
        if out is rc:
            return rc.at[slots, me]
        return out.at[slots, spans]

    def whole_copies(a, o):
        to = (me + o) % n
        src = names[a]
        if a == 3:
            pairs = [
                (
                    src.at[to * w + i],
                    cot.at[pl.ds(pl.multiple_of(ex.rows_p + i * ex.line_len + me * piece, piece), piece)],
                )
                for i in range(w)
            ]
        else:
            pairs = [(src.at[pl.ds(to * w, w)], line_dst((xs, rc, es)[a], pl.ds(k, w)))] if w else []
        return [
            remote(s, d, sem_w.at[0, a, i, o], sem_w.at[1, a, i, o], to)
            if o
            else pltpu.make_async_copy(s, d, sem_l.at[a, i])
            for i, (s, d) in enumerate(pairs)
        ]

    def shared_pairs(a, group):
        src = names[a]
        first = ex.shared0 + group * k
        if a == 3:
            return [
                (
                    src.at[first + i],
                    cot.at[pl.ds(pl.multiple_of(i * ex.part_len + ex.pos_chunk * piece, piece), piece)],
                )
                for i in range(k)
            ]
        return [(src.at[pl.ds(first, k)], line_dst((xs, rc, es)[a], pl.ds(0, k)))] if k else []

    def shared_send(a, u):
        group = (ex.group + u) % ex.groups
        to = ex.owner(group)
        return [
            remote(s, d, sem_p.at[0, a, i, u], sem_p.at[1, a, i, ex.pos_chunk], to)
            for i, (s, d) in enumerate(shared_pairs(a, group))
        ]

    def shared_local(a):
        return [
            pltpu.make_async_copy(s, d, sem_l.at[a, max(w, 1) + i])
            for i, (s, d) in enumerate(shared_pairs(a, ex.group))
        ]

    def shared_arrival(a, j):
        return [
            remote(s, d, sem_p.at[0, a, i, 0], sem_p.at[1, a, i, j], me)
            for i, (s, d) in enumerate(shared_pairs(a, ex.group))
        ]

    def forwards(a):
        out = (xs, rc, es)[a]
        mine = ex.part * ex.part_len
        if a == 1:
            view = rc.at[pl.ds(0, k), pl.ds(ex.part * ex.chunks, ex.chunks)]
        else:
            view = out.at[pl.ds(0, k), pl.ds(pl.multiple_of(mine, ex.part_len), ex.part_len)]
        return [
            remote(view, view, sem_f.at[0, a, v], sem_f.at[1, a, v], ex.group * ex.p + (me % ex.p + v) % ex.p)
            for v in range(1, ex.p)
        ]

    here = ex.pos_part == ex.part
    for a in range(4):
        for u in range(ex.groups if k else 0):
            if u == 0:

                @pl.when(here)
                def _():
                    for copy in shared_local(a):
                        copy.start()

                @pl.when(jnp.logical_not(here))
                def _():
                    for copy in shared_send(a, 0):
                        copy.start()

            else:
                for copy in shared_send(a, u):
                    copy.start()
        for o in range(n):
            for copy in whole_copies(a, o):
                copy.start()
    for a in range(4):
        for j in range(ex.chunks if k else 0):
            own = ex.part * ex.chunks + j == me

            @pl.when(own)
            def _():
                for copy in shared_local(a):
                    copy.wait()

            @pl.when(jnp.logical_not(own))
            def _():
                for copy in shared_arrival(a, j):
                    copy.wait_recv()

        if a < 3 and k:
            for copy in forwards(a):
                copy.start()
    for a in range(4):
        for o in range(n):
            for copy in whole_copies(a, o):
                copy.wait()
        for u in range(ex.groups if k else 0):
            if u == 0:

                @pl.when(jnp.logical_not(here))
                def _():
                    for copy in shared_send(a, 0):
                        copy.wait_send()

            else:
                for copy in shared_send(a, u):
                    copy.wait_send()
        if a < 3 and k:
            for copy in forwards(a):
                copy.wait()


def exchange_in(stream, rc, encoder, cotangent, lines, n, line_len):
    whole, p, k = plan(lines, n)
    slots, piece = k + whole, line_len // n
    rows_all = k * (line_len // p) + whole * line_len
    most = max(k, whole, 1)

    def kernel(*refs):
        in_kernel(Exchange(lines, n, line_len), *refs)

    dma = pltpu.SemaphoreType.DMA
    return pl.pallas_call(
        kernel,
        name="exchange_in",
        in_specs=[pl.BlockSpec(memory_space=pl.ANY)] * 4,
        out_specs=[pl.BlockSpec(memory_space=pl.ANY)] * 4,
        out_shape=(
            sds((slots, line_len, D), BF),
            sds((slots, n, 1, piece), jnp.int32),
            sds((slots, line_len, D), BF),
            sds((rows_all, D), BF),
        ),
        scratch_shapes=[
            dma((2, 4, most, n)), dma((2, 4, most, n)), dma((2, 3, max(p, 2))), dma((4, 2 * most)),
        ],
        compiler_params=pltpu.CompilerParams(collective_id=1, has_side_effects=True),
    )(stream, rc, encoder, cotangent)


class Dim:
    def __init__(self, axis, stride, size):
        self.axis, self.stride, self.size = axis, stride, size
        at = lax.axis_index(axis)
        self.index = at // stride % size
        self.rest = at - self.index * stride

    def peer(self, v):
        return (self.index + v) % self.size

    def device(self, v):
        return {self.axis: self.rest + self.peer(v) * self.stride}


def flat_loop(lead, run):
    @pl.loop(0, math.prod(lead))
    def _(i):
        index = []
        for size in reversed(lead):
            index.append(i % size)
            i = i // size
        run(tuple(reversed(index)))


def add_into(dst, sources, lead):
    def run(index):
        total = dst[index].astype(F32)
        for source in sources:
            total = total + source[index].astype(F32)
        dst[index] = total.astype(dst.dtype)

    flat_loop(lead, run)


def finish_kernel(
    ex, out_rows, enc_line, stream_line, ffn_grad, att_grad, qkv_grad, norm_grad,
    out, enc, stream, ffn, att, norms,
    ffn_v, att_v, norm_v, ffn_bufs, att_bufs, norm_bufs, own_v, part_v,
    sem_red, sem_w, sem_p, sem_l, sem_s, sem_in,
):
    n, piece, w, k, p, me = ex.n, ex.piece, ex.whole, ex.k, ex.p, ex.me
    outer = lax.axis_size("dp") // 2
    core, yy = Dim("dp", 1, 2), Dim("dp", 2, outer)
    xx, zz = Dim("seq", 1, p), Dim("seq", p, ex.groups)
    barrier = pltpu.get_barrier_semaphore()
    greeted = [{"seq": (me + o) % n} for o in range(1, n)]
    greeted += [dim.device(v) for dim in (core, yy) for v in range(1, dim.size)]
    for device in greeted:
        pl.semaphore_signal(barrier, inc=1, device_id=device, device_id_type=pl.DeviceIdType.MESH)

    loads = [
        pltpu.make_async_copy(ffn_grad, ffn_v, sem_in.at[0]),
        pltpu.make_async_copy(att_grad, att_v.at[pl.ds(0, 5 * D)], sem_in.at[1]),
        pltpu.make_async_copy(qkv_grad, att_v.at[pl.ds(5 * D, 3 * D)], sem_in.at[2]),
        pltpu.make_async_copy(norm_grad, norm_v, sem_in.at[3]),
    ]
    lines = (enc_line, stream_line)
    mine = pl.ds(pl.multiple_of(ex.part * ex.part_len, ex.part_len), ex.part_len)
    if k:
        loads += [
            pltpu.make_async_copy(lines[a].at[pl.ds(0, k), mine], own_v.at[a], sem_in.at[4 + a])
            for a in range(2)
        ]
    for copy in loads:
        copy.start()
    pl.semaphore_wait(barrier, len(greeted))

    def send(src, dst, sems, device):
        return pltpu.make_async_remote_copy(
            src_ref=src, dst_ref=dst, send_sem=sems[0], recv_sem=sems[1], device_id=device,
            device_id_type=pl.DeviceIdType.MESH,
        )

    fl = ffn_v.shape
    rows = fl[1] // (2 * outer)
    ffn_6 = ffn_v.reshape(ex.groups, p, outer, 2, rows, fl[2])
    att_rows = att_v.shape[0] // (2 * outer * n)
    att_6 = att_v.reshape(2, p, outer, ex.groups, att_rows, D)
    ffn_o = ffn.reshape(outer, 2, rows, fl[2])
    att_o = att.reshape(2, p, outer, ex.groups, att_rows, D)
    c, y, x, z = core.index, yy.index, xx.index, zz.index
    sem_at = [0]

    def next_sem():
        sem_at[0] += 1
        return sem_red.at[0, sem_at[0] - 1], sem_red.at[1, sem_at[0] - 1]

    def scatter(dim, view, buf, lead):
        copies = [
            send(view(dim.peer(v)), buf.at[v - 1], next_sem(), dim.device(v)) for v in range(1, dim.size)
        ]

        def finish():
            for copy in copies:
                copy.wait()
            add_into(view(dim.index), [buf.at[v - 1] for v in range(1, dim.size)], lead)

        return copies, finish

    def gather(dim, view):
        copies = [send(view, view, next_sem(), dim.device(v)) for v in range(1, dim.size)]

        def finish():
            for copy in copies:
                copy.wait()

        return copies, finish

    def place(src, dst, sem):
        copy = pltpu.make_async_copy(src, dst, sem)
        return [copy], copy.wait

    def exchange_all(dim, buf):
        copies = [send(norm_v, buf.at[v - 1], next_sem(), dim.device(v)) for v in range(1, dim.size)]

        def finish():
            for copy in copies:
                copy.wait()
            norm_v[...] = sum([buf[v - 1] for v in range(1, dim.size)], norm_v[...])

        return copies, finish

    g, o = ex.groups, outer
    streams = [
        [
            scatter(core, lambda t: ffn_6.at[:, :, :, t], ffn_bufs[0], (g, p, o)),
            scatter(yy, lambda t: ffn_6.at[:, :, t, c], ffn_bufs[1], (g, p)),
            scatter(xx, lambda t: ffn_6.at[:, t, y, c], ffn_bufs[2], (g,)),
            scatter(zz, lambda t: ffn_6.at[t, x, y, c], ffn_bufs[3], ()),
            place(ffn_6.at[z, x, y, c], ffn_o.at[y, c], sem_in.at[6]),
            gather(yy, ffn_o.at[y, c]),
            gather(core, ffn_o.at[:, c]),
        ],
        [
            scatter(core, lambda t: att_6.at[t], att_bufs[0], (p, o, g)),
            scatter(xx, lambda t: att_6.at[c, t], att_bufs[1], (o, g)),
            scatter(yy, lambda t: att_6.at[c, x, t], att_bufs[2], (g,)),
            scatter(zz, lambda t: att_6.at[c, x, y, t], att_bufs[3], ()),
            place(att_6.at[c, x, y, z], att_o.at[c, x, y, z], sem_in.at[7]),
            gather(zz, att_o.at[c, x, y, z]),
            gather(yy, att_o.at[c, x, y]),
            gather(xx, att_o.at[c, x]),
            gather(core, att_o.at[c]),
        ],
        [exchange_all(dim, norm_bufs[i]) for i, dim in enumerate((core, yy, xx, zz))],
    ]

    def whole_src(a, i, to):
        if a == 0:
            at = ex.rows_p + i * ex.line_len + to * piece
            return out_rows.at[pl.ds(pl.multiple_of(at, piece), piece)]
        return lines[a - 1].at[k + i, pl.ds(pl.multiple_of(to * piece, piece), piece)]

    outs = (out, enc, stream)

    def whole_copies(a, v):
        to = (me + v) % n
        result = []
        for i in range(w):
            src, dst = whole_src(a, i, to), outs[a].at[me * w + i]
            result.append(
                send(src, dst, (sem_w.at[0, a, i, v], sem_w.at[1, a, i, v]), {"seq": to})
                if v
                else pltpu.make_async_copy(src, dst, sem_l.at[a, i])
            )
        return result

    def shared_pair(a, i, j):
        at = pl.ds(pl.multiple_of(j * piece, piece), piece)
        if a == 0:
            src = out_rows.at[pl.ds(pl.multiple_of(i * ex.part_len + j * piece, piece), piece)]
        else:
            src = own_v.at[a - 1, i, at]
        return src, outs[a].at[ex.shared0 + ex.group * k + i]

    def shared_copies(a, u):
        j = (ex.group + u) % ex.chunks
        to = ex.part * ex.chunks + j
        return to, [
            send(*shared_pair(a, i, j), (sem_p.at[0, a, i, u], sem_p.at[1, a, i, ex.group]), {"seq": to})
            for i in range(k)
        ]

    def local_copies(a):
        return [
            pltpu.make_async_copy(*shared_pair(a, i, ex.pos_chunk), sem_l.at[a, max(w, 1) + i])
            for i in range(k)
        ]

    def each_shared(a, remote_run, local_run):
        for u in range(ex.chunks if k else 0):
            to, copies = shared_copies(a, u)

            @pl.when(to != me)
            def _():
                for copy in copies:
                    remote_run(copy)

            @pl.when(to == me)
            def _():
                for copy in local_copies(a):
                    local_run(copy)

    def sharing(a, v):
        part = (ex.part + v) % p
        theirs = pl.ds(pl.multiple_of(part * ex.part_len, ex.part_len), ex.part_len)
        return send(
            lines[a].at[pl.ds(0, k), theirs], part_v.at[a, v - 1], (sem_s.at[0, a, v], sem_s.at[1, a, v]),
            xx.device(v),
        )

    for copy in loads:
        copy.wait()
    for stages in streams:
        for copy in stages[0][0]:
            copy.start()
    shares = [sharing(a, v) for a in range(2) for v in range(1, p)] if k else []
    for copy in shares:
        copy.start()
    for a in range(3):
        for v in range(n):
            for copy in whole_copies(a, v):
                copy.start()
    each_shared(0, lambda copy: copy.start(), lambda copy: copy.start())
    if k:
        for copy in shares:
            copy.wait()
        for a in range(2):
            add_into(own_v.at[a], [part_v.at[a, v - 1] for v in range(1, p)], (k,))
        for a in (1, 2):
            each_shared(a, lambda copy: copy.start(), lambda copy: copy.start())
    for stage in range(max(len(stages) for stages in streams)):
        for stages in streams:
            if stage < len(stages):
                stages[stage][1]()
            if stage + 1 < len(stages):
                for copy in stages[stage + 1][0]:
                    copy.start()
    norms[...] = norm_v[...]
    for a in range(3):
        for v in range(n):
            for copy in whole_copies(a, v):
                copy.wait()
        each_shared(a, lambda copy: copy.wait_send(), lambda copy: copy.wait())
        for group in range(ex.groups if k else 0):

            @pl.when(ex.owner(group) != me)
            def _():
                for i in range(k):
                    sems = (sem_p.at[0, a, i, 0], sem_p.at[1, a, i, group])
                    send(*shared_pair(a, i, 0), sems, {"seq": me}).wait_recv()


def finish(arrays, lines, n, line_len, dp):
    whole, p, k = plan(lines, n)
    piece, most, groups, outer = line_len // n, max(k, whole, 1), n // p, dp // 2
    cols = arrays[3].shape[2]
    rows, att_rows = 2 * D // dp, 8 * D // (dp * n)
    part_len = line_len // p
    slots = max(k, 1)

    def kernel(*refs):
        refs = list(refs)
        grouped = refs[:16] + [refs[16:20], refs[20:24], refs[24:28]] + refs[28:]
        finish_kernel(Exchange(lines, n, line_len), *grouped)

    dma = pltpu.SemaphoreType.DMA
    hops = (1, outer - 1, p - 1, groups - 1)
    hbm = pl.BlockSpec(memory_space=pl.ANY)
    vmem = pl.BlockSpec(memory_space=pltpu.VMEM)
    at_least = lambda q: max(q, 1)
    return pl.pallas_call(
        kernel,
        name="finish",
        in_specs=[hbm] * 7,
        out_specs=[hbm] * 3 + [vmem] * 3,
        out_shape=[sds((lines, piece, D), BF)] * 3
        + [sds((2 * D, cols), BF), sds((8 * D, D), BF), sds((8, D), F32)],
        scratch_shapes=[
            pltpu.VMEM((n, 2 * D, cols), BF),
            pltpu.VMEM((8 * D, D), BF),
            pltpu.VMEM((8, D), F32),
            pltpu.VMEM((1, groups, p, outer, rows, cols), BF),
            pltpu.VMEM((at_least(outer - 1), groups, p, rows, cols), BF),
            pltpu.VMEM((at_least(p - 1), groups, rows, cols), BF),
            pltpu.VMEM((at_least(groups - 1), rows, cols), BF),
            pltpu.VMEM((1, p, outer, groups, att_rows, D), BF),
            pltpu.VMEM((at_least(p - 1), outer, groups, att_rows, D), BF),
            pltpu.VMEM((at_least(outer - 1), groups, att_rows, D), BF),
            pltpu.VMEM((at_least(groups - 1), att_rows, D), BF),
            *[pltpu.VMEM((at_least(q), 8, D), F32) for q in hops],
            pltpu.VMEM((2, slots, part_len, D), BF),
            pltpu.VMEM((2, at_least(p - 1), slots, part_len, D), BF),
            dma((2, 4 * sum(hops) + 8)),
            dma((2, 3, most, n)),
            dma((2, 3, most, n)),
            dma((3, 2 * most)),
            dma((2, 2, max(p, 2))),
            dma((8,)),
        ],
        compiler_params=pltpu.CompilerParams(
            collective_id=2, has_side_effects=True, vmem_limit_bytes=VMEM
        ),
    )(*arrays)


def doc_numbers(bounds, places):
    return jnp.sum((bounds[:, None, :] <= places[None, :, None]).astype(jnp.int32), axis=2)


def body(
    stream, encoder, cotangent, self_qkv, self_out, cross_q, cross_kv, cross_out, ffn_in, ffn_out,
    norm_gain, norm_bias, lengths, enc_lengths, ranks, cuts,
):
    n = lax.axis_size("seq")
    me = lax.axis_index("seq")
    lines, piece = stream.shape[0], stream.shape[1]
    line_len = piece * n
    whole, p, k = plan(lines, n)
    groups = n // p
    slots = k + whole
    part_len = line_len // p
    rows_p, rows_w = k * part_len, whole * line_len
    rows_all = rows_p + rows_w
    ff = ffn_in.shape[1] * n
    group, part = me // p, part_of(me, p)
    widths = widths_for(line_len)
    i32 = jnp.int32

    cost = jnp.sum(lengths * lengths, axis=1)
    order = jnp.arange(lines, dtype=i32)
    lighter = (cost[None, :] < cost[:, None]) | (
        (cost[None, :] == cost[:, None]) & (order[None, :] < order[:, None])
    )
    rank = jnp.sum(lighter.astype(i32), axis=1)
    slot_of = jnp.where(rank < whole * n, rank, whole * n + lines - 1 - rank)
    line_of = jnp.sum(jnp.where(slot_of[None, :] == order[:, None], order[None, :], 0), axis=1)

    rc_in = (ranks * 32 + cuts)[line_of][:, None, :]
    xs, rc, es, cot = exchange_in(
        stream[line_of], rc_in, encoder[line_of], cotangent[line_of], lines, n, line_len
    )
    rc = rc.reshape(slots, line_len)
    w1 = lax.all_gather(ffn_in, "seq", axis=1, tiled=True)
    w2 = lax.all_gather(ffn_out, "seq", axis=0, tiled=True)

    own_slots = jnp.concatenate([whole * n + group * k + jnp.arange(k), me * whole + jnp.arange(whole)])
    mine = line_of[own_slots.astype(i32)]
    cum_t = jnp.cumsum(lengths[mine], axis=1)
    cum_e = jnp.cumsum(enc_lengths[mine], axis=1)
    places = jnp.arange(line_len, dtype=i32)
    doc = doc_numbers(cum_t, places)
    src = doc_numbers(cum_e, places)
    zero = jnp.zeros_like(rc)
    mk = jnp.stack([doc, rc // 32, rc % 32, src, zero, zero, zero, zero], axis=1).astype(F32)

    block_line = [j for j in range(k) for _ in range(part_len // BLOCK)]
    block_line += [k + j for j in range(whole) for _ in range(line_len // BLOCK)]
    block_row = [r * BLOCK for j in range(k) for r in range(part_len // BLOCK)]
    block_row += [r * BLOCK for j in range(whole) for r in range(line_len // BLOCK)]
    blocks = len(block_line)
    begin = [int(i == 0 or block_line[i] != block_line[i - 1]) for i in range(blocks)]
    end = [int(i == blocks - 1 or block_line[i] != block_line[i + 1]) for i in range(blocks)]
    per = BLOCK // SUB
    bl = jnp.asarray(block_line, i32)
    br = jnp.asarray(block_row, i32) + jnp.where(bl < k, part * part_len, 0)
    sub_line = jnp.repeat(bl, per)
    sub_row = jnp.repeat(br, per) + jnp.tile(jnp.arange(per, dtype=i32) * SUB, blocks)
    ct, ce = cum_t[sub_line], cum_e[sub_line]
    before = ct <= sub_row[:, None]
    after = ct > sub_row[:, None] + (SUB - 1)

    def key_range(bounds):
        start = jnp.max(jnp.where(before, bounds, 0), axis=1)
        stop = jnp.min(jnp.where(after, bounds, line_len), axis=1)
        ks = start // SUB * SUB
        table = jnp.asarray([wd for wd, _ in widths], i32)
        var = jnp.sum((stop - ks)[:, None] > table[None, :], axis=1).astype(i32)
        wd = jnp.sum(jnp.where(var[:, None] == jnp.arange(len(widths)), table[None, :], 0), axis=1)
        return jnp.minimum(ks, line_len - wd), var

    sks, svar = key_range(ct)
    cks, cvar = key_range(ce)
    pad = jnp.zeros((blocks * (per - 1),), i32)
    wide = lambda v: jnp.concatenate([jnp.asarray(v, i32), pad])
    tab = jnp.stack([wide(bl), wide(br), wide(begin), wide(end), sks, svar, cks, cvar])

    arrays = kernels(
        n, tab, xs, es, cot, mk, self_qkv, self_out, cross_q, cross_kv, cross_out, w1, w2, norm_gain, norm_bias
    )
    output, encoder_grad, stream_grad, ffn, att, norms = finish(
        arrays, lines, n, line_len, lax.axis_size("dp")
    )
    ffn, att = ffn.astype(F32), att.astype(F32)
    square = lambda i: att[i * D : (i + 1) * D]
    return (
        output[slot_of],
        stream_grad[slot_of].astype(F32),
        encoder_grad[slot_of].astype(F32),
        jnp.concatenate([square(5), square(6).T, square(7).T], axis=1),
        square(2),
        square(3),
        jnp.concatenate([square(0).T, square(1).T], axis=1),
        square(4),
        ffn[:D],
        ffn[D:].T,
        norms[:3],
        norms[3:6],
    )


def solution(mesh):
    lines = P("dp", "seq", None)
    in_specs = (
        lines, lines, lines, P(), P(), P(), P(), P(), P(None, "seq"), P("seq", None), P(), P(),
        P("dp", None), P("dp", None), P("dp", "seq"), P("dp", "seq"),
    )
    out_specs = (
        lines, lines, lines, P(), P(), P(), P(), P(), P(None, "seq"), P("seq", None), P(), P(),
    )
    return jax.shard_map(body, mesh=mesh, in_specs=in_specs, out_specs=out_specs, check_vma=False)
```

```python
import functools
import math

import jax
import jax.numpy as jnp
from jax import lax
from jax.experimental import pallas as pl
from jax.experimental.pallas import tpu as pltpu
from jax.sharding import PartitionSpec as P

D = 512
HEADS = 8
HEAD = 64
PAIR = 2 * HEAD
PAIRS = HEADS // 2
NEGATIVE_FILL = -1e30
EPSILON = 1e-05
SCALE = HEAD ** (-0.5)
BLOCK = 256
SUB = 128
BF = jnp.bfloat16
F32 = jnp.float32
NT = (((1,), (1,)), ((), ()))
GELU_C = math.sqrt(2.0 / math.pi)
VMEM = 60 * 1024 * 1024


def mm(left, right):
    return jnp.dot(left, right, preferred_element_type=F32)


def mm_nt(left, right):
    return lax.dot_general(left, right, NT, preferred_element_type=F32)


def plan(lines, n):
    whole = lines // n
    rest = lines - whole * n
    groups = math.gcd(rest, n) if rest else n
    return whole, n // groups, rest // groups


def widths_for(line_len):
    some = ((256, 4), (384, 4), (512, 4), (640, 2))
    return tuple(w for w in some if w[0] < line_len) + ((line_len, 2),)


def norm_stats(r):
    centred = r - jnp.mean(r, axis=-1, keepdims=True)
    inv = lax.rsqrt(jnp.mean(centred * centred, axis=-1, keepdims=True) + EPSILON)
    return centred * inv, inv


def norm_back(dy, normed, inv, gain):
    scaled = dy * gain
    inner = (
        scaled
        - jnp.mean(scaled, axis=-1, keepdims=True)
        - normed * jnp.mean(scaled * normed, axis=-1, keepdims=True)
    )
    return inner * inv


def fold8(t):
    return jnp.sum(t.reshape(t.shape[0] // 8, 8, t.shape[1]), axis=0)


def head_lanes(half):
    lane = lax.broadcasted_iota(jnp.int32, (1, PAIR), 1)
    return (lane < HEAD) if half == 0 else (lane >= HEAD)


def query_meta(mk, at):
    return mk[0, :, pl.ds(at, SUB)].T


def self_mask(mk, meta, at, ks, wd):
    doc = mk[0, 0:1, pl.ds(ks, wd)] == meta[:, 0:1]
    low = mk[0, 1:2, pl.ds(ks, wd)] < meta[:, 2:3]
    key = lax.broadcasted_iota(jnp.int32, (SUB, wd), 1) + ks
    query = lax.broadcasted_iota(jnp.int32, (SUB, wd), 0) + at
    return doc & (low | (key == query))


def cross_mask(mk, meta, at, ks, wd):
    return mk[0, 3:4, pl.ds(ks, wd)] == meta[:, 0:1]


def by_width(var, ks, widths, run):
    ks = pl.multiple_of(ks, SUB)
    for index, (wd, together) in enumerate(widths):

        @pl.when(var == index)
        def _(wd=wd, together=together):
            if together == PAIRS:
                run(tuple(range(PAIRS)), ks, wd)
            else:

                @pl.loop(0, PAIRS // together)
                def _(i):
                    run(tuple(i * together + j for j in range(together)), ks, wd)


def stacked(t):
    zero = jnp.zeros((), t.dtype)
    return jnp.concatenate([jnp.where(head_lanes(half), t, zero) for half in range(2)])


def unstacked(t):
    return jnp.where(head_lanes(0), t[:SUB], t[SUB:])


def pair_cols(pair, base=0):
    if isinstance(pair, int):
        return slice(base + pair * PAIR, base + (pair + 1) * PAIR)
    return pl.ds(pl.multiple_of(base + pair * PAIR, PAIR), PAIR)


def head_col(values, pair):
    if isinstance(pair, int):
        return jnp.concatenate([values[:, 2 * pair : 2 * pair + 1], values[:, 2 * pair + 1 : 2 * pair + 2]])
    lane = lax.broadcasted_iota(jnp.int32, values.shape, 1)
    pick = lambda head: jnp.sum(jnp.where(lane == head, values, 0.0), axis=-1, keepdims=True)
    return jnp.concatenate([pick(2 * pair), pick(2 * pair + 1)])


def attend(pairs, q, rows, kv, mask, ks, wd, out, lse):
    mask = jnp.concatenate([mask, mask])
    keys = pl.ds(ks, wd)
    lane = lax.broadcasted_iota(jnp.int32, (SUB, 128), 1)
    scores = [mm_nt(stacked(q[rows, pair_cols(i)]), kv[keys, pair_cols(i)]) for i in pairs]
    scores = [jnp.where(mask, s, NEGATIVE_FILL) for s in scores]
    tops = [jnp.max(s, axis=-1, keepdims=True) for s in scores]
    exps = [jnp.exp(s - top) for s, top in zip(scores, tops)]
    sums = [jnp.sum(e, axis=-1, keepdims=True) for e in exps]
    probs = [(e * (1.0 / total)).astype(BF) for e, total in zip(exps, sums)]
    outs = [mm(prob, kv[keys, pair_cols(i, D)]) for prob, i in zip(probs, pairs)]
    logs_all = lse[rows, :]
    for i, o, top, total in zip(pairs, outs, tops, sums):
        out[rows, pair_cols(i)] = unstacked(o).astype(BF)
        logs = top + jnp.log(total)
        logs_all = jnp.where(lane == 2 * i, logs[:SUB], logs_all)
        logs_all = jnp.where(lane == 2 * i + 1, logs[SUB:], logs_all)
    lse[rows, :] = logs_all


def attend_back(pairs, q, g, lse, rows, kv, mask, ks, wd, acc, dq):
    mask = jnp.concatenate([mask, mask])
    keys = pl.ds(ks, wd)
    logs = lse[rows, :]
    qs = [stacked(q[rows, pair_cols(i)]) for i in pairs]
    gs = [stacked(g[rows, pair_cols(i)]) for i in pairs]
    scores = [mm_nt(qi, kv[keys, pair_cols(i)]) for qi, i in zip(qs, pairs)]
    dps = [mm_nt(gi, kv[keys, pair_cols(i, D)]) for gi, i in zip(gs, pairs)]
    probs = [jnp.exp(jnp.where(mask, s, NEGATIVE_FILL) - head_col(logs, i)) for s, i in zip(scores, pairs)]
    sums = [jnp.sum(prob * dp, axis=-1, keepdims=True) for prob, dp in zip(probs, dps)]
    dss = [(prob * (dp - total)).astype(BF) for prob, dp, total in zip(probs, dps, sums)]
    for i, gi, prob in zip(pairs, gs, probs):
        acc[pair_cols(i, D), keys] += mm(gi.T, prob.astype(BF))
    for i, qi, ds in zip(pairs, qs, dss):
        acc[pair_cols(i), keys] += mm(qi.T, ds)
    for i, ds in zip(pairs, dss):
        dq[rows, pair_cols(i)] = (unstacked(mm(ds, kv[keys, pair_cols(i)])) * SCALE).astype(BF)


def each_sub(row0, body):
    @pl.loop(0, BLOCK // SUB)
    def _(sub):
        body(sub, pl.ds(pl.multiple_of(sub * SUB, SUB), SUB), pl.multiple_of(row0 + sub * SUB, SUB))


def self_forward(widths, tab, xs, mk, wqkv, wso, kv, q_out, att_out, n0_out, s0_out, lse_out):
    b = pl.program_id(0)
    row0 = pl.multiple_of(tab[1, b], SUB)

    @pl.when(tab[2, b] == 1)
    def _():
        @pl.loop(0, kv.shape[1] // BLOCK)
        def _(i):
            rows = pl.ds(pl.multiple_of(i * BLOCK, BLOCK), BLOCK)
            kv[0, rows, :] = mm(xs[0, rows, :], wqkv[:, D:]).astype(BF)

    x = xs[0, pl.ds(row0, BLOCK), :]
    q_out[...] = mm(x, wqkv[:, :D]).astype(BF) * jnp.asarray(SCALE, BF)
    lse_out[...] = jnp.zeros_like(lse_out)

    def sub_block(sub, rows, at):
        meta = query_meta(mk, at)

        def run(pairs, ks, wd):
            mask = self_mask(mk, meta, at, ks, wd)
            attend(pairs, q_out, rows, kv.at[0], mask, ks, wd, att_out, lse_out)

        by_width(tab[5, 2 * b + sub], tab[4, 2 * b + sub], widths, run)

    each_sub(row0, sub_block)
    r = x.astype(F32) + mm(att_out[...], wso[...])
    normed, inv = norm_stats(r)
    n0_out[...] = normed
    s0_out[...] = jnp.broadcast_to(inv, s0_out.shape)


def cross_forward(widths, tab, es, mk, n0, wckv, wcq, gains, biases, mkv, cq, catt, clse):
    b = pl.program_id(0)
    row0 = pl.multiple_of(tab[1, b], SUB)

    @pl.when(tab[2, b] == 1)
    def _():
        @pl.loop(0, mkv.shape[1] // BLOCK)
        def _(i):
            rows = pl.ds(pl.multiple_of(i * BLOCK, BLOCK), BLOCK)
            mkv[0, rows, :] = mm(es[0, rows, :], wckv[...]).astype(BF)

    first = n0[...] * gains[0:1, :] + biases[0:1, :]
    cq[...] = mm(first.astype(BF), wcq[...]).astype(BF) * jnp.asarray(SCALE, BF)
    clse[...] = jnp.zeros_like(clse)

    def sub_block(sub, rows, at):
        meta = query_meta(mk, at)

        def run(pairs, ks, wd):
            mask = cross_mask(mk, meta, at, ks, wd)
            attend(pairs, cq, rows, mkv.at[0], mask, ks, wd, catt, clse)

        by_width(tab[7, 2 * b + sub], tab[6, 2 * b + sub], widths, run)

    each_sub(row0, sub_block)


def cross_backward(
    widths, tab, es, mk, n0, s0, att, gsecond, gatt, cq, clse, mkv, wckv, wso, wcq, gains,
    gfirst, gself, gline, att_grad, norm_grad,
    acc, dq_scr, dwckvt, dwcq, dwso, gb,
):
    b = pl.program_id(0)
    row0 = pl.multiple_of(tab[1, b], SUB)

    @pl.when(b == 0)
    def _():
        for ref in (dwckvt, dwcq, dwso, gb):
            ref[...] = jnp.zeros_like(ref)

    @pl.when(tab[2, b] == 1)
    def _():
        acc[...] = jnp.zeros_like(acc)

    def sub_block(sub, rows, at):
        meta = query_meta(mk, at)

        def run(pairs, ks, wd):
            mask = cross_mask(mk, meta, at, ks, wd)
            attend_back(pairs, cq, gatt, clse, rows, mkv.at[0], mask, ks, wd, acc, dq_scr)

        by_width(tab[7, 2 * b + sub], tab[6, 2 * b + sub], widths, run)

    each_sub(row0, sub_block)
    dq = dq_scr[...]
    first = n0[...] * gains[0:1, :] + gains[3:4, :]
    dwcq[...] += mm(first.astype(BF).T, dq)
    gf = gsecond[...] + mm_nt(dq, wcq[...])
    gb[0] += fold8(gf * n0[...])
    gb[1] += fold8(gf)
    gf = norm_back(gf, n0[...], s0[:, 0:1], gains[0:1, :])
    gfirst[...] = gf
    sg = gf.astype(BF)
    dwso[...] += mm(att[...].T, sg)
    gself[...] = mm_nt(sg, wso[...]).astype(BF)

    @pl.when(tab[3, b] == 1)
    def _():
        line_end(acc, es, wckv, 0, None, gline, dwckvt)

    @pl.when(b == pl.num_programs(0) - 1)
    def _():
        att_grad[: 2 * D, :] = dwckvt[...].astype(BF)
        att_grad[2 * D : 3 * D, :] = dwso[...].astype(BF)
        att_grad[3 * D :, :] = dwcq[...].astype(BF)
        sums = jnp.sum(gb[...], axis=1)
        none = jnp.zeros((2, D), F32)
        norm_grad[...] = jnp.concatenate([sums[0:1], none, sums[1:2], none, none])


def line_end(acc, inputs, weight, base, rows, gline, dwt):
    columns = 256

    @pl.loop(0, acc.shape[1] // columns)
    def _(i):
        cols = pl.ds(pl.multiple_of(i * columns, columns), columns)
        low = acc[:, cols].astype(BF)
        back = mm(weight[:, base:], low).T
        if rows is not None:
            back = back + rows[cols, :]
        gline[0, cols, :] = back.astype(BF)
        dwt[...] += mm(low, inputs[0, cols, :])


def self_backward(widths, tab, q, g, gf, lse, kv, mk, xs, wqkv, gline, qkv_grad, dq, acc, rows, dwq, dwkvt):
    b = pl.program_id(0)
    row0 = pl.multiple_of(tab[1, b], SUB)

    @pl.when(b == 0)
    def _():
        dwq[...] = jnp.zeros_like(dwq)
        dwkvt[...] = jnp.zeros_like(dwkvt)

    @pl.when(tab[2, b] == 1)
    def _():
        acc[...] = jnp.zeros_like(acc)
        rows[...] = jnp.zeros_like(rows)

    def sub_block(sub, here, at):
        meta = query_meta(mk, at)

        def run(pairs, ks, wd):
            mask = self_mask(mk, meta, at, ks, wd)
            attend_back(pairs, q, g, lse, here, kv.at[0], mask, ks, wd, acc, dq)

        by_width(tab[5, 2 * b + sub], tab[4, 2 * b + sub], widths, run)

    each_sub(row0, sub_block)

    x = xs[0, pl.ds(row0, BLOCK), :]
    dwq[...] += mm(x.T, dq[...])
    rows[pl.ds(row0, BLOCK), :] = gf[...] + mm_nt(dq[...], wqkv[:, :D])

    @pl.when(tab[3, b] == 1)
    def _():
        line_end(acc, xs, wqkv, D, rows, gline, dwkvt)

    @pl.when(b == pl.num_programs(0) - 1)
    def _():
        qkv_grad[:D, :] = dwq[...].astype(BF)
        qkv_grad[D:, :] = dwkvt[...].astype(BF)


def const_spec(shape):
    return pl.BlockSpec(shape, lambda b, t: (0,) * len(shape), pipeline_mode=pl.Buffered(1))


def row_spec(cols):
    return pl.BlockSpec((BLOCK, cols), lambda b, t: (b, 0))


def line_spec(shape):
    return pl.BlockSpec((1,) + shape, lambda b, t: (t[0, b],) + (0,) * len(shape))


def sds(shape, dtype):
    return jax.ShapeDtypeStruct(shape, dtype)


def kernels(
    lines, n, tab, xs, es, cot, mk, self_qkv, self_out, cross_q, cross_kv, cross_out, weights, norm_gain, norm_bias
):
    slots, line_len = xs.shape[0], xs.shape[1]
    whole, p, k = plan(lines, n)
    rows_all = whole * line_len + k * line_len // p
    blocks = rows_all // BLOCK
    widths = widths_for(line_len)
    params = pltpu.CompilerParams(vmem_limit_bytes=VMEM, dimension_semantics=("arbitrary",))

    def call(kernel, name, ins, in_specs, outs, out_specs, scratch, flops):
        return pl.pallas_call(
            kernel,
            name=name,
            grid_spec=pltpu.PrefetchScalarGridSpec(
                num_scalar_prefetch=1,
                grid=(blocks,),
                in_specs=in_specs,
                out_specs=out_specs,
                scratch_shapes=scratch,
            ),
            out_shape=outs,
            compiler_params=params,
            cost_estimate=pl.CostEstimate(
                flops=int(flops), bytes_accessed=16 << 20, transcendentals=1 << 20
            ),
        )(tab, *ins)

    line2 = (line_len, 2 * D)
    kv, q, att, n0, s0, lse = call(
        functools.partial(self_forward, widths),
        "self_forward",
        (xs, mk, self_qkv, self_out),
        [line_spec((line_len, D)), line_spec((8, line_len)), const_spec((D, 3 * D)), const_spec((D, D))],
        (
            sds((slots,) + line2, BF),
            sds((rows_all, D), BF),
            sds((rows_all, D), BF),
            sds((rows_all, D), F32),
            sds((rows_all, 128), F32),
            sds((rows_all, 128), F32),
        ),
        (line_spec(line2), row_spec(D), row_spec(D), row_spec(D), row_spec(128), row_spec(128)),
        [],
        2e10,
    )

    mkv, cq, catt, clse = call(
        functools.partial(cross_forward, widths),
        "cross_forward",
        (es, mk, n0, cross_kv, cross_q, norm_gain, norm_bias),
        [
            line_spec((line_len, D)), line_spec((8, line_len)), row_spec(D), const_spec((D, 2 * D)),
            const_spec((D, D)), const_spec((3, D)), const_spec((3, D)),
        ],
        (
            sds((slots,) + line2, BF),
            sds((rows_all, D), BF),
            sds((rows_all, D), BF),
            sds((rows_all, 128), F32),
        ),
        (line_spec(line2), row_spec(D), row_spec(D), row_spec(128)),
        [],
        2e10,
    )

    out, gsecond, gatt, ffn_grad, co_grad, norm_a = feed(
        cot, n0, catt, cross_out, weights, norm_gain, norm_bias, lines, n, line_len
    )

    gfirst, gself, enc_line, att_grad, norm_b = call(
        functools.partial(cross_backward, widths),
        "cross_backward",
        (
            es, mk, n0, s0, att, gsecond, gatt, cq, clse, mkv, cross_kv, self_out, cross_q,
            jnp.concatenate([norm_gain, norm_bias]),
        ),
        [
            line_spec((line_len, D)), line_spec((8, line_len)), row_spec(D), row_spec(128), row_spec(D),
            row_spec(D), row_spec(D), row_spec(D), row_spec(128), line_spec(line2), const_spec((D, 2 * D)),
            const_spec((D, D)), const_spec((D, D)), const_spec((6, D)),
        ],
        (
            sds((rows_all, D), F32),
            sds((rows_all, D), BF),
            sds((slots, line_len, D), BF),
            sds((4 * D, D), BF),
            sds((8, D), F32),
        ),
        (
            row_spec(D), row_spec(D), line_spec((line_len, D)), const_spec((4 * D, D)), const_spec((8, D)),
        ),
        [
            pltpu.VMEM((2 * D, line_len), F32),
            pltpu.VMEM((BLOCK, D), BF),
            pltpu.VMEM((2 * D, D), F32),
            pltpu.VMEM((D, D), F32),
            pltpu.VMEM((D, D), F32),
            pltpu.VMEM((2, 8, D), F32),
        ],
        3e10,
    )

    stream_line, qkv_grad = call(
        functools.partial(self_backward, widths),
        "self_backward",
        (q, gself, gfirst, lse, kv, mk, xs, self_qkv),
        [
            row_spec(D), row_spec(D), row_spec(D), row_spec(128), line_spec(line2), line_spec((8, line_len)),
            line_spec((line_len, D)), const_spec((D, 3 * D)),
        ],
        (sds((slots, line_len, D), BF), sds((3 * D, D), BF)),
        (line_spec((line_len, D)), const_spec((3 * D, D))),
        [
            pltpu.VMEM((BLOCK, D), BF),
            pltpu.VMEM((2 * D, line_len), F32),
            pltpu.VMEM((line_len, D), F32),
            pltpu.VMEM((D, D), F32),
            pltpu.VMEM((2 * D, D), F32),
        ],
        3e10,
    )
    return out, enc_line, stream_line, ffn_grad, att_grad, co_grad, qkv_grad, norm_a, norm_b


def remote(src, dst, send, recv, device):
    return pltpu.make_async_remote_copy(
        src_ref=src, dst_ref=dst, send_sem=send, recv_sem=recv, device_id={"seq": device},
        device_id_type=pl.DeviceIdType.MESH,
    )


def part_of(device, p):
    return (device % p + device // p) % p


class Exchange:
    def __init__(self, lines, n, line_len):
        self.n, self.piece = n, line_len // n
        self.whole, self.p, self.k = plan(lines, n)
        self.groups = n // self.p
        self.chunks = n // self.p
        self.part_len = line_len // self.p
        self.line_len = line_len
        self.shared0 = self.whole * n
        self.rows_p = self.k * self.part_len
        self.me = lax.axis_index("seq")
        self.group = self.me // self.p
        self.part = part_of(self.me, self.p)
        self.pos_part, self.pos_chunk = self.me // self.chunks, self.me % self.chunks

    def owner(self, group):
        return group * self.p + (self.pos_part + self.p * self.groups - group) % self.p


class Dim:
    def __init__(self, axis, stride, size):
        self.axis, self.stride, self.size = axis, stride, size
        at = lax.axis_index(axis)
        self.index = at // stride % size
        self.rest = at - self.index * stride

    def peer(self, v):
        return (self.index + v) % self.size

    def device(self, v):
        return {self.axis: self.rest + self.peer(v) * self.stride}


def send_to(src, dst, sems, device):
    return pltpu.make_async_remote_copy(
        src_ref=src, dst_ref=dst, send_sem=sems[0], recv_sem=sems[1], device_id=device,
        device_id_type=pl.DeviceIdType.MESH,
    )


class Sems:
    def __init__(self, ref):
        self.ref, self.used = ref, 0

    def next(self):
        self.used += 1
        return self.ref.at[0, self.used - 1], self.ref.at[1, self.used - 1]


def mesh_dims(ex):
    return (
        Dim("dp", 1, 2), Dim("dp", 2, lax.axis_size("dp") // 2), Dim("seq", 1, ex.p), Dim("seq", ex.p, ex.groups),
    )


def greet(ex, core, yy):
    barrier = pltpu.get_barrier_semaphore()
    greeted = [{"seq": (ex.me + o) % ex.n} for o in range(1, ex.n)]
    greeted += [dim.device(v) for dim in (core, yy) for v in range(1, dim.size)]
    for device in greeted:
        pl.semaphore_signal(barrier, inc=1, device_id=device, device_id_type=pl.DeviceIdType.MESH)
    pl.semaphore_wait(barrier, len(greeted))


def start_all(copies):
    for copy in copies:
        copy.start()


def gather(dim, view, sems):
    copies = [send_to(view, view, sems.next(), dim.device(v)) for v in range(1, dim.size)]

    def finish():
        for copy in copies:
            copy.wait()

    return copies, finish


def in_kernel(
    ex, x_ref, rc_ref, e_ref, w_ref, xs, rc, es, weights, sem_w, sem_p, sem_f, sem_l, sem_g
):
    n, piece, w, k, me = ex.n, ex.piece, ex.whole, ex.k, ex.me
    core, yy, xx, zz = mesh_dims(ex)
    c, y, x, z = core.index, yy.index, xx.index, zz.index
    quarter = w_ref.shape[0] // (2 * yy.size)
    weights = weights.reshape(ex.groups, ex.p, yy.size, 2, quarter, w_ref.shape[1])
    own = pltpu.make_async_copy(
        w_ref.at[pl.ds(pl.multiple_of((y * 2 + c) * quarter, quarter), quarter)],
        weights.at[z, x, y, c], sem_l.at[3, 0],
    )
    own.start()
    greet(ex, core, yy)
    own.wait()
    sems = Sems(sem_g)
    stages = [
        gather(zz, weights.at[z, x, y, c], sems),
        gather(xx, weights.at[:, x, y, c], sems),
        gather(yy, weights.at[:, :, y, c], sems),
        gather(core, weights.at[:, :, :, c], sems),
    ]
    start_all(stages[0][0])

    def next_stage(i):
        stages[i][1]()
        if i + 1 < len(stages):
            start_all(stages[i + 1][0])

    spans = pl.ds(pl.multiple_of(me * piece, piece), piece)
    names = (x_ref, rc_ref, e_ref)

    def line_dst(out, slots):
        if out is rc:
            return rc.at[slots, me]
        return out.at[slots, spans]

    def whole_copies(a, o):
        to = (me + o) % n
        src = names[a]
        pairs = [(src.at[pl.ds(to * w, w)], line_dst((xs, rc, es)[a], pl.ds(k, w)))] if w else []
        return [
            remote(s, d, sem_w.at[0, a, i, o], sem_w.at[1, a, i, o], to)
            if o
            else pltpu.make_async_copy(s, d, sem_l.at[a, i])
            for i, (s, d) in enumerate(pairs)
        ]

    def shared_pairs(a, group):
        src = names[a]
        first = ex.shared0 + group * k
        return [(src.at[pl.ds(first, k)], line_dst((xs, rc, es)[a], pl.ds(0, k)))] if k else []

    def shared_send(a, u):
        group = (ex.group + u) % ex.groups
        to = ex.owner(group)
        return [
            remote(s, d, sem_p.at[0, a, i, u], sem_p.at[1, a, i, ex.pos_chunk], to)
            for i, (s, d) in enumerate(shared_pairs(a, group))
        ]

    def shared_local(a):
        return [
            pltpu.make_async_copy(s, d, sem_l.at[a, max(w, 1) + i])
            for i, (s, d) in enumerate(shared_pairs(a, ex.group))
        ]

    def shared_arrival(a, j):
        return [
            remote(s, d, sem_p.at[0, a, i, 0], sem_p.at[1, a, i, j], me)
            for i, (s, d) in enumerate(shared_pairs(a, ex.group))
        ]

    def forwards(a):
        out = (xs, rc, es)[a]
        mine = ex.part * ex.part_len
        if a == 1:
            view = rc.at[pl.ds(0, k), pl.ds(ex.part * ex.chunks, ex.chunks)]
        else:
            view = out.at[pl.ds(0, k), pl.ds(pl.multiple_of(mine, ex.part_len), ex.part_len)]
        return [
            remote(view, view, sem_f.at[0, a, v], sem_f.at[1, a, v], ex.group * ex.p + (me % ex.p + v) % ex.p)
            for v in range(1, ex.p)
        ]

    here = ex.pos_part == ex.part
    for a in range(3):
        for u in range(ex.groups if k else 0):
            if u == 0:

                @pl.when(here)
                def _():
                    for copy in shared_local(a):
                        copy.start()

                @pl.when(jnp.logical_not(here))
                def _():
                    for copy in shared_send(a, 0):
                        copy.start()

            else:
                for copy in shared_send(a, u):
                    copy.start()
        for o in range(n):
            for copy in whole_copies(a, o):
                copy.start()
    next_stage(0)
    for a in range(3):
        next_stage(a + 1)
        for j in range(ex.chunks if k else 0):
            own = ex.part * ex.chunks + j == me

            @pl.when(own)
            def _():
                for copy in shared_local(a):
                    copy.wait()

            @pl.when(jnp.logical_not(own))
            def _():
                for copy in shared_arrival(a, j):
                    copy.wait_recv()

        if k:
            for copy in forwards(a):
                copy.start()
    for a in range(3):
        for o in range(n):
            for copy in whole_copies(a, o):
                copy.wait()
        for u in range(ex.groups if k else 0):
            if u == 0:

                @pl.when(jnp.logical_not(here))
                def _():
                    for copy in shared_send(a, 0):
                        copy.wait_send()

            else:
                for copy in shared_send(a, u):
                    copy.wait_send()
        if k:
            for copy in forwards(a):
                copy.wait()


def feed_kernel(
    ex, cot_src, n0, catt, wco, wff, gains, biases,
    out, gsecond_out, gatt, ffn_grad, co_grad, norm_grad,
    cot, out_v, hid, gprime, dw1, dw2t, dwco, gb, sem_cs, sem_cw, sem_os, sem_ow,
):
    b, last = pl.program_id(0), pl.num_programs(0) - 1
    n, piece, w, k, me = ex.n, ex.piece, ex.whole, ex.k, ex.me

    def rows_at(row):
        return pl.ds(pl.multiple_of(row, piece), piece)

    def cot_copy(i, slot, row, sems, at, to):
        src, dst = cot_src.at[slot], cot.at[rows_at(row)]
        local = lambda: pltpu.make_async_copy(src, dst, sems.at[1, i, at])
        return local, lambda sent: send_to(src, dst, (sems.at[0, i, sent], sems.at[1, i, at]), {"seq": to})

    def cot_sends():
        for u in range(ex.groups if k else 0):
            group = (ex.group + u) % ex.groups
            to = ex.owner(group)
            for i in range(k):
                row = i * ex.part_len + ex.pos_chunk * piece
                local, far = cot_copy(i, ex.shared0 + group * k + i, row, sem_cs, ex.pos_chunk, to)
                yield to, local, functools.partial(far, u)
        for v in range(n):
            to = (me + v) % n
            for i in range(w):
                row = ex.rows_p + i * ex.line_len + me * piece
                local, far = cot_copy(i, to * w + i, row, sem_cw, me, to)
                yield to, local, functools.partial(far, v)

    def out_copy(row, slot, i, sems, sent, at, to):
        src, dst = out_v.at[rows_at(row)], out.at[slot]
        return (
            to,
            lambda: pltpu.make_async_copy(src, dst, sems.at[1, i, at]),
            lambda: send_to(src, dst, (sems.at[0, i, sent], sems.at[1, i, at]), {"seq": to}),
        )

    def out_shared(row):
        i, j = row // ex.part_len, row % ex.part_len // piece
        return out_copy(
            row, ex.shared0 + ex.group * k + i, i, sem_os, j, ex.group, ex.part * ex.chunks + j
        )

    def out_whole(row):
        at = row - ex.rows_p
        i, s = at // ex.line_len, at % ex.line_len // piece
        return out_copy(row, me * w + i, i, sem_ow, s, me, s)

    def either(to, here, there):
        @pl.when(to == me)
        def _():
            here()

        @pl.when(to != me)
        def _():
            there()

    @pl.when(b == 0)
    def _():
        for ref in (dw1, dw2t, dwco, gb):
            ref[...] = jnp.zeros_like(ref)
        core, yy = mesh_dims(ex)[:2]
        greet(ex, core, yy)
        for to, local, far in cot_sends():
            either(to, lambda: local().start(), lambda: far().start())

    first = n0[...] * gains[0:1, :] + biases[0:1, :]
    n1, s1 = norm_stats(first + mm(catt[...], wco[...]))
    second = n1 * gains[1:2, :] + biases[1:2, :]
    second_low = second.astype(BF)
    chunks, chunk = wff.shape[0], wff.shape[2]
    total = second
    for c in range(chunks):
        cols = slice(c * chunk, (c + 1) * chunk)
        v = mm(second_low, wff[c, :D, :])
        v2 = v * v
        t = jnp.tanh(GELU_C * (v + 0.044715 * (v2 * v)))
        half = 0.5 * (1.0 + t)
        h = (v * half).astype(BF)
        hid[:, cols] = h
        gprime[:, cols] = half + (0.5 * v) * (1.0 - t * t) * (GELU_C + (3 * 0.044715 * GELU_C) * v2)
        total = total + mm_nt(h, wff[c, D:, :])
    n2, s2 = norm_stats(total)
    here = pl.ds(pl.multiple_of(b * BLOCK, BLOCK), BLOCK)
    out_v[here, :] = (n2 * gains[2:3, :] + biases[2:3, :]).astype(BF)

    for q in range(BLOCK // piece):
        row = b * BLOCK + q * piece

        @pl.when(row < ex.rows_p)
        def _():
            i, j = row // ex.part_len, row % ex.part_len // piece
            local, far = cot_copy(i, 0, row, sem_cs, j, me)
            either(ex.part * ex.chunks + j, lambda: local().wait(), lambda: far(0).wait_recv())
            to, local, far = out_shared(row)
            either(to, lambda: local().start(), lambda: far().start())

        @pl.when(row >= ex.rows_p)
        def _():
            at = row - ex.rows_p
            i, s = at // ex.line_len, at % ex.line_len // piece
            local, far = cot_copy(i, 0, row, sem_cw, s, me)
            either(s, lambda: local().wait(), lambda: far(0).wait_recv())
            to, local, far = out_whole(row)
            either(to, lambda: local().start(), lambda: far().start())

    dy = cot[here, :].astype(F32)
    gb[1] += fold8(dy * n2)
    gb[3] += fold8(dy)
    gthird = norm_back(dy, n2, s2, gains[2:3, :])
    fg = gthird.astype(BF)
    fgt, sect = fg.T, second_low.T
    back = gthird
    for c in range(chunks):
        cols = slice(c * chunk, (c + 1) * chunk)
        pg = (mm(fg, wff[c, D:, :]) * gprime[:, cols]).astype(BF)
        dw2t[:, cols] += mm(fgt, hid[:, cols])
        dw1[:, cols] += mm(sect, pg)
        back = back + mm_nt(pg, wff[c, :D, :])
    gb[0] += fold8(back * n1)
    gb[2] += fold8(back)
    gsecond = norm_back(back, n1, s1, gains[1:2, :])
    gsecond_out[...] = gsecond
    cg = gsecond.astype(BF)
    dwco[...] += mm(catt[...].T, cg)
    gatt[...] = mm_nt(cg, wco[...]).astype(BF)

    @pl.when(b == last)
    def _():
        for c in range(chunks):
            cols = slice(c * chunk, (c + 1) * chunk)
            ffn_grad[c, :D, :] = dw1[:, cols].astype(BF)
            ffn_grad[c, D:, :] = dw2t[:, cols].astype(BF)
        co_grad[...] = dwco[...].astype(BF)
        sums = jnp.sum(gb[...], axis=1)
        none = jnp.zeros((1, D), F32)
        norm_grad[...] = jnp.concatenate([none, sums[:2], none, sums[2:], none, none])
        for to, local, far in cot_sends():
            either(to, lambda: None, lambda: far().wait_send())
        for row in range(0, ex.rows_p, piece):
            to, local, far = out_shared(row)
            either(to, lambda: local().wait(), lambda: far().wait_send())
        for row in range(ex.rows_p, cot.shape[0], piece):
            to, local, far = out_whole(row)
            either(to, lambda: local().wait(), lambda: far().wait_send())
        for i in range(k):
            for group in range(ex.groups):
                arrival = out_copy(0, ex.shared0 + group * k + i, i, sem_os, 0, group, me)[2]
                either(ex.owner(group), lambda: None, lambda: arrival().wait_recv())
        for i in range(w):
            for s in range(n):
                arrival = out_copy(0, s * w + i, i, sem_ow, 0, s, me)[2]
                either(s, lambda: None, lambda: arrival().wait_recv())


def feed(cot_src, n0, catt, wco, weights, gains, biases, lines, n, line_len):
    whole, p, k = plan(lines, n)
    most = max(k, whole, 1)
    rows_all, cols = n0.shape[0], weights.shape[2]
    ff = n * cols

    def kernel(*refs):
        feed_kernel(Exchange(lines, n, line_len), *refs)

    row = lambda c: pl.BlockSpec((BLOCK, c), lambda b: (b, 0))
    const = lambda *shape: pl.BlockSpec(shape, lambda b: (0,) * len(shape), pipeline_mode=pl.Buffered(1))
    hbm = pl.BlockSpec(memory_space=pl.ANY)
    dma = pltpu.SemaphoreType.DMA
    return pl.pallas_call(
        kernel,
        name="feed",
        grid=(rows_all // BLOCK,),
        in_specs=[hbm, row(D), row(D), const(D, D), const(n, 2 * D, cols), const(3, D), const(3, D)],
        out_specs=[hbm, row(D), row(D), const(n, 2 * D, cols), const(D, D), const(8, D)],
        out_shape=(
            sds((lines, line_len // n, D), BF),
            sds((rows_all, D), F32),
            sds((rows_all, D), BF),
            sds((n, 2 * D, cols), BF),
            sds((D, D), BF),
            sds((8, D), F32),
        ),
        scratch_shapes=[
            pltpu.VMEM((rows_all, D), BF),
            pltpu.VMEM((rows_all, D), BF),
            pltpu.VMEM((BLOCK, ff), BF),
            pltpu.VMEM((BLOCK, ff), F32),
            pltpu.VMEM((D, ff), F32),
            pltpu.VMEM((D, ff), F32),
            pltpu.VMEM((D, D), F32),
            pltpu.VMEM((4, 8, D), F32),
            dma((2, most, n)),
            dma((2, most, n)),
            dma((2, most, n)),
            dma((2, most, n)),
        ],
        compiler_params=pltpu.CompilerParams(
            collective_id=3, has_side_effects=True, vmem_limit_bytes=VMEM,
            dimension_semantics=("arbitrary",),
        ),
        cost_estimate=pl.CostEstimate(flops=int(4e10), bytes_accessed=16 << 20, transcendentals=1 << 20),
    )(cot_src, n0, catt, wco, weights, gains, biases)


def exchange_in(stream, rc, encoder, weights, lines, n, line_len, dp):
    whole, p, k = plan(lines, n)
    hops = 1 + dp // 2 - 1 + p - 1 + n // p - 1
    slots, piece = k + whole, line_len // n
    most = max(k, whole, 1)

    def kernel(*refs):
        in_kernel(Exchange(lines, n, line_len), *refs)

    dma = pltpu.SemaphoreType.DMA
    return pl.pallas_call(
        kernel,
        name="exchange_in",
        in_specs=[pl.BlockSpec(memory_space=pl.ANY)] * 4,
        out_specs=[pl.BlockSpec(memory_space=pl.ANY)] * 4,
        out_shape=(
            sds((slots, line_len, D), BF),
            sds((slots, n, 1, piece), jnp.int32),
            sds((slots, line_len, D), BF),
            sds((n,) + weights.shape, BF),
        ),
        scratch_shapes=[
            dma((2, 3, most, n)), dma((2, 3, most, n)), dma((2, 3, max(p, 2))), dma((4, 2 * most)),
            dma((2, hops)),
        ],
        compiler_params=pltpu.CompilerParams(collective_id=1, has_side_effects=True),
    )(stream, rc, encoder, weights)


def flat_loop(lead, run):
    @pl.loop(0, math.prod(lead))
    def _(i):
        index = []
        for size in reversed(lead):
            index.append(i % size)
            i = i // size
        run(tuple(reversed(index)))


def add_into(dst, sources, lead):
    def run(index):
        total = dst[index].astype(F32)
        for source in sources:
            total = total + source[index].astype(F32)
        dst[index] = total.astype(dst.dtype)

    flat_loop(lead, run)


def finish_kernel(
    ex, enc_line, stream_line, ffn_grad, att_grad, co_grad, qkv_grad, norm_a, norm_b,
    enc, stream, ffn, att, norms,
    ffn_v, att_v, norm_v, ffn_bufs, att_bufs, norm_bufs, own_v, part_v,
    sem_red, sem_w, sem_p, sem_l, sem_s, sem_in,
):
    n, piece, w, k, p, me = ex.n, ex.piece, ex.whole, ex.k, ex.p, ex.me
    core, yy, xx, zz = mesh_dims(ex)
    outer = yy.size

    loads = [
        pltpu.make_async_copy(ffn_grad, ffn_v, sem_in.at[0]),
        pltpu.make_async_copy(att_grad, att_v.at[pl.ds(0, 4 * D)], sem_in.at[1]),
        pltpu.make_async_copy(co_grad, att_v.at[pl.ds(4 * D, D)], sem_in.at[2]),
        pltpu.make_async_copy(qkv_grad, att_v.at[pl.ds(5 * D, 3 * D)], sem_in.at[3]),
    ]
    lines = (enc_line, stream_line)
    mine = pl.ds(pl.multiple_of(ex.part * ex.part_len, ex.part_len), ex.part_len)
    if k:
        loads += [
            pltpu.make_async_copy(lines[a].at[pl.ds(0, k), mine], own_v.at[a], sem_in.at[4 + a])
            for a in range(2)
        ]
    start_all(loads)
    norm_v[...] = norm_a[...] + norm_b[...]
    greet(ex, core, yy)

    fl = ffn_v.shape
    rows = fl[1] // (2 * outer)
    ffn_6 = ffn_v.reshape(ex.groups, p, outer, 2, rows, fl[2])
    att_rows = att_v.shape[0] // (2 * outer * n)
    att_6 = att_v.reshape(2, outer, p, ex.groups, att_rows, D)
    ffn_o = ffn.reshape(outer, 2, rows, fl[2])
    att_o = att.reshape(2, outer, p, ex.groups, att_rows, D)
    c, y, x, z = core.index, yy.index, xx.index, zz.index
    sems = Sems(sem_red)

    def scatter(dim, view, buf, lead):
        copies = [
            send_to(view(dim.peer(v)), buf.at[v - 1], sems.next(), dim.device(v)) for v in range(1, dim.size)
        ]

        def finish():
            for copy in copies:
                copy.wait()
            add_into(view(dim.index), [buf.at[v - 1] for v in range(1, dim.size)], lead)

        return copies, finish

    def place(src, dst, sem):
        copy = pltpu.make_async_copy(src, dst, sem)
        return [copy], copy.wait

    def exchange_all(dim, buf):
        copies = [send_to(norm_v, buf.at[v - 1], sems.next(), dim.device(v)) for v in range(1, dim.size)]

        def finish():
            for copy in copies:
                copy.wait()
            norm_v[...] = sum([buf[v - 1] for v in range(1, dim.size)], norm_v[...])

        return copies, finish

    g, o = ex.groups, outer

    def att_stream(h, half):
        r = pl.ds(h * half, half)
        bufs = [buf.at[..., r, :] for buf in att_bufs]
        return [
            scatter(core, lambda t: att_6.at[t, :, :, :, r], bufs[0], (o, p, g)),
            scatter(yy, lambda t: att_6.at[c, t, :, :, r], bufs[1], (p, g)),
            scatter(xx, lambda t: att_6.at[c, y, t, :, r], bufs[2], (g,)),
            scatter(zz, lambda t: att_6.at[c, y, x, t, r], bufs[3], ()),
            place(att_6.at[c, y, x, z, r], att_o.at[c, y, x, z, r], sem_in.at[7 + h]),
            gather(zz, att_o.at[c, y, x, z, r], sems),
            gather(xx, att_o.at[c, y, x, :, r], sems),
            gather(yy, att_o.at[c, y, :, :, r], sems),
            gather(core, att_o.at[c, :, :, :, r], sems),
        ]

    halves = 2 if att_rows % 32 == 0 else 1
    streams = [att_stream(h, att_rows // halves) for h in range(halves)]
    streams += [
        [
            scatter(core, lambda t: ffn_6.at[:, :, :, t], ffn_bufs[0], (g, p, o)),
            scatter(xx, lambda t: ffn_6.at[:, t, :, c], ffn_bufs[1], (g, o)),
            scatter(yy, lambda t: ffn_6.at[:, x, t, c], ffn_bufs[2], (g,)),
            scatter(zz, lambda t: ffn_6.at[t, x, y, c], ffn_bufs[3], ()),
            place(ffn_6.at[z, x, y, c], ffn_o.at[y, c], sem_in.at[6]),
            gather(yy, ffn_o.at[y, c], sems),
            gather(core, ffn_o.at[:, c], sems),
        ],
        [exchange_all(dim, norm_bufs[i]) for i, dim in enumerate((core, yy, xx, zz))],
    ]

    def whole_src(a, i, to):
        return lines[a].at[k + i, pl.ds(pl.multiple_of(to * piece, piece), piece)]

    outs = (enc, stream)

    def whole_copies(a, v):
        to = (me + v) % n
        result = []
        for i in range(w):
            src, dst = whole_src(a, i, to), outs[a].at[me * w + i]
            result.append(
                send_to(src, dst, (sem_w.at[0, a, i, v], sem_w.at[1, a, i, v]), {"seq": to})
                if v
                else pltpu.make_async_copy(src, dst, sem_l.at[a, i])
            )
        return result

    def shared_pair(a, i, j):
        at = pl.ds(pl.multiple_of(j * piece, piece), piece)
        src = own_v.at[a, i, at]
        return src, outs[a].at[ex.shared0 + ex.group * k + i]

    def shared_copies(a, u):
        j = (ex.group + u) % ex.chunks
        to = ex.part * ex.chunks + j
        return to, [
            send_to(*shared_pair(a, i, j), (sem_p.at[0, a, i, u], sem_p.at[1, a, i, ex.group]), {"seq": to})
            for i in range(k)
        ]

    def local_copies(a):
        return [
            pltpu.make_async_copy(*shared_pair(a, i, ex.pos_chunk), sem_l.at[a, max(w, 1) + i])
            for i in range(k)
        ]

    def each_shared(a, remote_run, local_run):
        for u in range(ex.chunks if k else 0):
            to, copies = shared_copies(a, u)

            @pl.when(to != me)
            def _():
                for copy in copies:
                    remote_run(copy)

            @pl.when(to == me)
            def _():
                for copy in local_copies(a):
                    local_run(copy)

    def sharing(a, v):
        part = (ex.part + v) % p
        theirs = pl.ds(pl.multiple_of(part * ex.part_len, ex.part_len), ex.part_len)
        return send_to(
            lines[a].at[pl.ds(0, k), theirs], part_v.at[a, v - 1], (sem_s.at[0, a, v], sem_s.at[1, a, v]),
            xx.device(v),
        )

    for copy in loads:
        copy.wait()
    for stages in streams:
        start_all(stages[0][0])
    shares = [sharing(a, v) for a in range(2) for v in range(1, p)] if k else []
    start_all(shares)

    def start_rows(a):
        each_shared(a, lambda copy: copy.start(), lambda copy: copy.start())
        for v in range(n):
            start_all(whole_copies(a, v))

    for stage in range(max(len(stages) for stages in streams)):
        for stages in streams:
            if stage < len(stages):
                stages[stage][1]()
            if stage + 1 < len(stages):
                start_all(stages[stage + 1][0])
        if stage == 0:
            for copy in shares:
                copy.wait()
            for a in range(2 if k else 0):
                add_into(own_v.at[a], [part_v.at[a, v - 1] for v in range(1, p)], (k,))
            start_rows(0)
        if stage == 1:
            start_rows(1)
    norms[...] = norm_v[...]
    for a in range(2):
        for v in range(n):
            for copy in whole_copies(a, v):
                copy.wait()
        each_shared(a, lambda copy: copy.wait_send(), lambda copy: copy.wait())
        for group in range(ex.groups if k else 0):

            @pl.when(ex.owner(group) != me)
            def _():
                for i in range(k):
                    sems = (sem_p.at[0, a, i, 0], sem_p.at[1, a, i, group])
                    send_to(*shared_pair(a, i, 0), sems, {"seq": me}).wait_recv()


def finish(arrays, lines, n, line_len, dp):
    whole, p, k = plan(lines, n)
    piece, most, groups, outer = line_len // n, max(k, whole, 1), n // p, dp // 2
    cols = arrays[2].shape[2]
    rows, att_rows = 2 * D // dp, 8 * D // (dp * n)
    part_len = line_len // p
    slots = max(k, 1)

    def kernel(*refs):
        refs = list(refs)
        grouped = refs[:16] + [refs[16:20], refs[20:24], refs[24:28]] + refs[28:]
        finish_kernel(Exchange(lines, n, line_len), *grouped)

    dma = pltpu.SemaphoreType.DMA
    hops = (1, outer - 1, p - 1, groups - 1)
    hbm = pl.BlockSpec(memory_space=pl.ANY)
    vmem = pl.BlockSpec(memory_space=pltpu.VMEM)
    at_least = lambda q: max(q, 1)
    return pl.pallas_call(
        kernel,
        name="finish",
        in_specs=[hbm] * 6 + [vmem] * 2,
        out_specs=[hbm] * 2 + [vmem] * 3,
        out_shape=[sds((lines, piece, D), BF)] * 2
        + [sds((2 * D, cols), BF), sds((8 * D, D), BF), sds((8, D), F32)],
        scratch_shapes=[
            pltpu.VMEM((n, 2 * D, cols), BF),
            pltpu.VMEM((8 * D, D), BF),
            pltpu.VMEM((8, D), F32),
            pltpu.VMEM((1, groups, p, outer, rows, cols), BF),
            pltpu.VMEM((at_least(p - 1), groups, outer, rows, cols), BF),
            pltpu.VMEM((at_least(outer - 1), groups, rows, cols), BF),
            pltpu.VMEM((at_least(groups - 1), rows, cols), BF),
            pltpu.VMEM((1, outer, p, groups, att_rows, D), BF),
            pltpu.VMEM((at_least(outer - 1), p, groups, att_rows, D), BF),
            pltpu.VMEM((at_least(p - 1), groups, att_rows, D), BF),
            pltpu.VMEM((at_least(groups - 1), att_rows, D), BF),
            *[pltpu.VMEM((at_least(q), 8, D), F32) for q in hops],
            pltpu.VMEM((2, slots, part_len, D), BF),
            pltpu.VMEM((2, at_least(p - 1), slots, part_len, D), BF),
            dma((2, 7 * sum(hops))),
            dma((2, 2, most, n)),
            dma((2, 2, most, n)),
            dma((2, 2 * most)),
            dma((2, 2, max(p, 2))),
            dma((9,)),
        ],
        compiler_params=pltpu.CompilerParams(
            collective_id=2, has_side_effects=True, vmem_limit_bytes=VMEM
        ),
    )(*arrays)


def doc_numbers(bounds, places):
    return jnp.sum((bounds[:, None, :] <= places[None, :, None]).astype(jnp.int32), axis=2)


def body(
    stream, encoder, cotangent, self_qkv, self_out, cross_q, cross_kv, cross_out, ffn_in, ffn_out,
    norm_gain, norm_bias, lengths, enc_lengths, ranks, cuts,
):
    n = lax.axis_size("seq")
    me = lax.axis_index("seq")
    lines, piece = stream.shape[0], stream.shape[1]
    line_len = piece * n
    whole, p, k = plan(lines, n)
    groups = n // p
    slots = k + whole
    part_len = line_len // p
    rows_p, rows_w = k * part_len, whole * line_len
    rows_all = rows_p + rows_w
    ff = ffn_in.shape[1] * n
    group, part = me // p, part_of(me, p)
    widths = widths_for(line_len)
    i32 = jnp.int32

    cost = jnp.sum(lengths * lengths, axis=1)
    order = jnp.arange(lines, dtype=i32)
    lighter = (cost[None, :] < cost[:, None]) | (
        (cost[None, :] == cost[:, None]) & (order[None, :] < order[:, None])
    )
    rank = jnp.sum(lighter.astype(i32), axis=1)
    slot_of = jnp.where(rank < whole * n, rank, whole * n + lines - 1 - rank)
    line_of = jnp.sum(jnp.where(slot_of[None, :] == order[:, None], order[None, :], 0), axis=1)

    rc_in = (ranks * 32 + cuts)[line_of][:, None, :]
    shard = jnp.concatenate([ffn_in, ffn_out.T])
    cot = cotangent[line_of]
    xs, rc, es, weights = exchange_in(
        stream[line_of], rc_in, encoder[line_of], shard, lines, n, line_len, lax.axis_size("dp")
    )
    rc = rc.reshape(slots, line_len)
    own_slots = jnp.concatenate([whole * n + group * k + jnp.arange(k), me * whole + jnp.arange(whole)])
    mine = line_of[own_slots.astype(i32)]
    cum_t = jnp.cumsum(lengths[mine], axis=1)
    cum_e = jnp.cumsum(enc_lengths[mine], axis=1)
    places = jnp.arange(line_len, dtype=i32)
    doc = doc_numbers(cum_t, places)
    src = doc_numbers(cum_e, places)
    zero = jnp.zeros_like(rc)
    mk = jnp.stack([doc, rc // 32, rc % 32, src, zero, zero, zero, zero], axis=1).astype(F32)

    block_line = [j for j in range(k) for _ in range(part_len // BLOCK)]
    block_line += [k + j for j in range(whole) for _ in range(line_len // BLOCK)]
    block_row = [r * BLOCK for j in range(k) for r in range(part_len // BLOCK)]
    block_row += [r * BLOCK for j in range(whole) for r in range(line_len // BLOCK)]
    blocks = len(block_line)
    begin = [int(i == 0 or block_line[i] != block_line[i - 1]) for i in range(blocks)]
    end = [int(i == blocks - 1 or block_line[i] != block_line[i + 1]) for i in range(blocks)]
    per = BLOCK // SUB
    bl = jnp.asarray(block_line, i32)
    br = jnp.asarray(block_row, i32) + jnp.where(bl < k, part * part_len, 0)
    sub_line = jnp.repeat(bl, per)
    sub_row = jnp.repeat(br, per) + jnp.tile(jnp.arange(per, dtype=i32) * SUB, blocks)
    ct, ce = cum_t[sub_line], cum_e[sub_line]
    before = ct <= sub_row[:, None]
    after = ct > sub_row[:, None] + (SUB - 1)

    def key_range(bounds):
        start = jnp.max(jnp.where(before, bounds, 0), axis=1)
        stop = jnp.min(jnp.where(after, bounds, line_len), axis=1)
        ks = start // SUB * SUB
        table = jnp.asarray([wd for wd, _ in widths], i32)
        var = jnp.sum((stop - ks)[:, None] > table[None, :], axis=1).astype(i32)
        wd = jnp.sum(jnp.where(var[:, None] == jnp.arange(len(widths)), table[None, :], 0), axis=1)
        return jnp.minimum(ks, line_len - wd), var

    sks, svar = key_range(ct)
    cks, cvar = key_range(ce)
    pad = jnp.zeros((blocks * (per - 1),), i32)
    wide = lambda v: jnp.concatenate([jnp.asarray(v, i32), pad])
    tab = jnp.stack([wide(bl), wide(br), wide(begin), wide(end), sks, svar, cks, cvar])

    output, *arrays = kernels(
        lines, n, tab, xs, es, cot, mk, self_qkv, self_out, cross_q, cross_kv, cross_out, weights, norm_gain, norm_bias
    )
    encoder_grad, stream_grad, ffn, att, norms = finish(
        arrays, lines, n, line_len, lax.axis_size("dp")
    )
    ffn, att = ffn.astype(F32), att.astype(F32)
    square = lambda i: att[i * D : (i + 1) * D]
    return (
        output[slot_of],
        stream_grad[slot_of].astype(F32),
        encoder_grad[slot_of].astype(F32),
        jnp.concatenate([square(5), square(6).T, square(7).T], axis=1),
        square(2),
        square(3),
        jnp.concatenate([square(0).T, square(1).T], axis=1),
        square(4),
        ffn[:D],
        ffn[D:].T,
        norms[:3],
        norms[3:6],
    )


def solution(mesh):
    lines = P("dp", "seq", None)
    in_specs = (
        lines, lines, lines, P(), P(), P(), P(), P(), P(None, "seq"), P("seq", None), P(), P(),
        P("dp", None), P("dp", None), P("dp", "seq"), P("dp", "seq"),
    )
    out_specs = (
        lines, lines, lines, P(), P(), P(), P(), P(), P(None, "seq"), P("seq", None), P(), P(),
    )
    return jax.shard_map(body, mesh=mesh, in_specs=in_specs, out_specs=out_specs, check_vma=False)
```

```python
import functools
import math

import jax
import jax.numpy as jnp
from jax import lax
from jax.experimental import pallas as pl
from jax.experimental.pallas import tpu as pltpu
from jax.sharding import PartitionSpec as P

D = 512
HEADS = 8
HEAD = 64
PAIR = 2 * HEAD
PAIRS = HEADS // 2
NEGATIVE_FILL = -1e30
EPSILON = 1e-05
SCALE = HEAD ** (-0.5)
BLOCK = 256
SUB = 128
BF = jnp.bfloat16
F32 = jnp.float32
NT = (((1,), (1,)), ((), ()))
GELU_C = math.sqrt(2.0 / math.pi)
VMEM = 60 * 1024 * 1024


def mm(left, right):
    return jnp.dot(left, right, preferred_element_type=F32)


def mm_nt(left, right):
    return lax.dot_general(left, right, NT, preferred_element_type=F32)


def plan(lines, n):
    whole = lines // n
    rest = lines - whole * n
    groups = math.gcd(rest, n) if rest else n
    return whole, n // groups, rest // groups


def widths_for(line_len):
    some = ((256, 4), (384, 4), (512, 4), (640, 2))
    return tuple(w for w in some if w[0] < line_len) + ((line_len, 2),)


def norm_stats(r):
    centred = r - jnp.mean(r, axis=-1, keepdims=True)
    inv = lax.rsqrt(jnp.mean(centred * centred, axis=-1, keepdims=True) + EPSILON)
    return centred * inv, inv


def norm_back(dy, normed, inv, gain):
    scaled = dy * gain
    inner = (
        scaled
        - jnp.mean(scaled, axis=-1, keepdims=True)
        - normed * jnp.mean(scaled * normed, axis=-1, keepdims=True)
    )
    return inner * inv


def fold8(t):
    return jnp.sum(t.reshape(t.shape[0] // 8, 8, t.shape[1]), axis=0)


def head_lanes(half):
    lane = lax.broadcasted_iota(jnp.int32, (1, PAIR), 1)
    return (lane < HEAD) if half == 0 else (lane >= HEAD)


def query_meta(mk, at):
    return mk[0, :, pl.ds(at, SUB)].T


def self_mask(mk, meta, at, ks, wd):
    doc = mk[0, 0:1, pl.ds(ks, wd)] == meta[:, 0:1]
    low = mk[0, 1:2, pl.ds(ks, wd)] < meta[:, 2:3]
    key = lax.broadcasted_iota(jnp.int32, (SUB, wd), 1) + ks
    query = lax.broadcasted_iota(jnp.int32, (SUB, wd), 0) + at
    return doc & (low | (key == query))


def cross_mask(mk, meta, at, ks, wd):
    return mk[0, 3:4, pl.ds(ks, wd)] == meta[:, 0:1]


def by_width(var, ks, widths, run):
    ks = pl.multiple_of(ks, SUB)
    for index, (wd, together) in enumerate(widths):

        @pl.when(var == index)
        def _(wd=wd, together=together):
            if together == PAIRS:
                run(tuple(range(PAIRS)), ks, wd)
            else:

                @pl.loop(0, PAIRS // together)
                def _(i):
                    run(tuple(i * together + j for j in range(together)), ks, wd)


def stacked(t):
    zero = jnp.zeros((), t.dtype)
    return jnp.concatenate([jnp.where(head_lanes(half), t, zero) for half in range(2)])


def unstacked(t):
    return jnp.where(head_lanes(0), t[:SUB], t[SUB:])


def pair_cols(pair, base=0):
    if isinstance(pair, int):
        return slice(base + pair * PAIR, base + (pair + 1) * PAIR)
    return pl.ds(pl.multiple_of(base + pair * PAIR, PAIR), PAIR)


def head_col(values, pair):
    if isinstance(pair, int):
        return jnp.concatenate([values[:, 2 * pair : 2 * pair + 1], values[:, 2 * pair + 1 : 2 * pair + 2]])
    lane = lax.broadcasted_iota(jnp.int32, values.shape, 1)
    pick = lambda head: jnp.sum(jnp.where(lane == head, values, 0.0), axis=-1, keepdims=True)
    return jnp.concatenate([pick(2 * pair), pick(2 * pair + 1)])


def attend(pairs, q, rows, kv, mask, ks, wd, out, lse):
    mask = jnp.concatenate([mask, mask])
    keys = pl.ds(ks, wd)
    lane = lax.broadcasted_iota(jnp.int32, (SUB, 128), 1)
    scores = [mm_nt(stacked(q[rows, pair_cols(i)]), kv[keys, pair_cols(i)]) for i in pairs]
    scores = [jnp.where(mask, s, NEGATIVE_FILL) for s in scores]
    tops = [jnp.max(s, axis=-1, keepdims=True) for s in scores]
    exps = [jnp.exp(s - top) for s, top in zip(scores, tops)]
    sums = [jnp.sum(e, axis=-1, keepdims=True) for e in exps]
    probs = [(e * (1.0 / total)).astype(BF) for e, total in zip(exps, sums)]
    outs = [mm(prob, kv[keys, pair_cols(i, D)]) for prob, i in zip(probs, pairs)]
    logs_all = lse[rows, :]
    for i, o, top, total in zip(pairs, outs, tops, sums):
        out[rows, pair_cols(i)] = unstacked(o).astype(BF)
        logs = top + jnp.log(total)
        logs_all = jnp.where(lane == 2 * i, logs[:SUB], logs_all)
        logs_all = jnp.where(lane == 2 * i + 1, logs[SUB:], logs_all)
    lse[rows, :] = logs_all


def attend_back(pairs, q, g, lse, rows, kv, mask, ks, wd, acc, dq):
    mask = jnp.concatenate([mask, mask])
    keys = pl.ds(ks, wd)
    logs = lse[rows, :]
    qs = [stacked(q[rows, pair_cols(i)]) for i in pairs]
    gs = [stacked(g[rows, pair_cols(i)]) for i in pairs]
    scores = [mm_nt(qi, kv[keys, pair_cols(i)]) for qi, i in zip(qs, pairs)]
    dps = [mm_nt(gi, kv[keys, pair_cols(i, D)]) for gi, i in zip(gs, pairs)]
    probs = [jnp.exp(jnp.where(mask, s, NEGATIVE_FILL) - head_col(logs, i)) for s, i in zip(scores, pairs)]
    sums = [jnp.sum(prob * dp, axis=-1, keepdims=True) for prob, dp in zip(probs, dps)]
    dss = [(prob * (dp - total)).astype(BF) for prob, dp, total in zip(probs, dps, sums)]
    for i, gi, prob in zip(pairs, gs, probs):
        acc[pair_cols(i, D), keys] += mm(gi.T, prob.astype(BF))
    for i, qi, ds in zip(pairs, qs, dss):
        acc[pair_cols(i), keys] += mm(qi.T, ds)
    for i, ds in zip(pairs, dss):
        dq[rows, pair_cols(i)] = (unstacked(mm(ds, kv[keys, pair_cols(i)])) * SCALE).astype(BF)


def each_sub(row0, body):
    @pl.loop(0, BLOCK // SUB)
    def _(sub):
        body(sub, pl.ds(pl.multiple_of(sub * SUB, SUB), SUB), pl.multiple_of(row0 + sub * SUB, SUB))


def self_forward(widths, tab, xs, mk, wqkv, wso, kv, q_out, att_out, n0_out, s0_out, lse_out):
    b = pl.program_id(0)
    row0 = pl.multiple_of(tab[1, b], SUB)

    @pl.when(tab[2, b] == 1)
    def _():
        @pl.loop(0, kv.shape[1] // BLOCK)
        def _(i):
            rows = pl.ds(pl.multiple_of(i * BLOCK, BLOCK), BLOCK)
            kv[0, rows, :] = mm(xs[0, rows, :], wqkv[:, D:]).astype(BF)

    x = xs[0, pl.ds(row0, BLOCK), :]
    q_out[...] = mm(x, wqkv[:, :D]).astype(BF) * jnp.asarray(SCALE, BF)
    lse_out[...] = jnp.zeros_like(lse_out)

    def sub_block(sub, rows, at):
        meta = query_meta(mk, at)

        def run(pairs, ks, wd):
            mask = self_mask(mk, meta, at, ks, wd)
            attend(pairs, q_out, rows, kv.at[0], mask, ks, wd, att_out, lse_out)

        by_width(tab[5, 2 * b + sub], tab[4, 2 * b + sub], widths, run)

    each_sub(row0, sub_block)
    r = x.astype(F32) + mm(att_out[...], wso[...])
    normed, inv = norm_stats(r)
    n0_out[...] = normed
    s0_out[...] = jnp.broadcast_to(inv, s0_out.shape)


def cross_forward(widths, tab, es, mk, n0, wckv, wcq, gains, biases, mkv, cq, catt, clse):
    b = pl.program_id(0)
    row0 = pl.multiple_of(tab[1, b], SUB)

    @pl.when(tab[2, b] == 1)
    def _():
        @pl.loop(0, mkv.shape[1] // BLOCK)
        def _(i):
            rows = pl.ds(pl.multiple_of(i * BLOCK, BLOCK), BLOCK)
            mkv[0, rows, :] = mm(es[0, rows, :], wckv[...]).astype(BF)

    first = n0[...] * gains[0:1, :] + biases[0:1, :]
    cq[...] = mm(first.astype(BF), wcq[...]).astype(BF) * jnp.asarray(SCALE, BF)
    clse[...] = jnp.zeros_like(clse)

    def sub_block(sub, rows, at):
        meta = query_meta(mk, at)

        def run(pairs, ks, wd):
            mask = cross_mask(mk, meta, at, ks, wd)
            attend(pairs, cq, rows, mkv.at[0], mask, ks, wd, catt, clse)

        by_width(tab[7, 2 * b + sub], tab[6, 2 * b + sub], widths, run)

    each_sub(row0, sub_block)


def cross_backward(
    widths, tab, es, mk, n0, s0, att, gsecond, gatt, cq, clse, mkv, wckv, wso, wcq, gains,
    gfirst, gself, gline, att_grad, norm_grad,
    acc, dq_scr, dwckvt, dwcq, dwso, gb,
):
    b = pl.program_id(0)
    row0 = pl.multiple_of(tab[1, b], SUB)

    @pl.when(b == 0)
    def _():
        for ref in (dwckvt, dwcq, dwso, gb):
            ref[...] = jnp.zeros_like(ref)

    @pl.when(tab[2, b] == 1)
    def _():
        acc[...] = jnp.zeros_like(acc)

    def sub_block(sub, rows, at):
        meta = query_meta(mk, at)

        def run(pairs, ks, wd):
            mask = cross_mask(mk, meta, at, ks, wd)
            attend_back(pairs, cq, gatt, clse, rows, mkv.at[0], mask, ks, wd, acc, dq_scr)

        by_width(tab[7, 2 * b + sub], tab[6, 2 * b + sub], widths, run)

    each_sub(row0, sub_block)
    dq = dq_scr[...]
    first = n0[...] * gains[0:1, :] + gains[3:4, :]
    dwcq[...] += mm(first.astype(BF).T, dq)
    gf = gsecond[...] + mm_nt(dq, wcq[...])
    gb[0] += fold8(gf * n0[...])
    gb[1] += fold8(gf)
    gf = norm_back(gf, n0[...], s0[:, 0:1], gains[0:1, :])
    gfirst[...] = gf
    sg = gf.astype(BF)
    dwso[...] += mm(att[...].T, sg)
    gself[...] = mm_nt(sg, wso[...]).astype(BF)

    @pl.when(tab[3, b] == 1)
    def _():
        line_end(acc, es, wckv, 0, None, gline, dwckvt)

    @pl.when(b == pl.num_programs(0) - 1)
    def _():
        att_grad[: 2 * D, :] = dwckvt[...].astype(BF)
        att_grad[2 * D : 3 * D, :] = dwso[...].astype(BF)
        att_grad[3 * D :, :] = dwcq[...].astype(BF)
        sums = jnp.sum(gb[...], axis=1)
        none = jnp.zeros((2, D), F32)
        norm_grad[...] = jnp.concatenate([sums[0:1], none, sums[1:2], none, none])


def line_end(acc, inputs, weight, base, rows, gline, dwt):
    columns = 256

    @pl.loop(0, acc.shape[1] // columns)
    def _(i):
        cols = pl.ds(pl.multiple_of(i * columns, columns), columns)
        low = acc[:, cols].astype(BF)
        back = mm(weight[:, base:], low).T
        if rows is not None:
            back = back + rows[cols, :]
        gline[0, cols, :] = back.astype(BF)
        dwt[...] += mm(low, inputs[0, cols, :])


def self_backward(widths, tab, q, g, gf, lse, kv, mk, xs, wqkv, gline, qkv_grad, dq, acc, rows, dwq, dwkvt):
    b = pl.program_id(0)
    row0 = pl.multiple_of(tab[1, b], SUB)

    @pl.when(b == 0)
    def _():
        dwq[...] = jnp.zeros_like(dwq)
        dwkvt[...] = jnp.zeros_like(dwkvt)

    @pl.when(tab[2, b] == 1)
    def _():
        acc[...] = jnp.zeros_like(acc)
        rows[...] = jnp.zeros_like(rows)

    def sub_block(sub, here, at):
        meta = query_meta(mk, at)

        def run(pairs, ks, wd):
            mask = self_mask(mk, meta, at, ks, wd)
            attend_back(pairs, q, g, lse, here, kv.at[0], mask, ks, wd, acc, dq)

        by_width(tab[5, 2 * b + sub], tab[4, 2 * b + sub], widths, run)

    each_sub(row0, sub_block)

    x = xs[0, pl.ds(row0, BLOCK), :]
    dwq[...] += mm(x.T, dq[...])
    rows[pl.ds(row0, BLOCK), :] = gf[...] + mm_nt(dq[...], wqkv[:, :D])

    @pl.when(tab[3, b] == 1)
    def _():
        line_end(acc, xs, wqkv, D, rows, gline, dwkvt)

    @pl.when(b == pl.num_programs(0) - 1)
    def _():
        qkv_grad[:D, :] = dwq[...].astype(BF)
        qkv_grad[D:, :] = dwkvt[...].astype(BF)


def const_spec(shape):
    return pl.BlockSpec(shape, lambda b, t: (0,) * len(shape), pipeline_mode=pl.Buffered(1))


def row_spec(cols):
    return pl.BlockSpec((BLOCK, cols), lambda b, t: (b, 0))


def line_spec(shape):
    return pl.BlockSpec((1,) + shape, lambda b, t: (t[0, b],) + (0,) * len(shape))


def sds(shape, dtype):
    return jax.ShapeDtypeStruct(shape, dtype)


def kernels(
    lines, n, tab, xs, es, cot, mk, self_qkv, self_out, cross_q, cross_kv, cross_out, weights, norm_gain, norm_bias
):
    slots, line_len = xs.shape[0], xs.shape[1]
    whole, p, k = plan(lines, n)
    rows_all = whole * line_len + k * line_len // p
    blocks = rows_all // BLOCK
    widths = widths_for(line_len)
    params = pltpu.CompilerParams(vmem_limit_bytes=VMEM, dimension_semantics=("arbitrary",))

    def call(kernel, name, ins, in_specs, outs, out_specs, scratch, flops):
        return pl.pallas_call(
            kernel,
            name=name,
            grid_spec=pltpu.PrefetchScalarGridSpec(
                num_scalar_prefetch=1,
                grid=(blocks,),
                in_specs=in_specs,
                out_specs=out_specs,
                scratch_shapes=scratch,
            ),
            out_shape=outs,
            compiler_params=params,
            cost_estimate=pl.CostEstimate(
                flops=int(flops), bytes_accessed=16 << 20, transcendentals=1 << 20
            ),
        )(tab, *ins)

    line2 = (line_len, 2 * D)
    kv, q, att, n0, s0, lse = call(
        functools.partial(self_forward, widths),
        "self_forward",
        (xs, mk, self_qkv, self_out),
        [line_spec((line_len, D)), line_spec((8, line_len)), const_spec((D, 3 * D)), const_spec((D, D))],
        (
            sds((slots,) + line2, BF),
            sds((rows_all, D), BF),
            sds((rows_all, D), BF),
            sds((rows_all, D), F32),
            sds((rows_all, 128), F32),
            sds((rows_all, 128), F32),
        ),
        (line_spec(line2), row_spec(D), row_spec(D), row_spec(D), row_spec(128), row_spec(128)),
        [],
        2e10,
    )

    mkv, cq, catt, clse = call(
        functools.partial(cross_forward, widths),
        "cross_forward",
        (es, mk, n0, cross_kv, cross_q, norm_gain, norm_bias),
        [
            line_spec((line_len, D)), line_spec((8, line_len)), row_spec(D), const_spec((D, 2 * D)),
            const_spec((D, D)), const_spec((3, D)), const_spec((3, D)),
        ],
        (
            sds((slots,) + line2, BF),
            sds((rows_all, D), BF),
            sds((rows_all, D), BF),
            sds((rows_all, 128), F32),
        ),
        (line_spec(line2), row_spec(D), row_spec(D), row_spec(128)),
        [],
        2e10,
    )

    out, gsecond, gatt, ffn_grad, co_grad, norm_a = feed(
        cot, n0, catt, cross_out, weights, norm_gain, norm_bias, lines, n, line_len
    )

    gfirst, gself, enc_line, att_grad, norm_b = call(
        functools.partial(cross_backward, widths),
        "cross_backward",
        (
            es, mk, n0, s0, att, gsecond, gatt, cq, clse, mkv, cross_kv, self_out, cross_q,
            jnp.concatenate([norm_gain, norm_bias]),
        ),
        [
            line_spec((line_len, D)), line_spec((8, line_len)), row_spec(D), row_spec(128), row_spec(D),
            row_spec(D), row_spec(D), row_spec(D), row_spec(128), line_spec(line2), const_spec((D, 2 * D)),
            const_spec((D, D)), const_spec((D, D)), const_spec((6, D)),
        ],
        (
            sds((rows_all, D), F32),
            sds((rows_all, D), BF),
            sds((slots, line_len, D), BF),
            sds((4 * D, D), BF),
            sds((8, D), F32),
        ),
        (
            row_spec(D), row_spec(D), line_spec((line_len, D)), const_spec((4 * D, D)), const_spec((8, D)),
        ),
        [
            pltpu.VMEM((2 * D, line_len), F32),
            pltpu.VMEM((BLOCK, D), BF),
            pltpu.VMEM((2 * D, D), F32),
            pltpu.VMEM((D, D), F32),
            pltpu.VMEM((D, D), F32),
            pltpu.VMEM((2, 8, D), F32),
        ],
        3e10,
    )

    stream_line, qkv_grad = call(
        functools.partial(self_backward, widths),
        "self_backward",
        (q, gself, gfirst, lse, kv, mk, xs, self_qkv),
        [
            row_spec(D), row_spec(D), row_spec(D), row_spec(128), line_spec(line2), line_spec((8, line_len)),
            line_spec((line_len, D)), const_spec((D, 3 * D)),
        ],
        (sds((slots, line_len, D), BF), sds((3 * D, D), BF)),
        (line_spec((line_len, D)), const_spec((3 * D, D))),
        [
            pltpu.VMEM((BLOCK, D), BF),
            pltpu.VMEM((2 * D, line_len), F32),
            pltpu.VMEM((line_len, D), F32),
            pltpu.VMEM((D, D), F32),
            pltpu.VMEM((2 * D, D), F32),
        ],
        3e10,
    )
    return out, enc_line, stream_line, ffn_grad, att_grad, co_grad, qkv_grad, norm_a, norm_b


def remote(src, dst, send, recv, device):
    return pltpu.make_async_remote_copy(
        src_ref=src, dst_ref=dst, send_sem=send, recv_sem=recv, device_id={"seq": device},
        device_id_type=pl.DeviceIdType.MESH,
    )


def part_of(device, p):
    return (device % p + device // p) % p


class Exchange:
    def __init__(self, lines, n, line_len):
        self.n, self.piece = n, line_len // n
        self.whole, self.p, self.k = plan(lines, n)
        self.groups = n // self.p
        self.chunks = n // self.p
        self.part_len = line_len // self.p
        self.line_len = line_len
        self.shared0 = self.whole * n
        self.rows_p = self.k * self.part_len
        self.me = lax.axis_index("seq")
        self.group = self.me // self.p
        self.part = part_of(self.me, self.p)
        self.pos_part, self.pos_chunk = self.me // self.chunks, self.me % self.chunks

    def owner(self, group):
        return group * self.p + (self.pos_part + self.p * self.groups - group) % self.p


ROWS_AT, SHARES_AT = (-1, -1, 0, 5, 6), 1
FFN_LAG, NORM_LAG = 0, 1


class Dim:
    def __init__(self, axis, stride, size):
        self.axis, self.stride, self.size = axis, stride, size
        at = lax.axis_index(axis)
        self.index = at // stride % size
        self.rest = at - self.index * stride

    def peer(self, v):
        return (self.index + v) % self.size

    def device(self, v):
        return {self.axis: self.rest + self.peer(v) * self.stride}


def send_to(src, dst, sems, device):
    return pltpu.make_async_remote_copy(
        src_ref=src, dst_ref=dst, send_sem=sems[0], recv_sem=sems[1], device_id=device,
        device_id_type=pl.DeviceIdType.MESH,
    )


class Sems:
    def __init__(self, ref):
        self.ref, self.used = ref, 0

    def next(self):
        self.used += 1
        return self.ref.at[0, self.used - 1], self.ref.at[1, self.used - 1]


def mesh_dims(ex):
    return (
        Dim("dp", 1, 2), Dim("dp", 2, lax.axis_size("dp") // 2), Dim("seq", 1, ex.p), Dim("seq", ex.p, ex.groups),
    )


def greet(ex, core, yy):
    barrier = pltpu.get_barrier_semaphore()
    greeted = [{"seq": (ex.me + o) % ex.n} for o in range(1, ex.n)]
    greeted += [dim.device(v) for dim in (core, yy) for v in range(1, dim.size)]
    for device in greeted:
        pl.semaphore_signal(barrier, inc=1, device_id=device, device_id_type=pl.DeviceIdType.MESH)
    pl.semaphore_wait(barrier, len(greeted))


def start_all(copies):
    for copy in copies:
        copy.start()


def gather(dim, view, sems):
    copies = [send_to(view, view, sems.next(), dim.device(v)) for v in range(1, dim.size)]

    def finish():
        for copy in copies:
            copy.wait()

    return copies, finish


def in_kernel(
    ex, x_ref, rc_ref, e_ref, w_ref, xs, rc, es, weights, sem_w, sem_p, sem_f, sem_l, sem_g
):
    n, piece, w, k, me = ex.n, ex.piece, ex.whole, ex.k, ex.me
    core, yy, xx, zz = mesh_dims(ex)
    c, y, x, z = core.index, yy.index, xx.index, zz.index
    quarter = w_ref.shape[0] // (2 * yy.size)
    weights = weights.reshape(ex.groups, ex.p, yy.size, 2, quarter, w_ref.shape[1])
    own = pltpu.make_async_copy(
        w_ref.at[pl.ds(pl.multiple_of((y * 2 + c) * quarter, quarter), quarter)],
        weights.at[z, x, y, c], sem_l.at[3, 0],
    )
    own.start()
    greet(ex, core, yy)
    own.wait()
    sems = Sems(sem_g)
    stages = [
        gather(zz, weights.at[z, x, y, c], sems),
        gather(xx, weights.at[:, x, y, c], sems),
        gather(yy, weights.at[:, :, y, c], sems),
        gather(core, weights.at[:, :, :, c], sems),
    ]
    start_all(stages[0][0])

    def next_stage(i):
        stages[i][1]()
        if i + 1 < len(stages):
            start_all(stages[i + 1][0])

    spans = pl.ds(pl.multiple_of(me * piece, piece), piece)
    names = (x_ref, rc_ref, e_ref)

    def line_dst(out, slots):
        if out is rc:
            return rc.at[slots, me]
        return out.at[slots, spans]

    def whole_copies(a, o):
        to = (me + o) % n
        src = names[a]
        pairs = [(src.at[pl.ds(to * w, w)], line_dst((xs, rc, es)[a], pl.ds(k, w)))] if w else []
        return [
            remote(s, d, sem_w.at[0, a, i, o], sem_w.at[1, a, i, o], to)
            if o
            else pltpu.make_async_copy(s, d, sem_l.at[a, i])
            for i, (s, d) in enumerate(pairs)
        ]

    def shared_pairs(a, group):
        src = names[a]
        first = ex.shared0 + group * k
        return [(src.at[pl.ds(first, k)], line_dst((xs, rc, es)[a], pl.ds(0, k)))] if k else []

    def shared_send(a, u):
        group = (ex.group + u) % ex.groups
        to = ex.owner(group)
        return [
            remote(s, d, sem_p.at[0, a, i, u], sem_p.at[1, a, i, ex.pos_chunk], to)
            for i, (s, d) in enumerate(shared_pairs(a, group))
        ]

    def shared_local(a):
        return [
            pltpu.make_async_copy(s, d, sem_l.at[a, max(w, 1) + i])
            for i, (s, d) in enumerate(shared_pairs(a, ex.group))
        ]

    def shared_arrival(a, j):
        return [
            remote(s, d, sem_p.at[0, a, i, 0], sem_p.at[1, a, i, j], me)
            for i, (s, d) in enumerate(shared_pairs(a, ex.group))
        ]

    def forwards(a):
        out = (xs, rc, es)[a]
        mine = ex.part * ex.part_len
        if a == 1:
            view = rc.at[pl.ds(0, k), pl.ds(ex.part * ex.chunks, ex.chunks)]
        else:
            view = out.at[pl.ds(0, k), pl.ds(pl.multiple_of(mine, ex.part_len), ex.part_len)]
        return [
            remote(view, view, sem_f.at[0, a, v], sem_f.at[1, a, v], ex.group * ex.p + (me % ex.p + v) % ex.p)
            for v in range(1, ex.p)
        ]

    here = ex.pos_part == ex.part
    for a in range(3):
        for u in range(ex.groups if k else 0):
            if u == 0:

                @pl.when(here)
                def _():
                    for copy in shared_local(a):
                        copy.start()

                @pl.when(jnp.logical_not(here))
                def _():
                    for copy in shared_send(a, 0):
                        copy.start()

            else:
                for copy in shared_send(a, u):
                    copy.start()
        for o in range(n):
            for copy in whole_copies(a, o):
                copy.start()
    next_stage(0)
    for a in range(3):
        next_stage(a + 1)
        for j in range(ex.chunks if k else 0):
            own = ex.part * ex.chunks + j == me

            @pl.when(own)
            def _():
                for copy in shared_local(a):
                    copy.wait()

            @pl.when(jnp.logical_not(own))
            def _():
                for copy in shared_arrival(a, j):
                    copy.wait_recv()

        if k:
            for copy in forwards(a):
                copy.start()
    for a in range(3):
        for o in range(n):
            for copy in whole_copies(a, o):
                copy.wait()
        for u in range(ex.groups if k else 0):
            if u == 0:

                @pl.when(jnp.logical_not(here))
                def _():
                    for copy in shared_send(a, 0):
                        copy.wait_send()

            else:
                for copy in shared_send(a, u):
                    copy.wait_send()
        if k:
            for copy in forwards(a):
                copy.wait()


def feed_kernel(
    ex, cot_src, n0, catt, wco, wff, gains, biases,
    out, gsecond_out, gatt, ffn_grad, co_grad, norm_grad,
    cot, out_v, hid, gprime, dw1, dw2t, dwco, gb, sem_cs, sem_cw, sem_os, sem_ow,
):
    b, last = pl.program_id(0), pl.num_programs(0) - 1
    n, piece, w, k, me = ex.n, ex.piece, ex.whole, ex.k, ex.me

    def rows_at(row):
        return pl.ds(pl.multiple_of(row, piece), piece)

    def cot_copy(i, slot, row, sems, at, to):
        src, dst = cot_src.at[slot], cot.at[rows_at(row)]
        local = lambda: pltpu.make_async_copy(src, dst, sems.at[1, i, at])
        return local, lambda sent: send_to(src, dst, (sems.at[0, i, sent], sems.at[1, i, at]), {"seq": to})

    def cot_sends():
        for u in range(ex.groups if k else 0):
            group = (ex.group + u) % ex.groups
            to = ex.owner(group)
            for i in range(k):
                row = i * ex.part_len + ex.pos_chunk * piece
                local, far = cot_copy(i, ex.shared0 + group * k + i, row, sem_cs, ex.pos_chunk, to)
                yield to, local, functools.partial(far, u)
        for v in range(n):
            to = (me + v) % n
            for i in range(w):
                row = ex.rows_p + i * ex.line_len + me * piece
                local, far = cot_copy(i, to * w + i, row, sem_cw, me, to)
                yield to, local, functools.partial(far, v)

    def out_copy(row, slot, i, sems, sent, at, to):
        src, dst = out_v.at[rows_at(row)], out.at[slot]
        return (
            to,
            lambda: pltpu.make_async_copy(src, dst, sems.at[1, i, at]),
            lambda: send_to(src, dst, (sems.at[0, i, sent], sems.at[1, i, at]), {"seq": to}),
        )

    def out_shared(row):
        i, j = row // ex.part_len, row % ex.part_len // piece
        return out_copy(
            row, ex.shared0 + ex.group * k + i, i, sem_os, j, ex.group, ex.part * ex.chunks + j
        )

    def out_whole(row):
        at = row - ex.rows_p
        i, s = at // ex.line_len, at % ex.line_len // piece
        return out_copy(row, me * w + i, i, sem_ow, s, me, s)

    def either(to, here, there):
        @pl.when(to == me)
        def _():
            here()

        @pl.when(to != me)
        def _():
            there()

    @pl.when(b == 0)
    def _():
        for ref in (dw1, dw2t, dwco, gb):
            ref[...] = jnp.zeros_like(ref)
        core, yy = mesh_dims(ex)[:2]
        greet(ex, core, yy)
        for to, local, far in cot_sends():
            either(to, lambda: local().start(), lambda: far().start())

    first = n0[...] * gains[0:1, :] + biases[0:1, :]
    n1, s1 = norm_stats(first + mm(catt[...], wco[...]))
    second = n1 * gains[1:2, :] + biases[1:2, :]
    second_low = second.astype(BF)
    chunks, chunk = wff.shape[0], wff.shape[2]
    total = second
    for c in range(chunks):
        cols = slice(c * chunk, (c + 1) * chunk)
        v = mm(second_low, wff[c, :D, :])
        v2 = v * v
        t = jnp.tanh(GELU_C * (v + 0.044715 * (v2 * v)))
        half = 0.5 * (1.0 + t)
        h = (v * half).astype(BF)
        hid[:, cols] = h
        gprime[:, cols] = half + (0.5 * v) * (1.0 - t * t) * (GELU_C + (3 * 0.044715 * GELU_C) * v2)
        total = total + mm_nt(h, wff[c, D:, :])
    n2, s2 = norm_stats(total)
    here = pl.ds(pl.multiple_of(b * BLOCK, BLOCK), BLOCK)
    out_v[here, :] = (n2 * gains[2:3, :] + biases[2:3, :]).astype(BF)

    for q in range(BLOCK // piece):
        row = b * BLOCK + q * piece

        @pl.when(row < ex.rows_p)
        def _():
            i, j = row // ex.part_len, row % ex.part_len // piece
            local, far = cot_copy(i, 0, row, sem_cs, j, me)
            either(ex.part * ex.chunks + j, lambda: local().wait(), lambda: far(0).wait_recv())
            to, local, far = out_shared(row)
            either(to, lambda: local().start(), lambda: far().start())

        @pl.when(row >= ex.rows_p)
        def _():
            at = row - ex.rows_p
            i, s = at // ex.line_len, at % ex.line_len // piece
            local, far = cot_copy(i, 0, row, sem_cw, s, me)
            either(s, lambda: local().wait(), lambda: far(0).wait_recv())
            to, local, far = out_whole(row)
            either(to, lambda: local().start(), lambda: far().start())

    dy = cot[here, :].astype(F32)
    gb[1] += fold8(dy * n2)
    gb[3] += fold8(dy)
    gthird = norm_back(dy, n2, s2, gains[2:3, :])
    fg = gthird.astype(BF)
    fgt, sect = fg.T, second_low.T
    back = gthird
    for c in range(chunks):
        cols = slice(c * chunk, (c + 1) * chunk)
        pg = (mm(fg, wff[c, D:, :]) * gprime[:, cols]).astype(BF)
        dw2t[:, cols] += mm(fgt, hid[:, cols])
        dw1[:, cols] += mm(sect, pg)
        back = back + mm_nt(pg, wff[c, :D, :])
    gb[0] += fold8(back * n1)
    gb[2] += fold8(back)
    gsecond = norm_back(back, n1, s1, gains[1:2, :])
    gsecond_out[...] = gsecond
    cg = gsecond.astype(BF)
    dwco[...] += mm(catt[...].T, cg)
    gatt[...] = mm_nt(cg, wco[...]).astype(BF)

    @pl.when(b == last)
    def _():
        for c in range(chunks):
            cols = slice(c * chunk, (c + 1) * chunk)
            ffn_grad[c, :D, :] = dw1[:, cols].astype(BF)
            ffn_grad[c, D:, :] = dw2t[:, cols].astype(BF)
        co_grad[...] = dwco[...].astype(BF)
        sums = jnp.sum(gb[...], axis=1)
        none = jnp.zeros((1, D), F32)
        norm_grad[...] = jnp.concatenate([none, sums[:2], none, sums[2:], none, none])
        for to, local, far in cot_sends():
            either(to, lambda: None, lambda: far().wait_send())
        for row in range(0, ex.rows_p, piece):
            to, local, far = out_shared(row)
            either(to, lambda: local().wait(), lambda: far().wait_send())
        for row in range(ex.rows_p, cot.shape[0], piece):
            to, local, far = out_whole(row)
            either(to, lambda: local().wait(), lambda: far().wait_send())
        for i in range(k):
            for group in range(ex.groups):
                arrival = out_copy(0, ex.shared0 + group * k + i, i, sem_os, 0, group, me)[2]
                either(ex.owner(group), lambda: None, lambda: arrival().wait_recv())
        for i in range(w):
            for s in range(n):
                arrival = out_copy(0, s * w + i, i, sem_ow, 0, s, me)[2]
                either(s, lambda: None, lambda: arrival().wait_recv())


def feed(cot_src, n0, catt, wco, weights, gains, biases, lines, n, line_len):
    whole, p, k = plan(lines, n)
    most = max(k, whole, 1)
    rows_all, cols = n0.shape[0], weights.shape[2]
    ff = n * cols

    def kernel(*refs):
        feed_kernel(Exchange(lines, n, line_len), *refs)

    row = lambda c: pl.BlockSpec((BLOCK, c), lambda b: (b, 0))
    const = lambda *shape: pl.BlockSpec(shape, lambda b: (0,) * len(shape), pipeline_mode=pl.Buffered(1))
    hbm = pl.BlockSpec(memory_space=pl.ANY)
    dma = pltpu.SemaphoreType.DMA
    return pl.pallas_call(
        kernel,
        name="feed",
        grid=(rows_all // BLOCK,),
        in_specs=[hbm, row(D), row(D), const(D, D), const(n, 2 * D, cols), const(3, D), const(3, D)],
        out_specs=[hbm, row(D), row(D), const(n, 2 * D, cols), const(D, D), const(8, D)],
        out_shape=(
            sds((lines, line_len // n, D), BF),
            sds((rows_all, D), F32),
            sds((rows_all, D), BF),
            sds((n, 2 * D, cols), BF),
            sds((D, D), BF),
            sds((8, D), F32),
        ),
        scratch_shapes=[
            pltpu.VMEM((rows_all, D), BF),
            pltpu.VMEM((rows_all, D), BF),
            pltpu.VMEM((BLOCK, ff), BF),
            pltpu.VMEM((BLOCK, ff), F32),
            pltpu.VMEM((D, ff), F32),
            pltpu.VMEM((D, ff), F32),
            pltpu.VMEM((D, D), F32),
            pltpu.VMEM((4, 8, D), F32),
            dma((2, most, n)),
            dma((2, most, n)),
            dma((2, most, n)),
            dma((2, most, n)),
        ],
        compiler_params=pltpu.CompilerParams(
            collective_id=3, has_side_effects=True, vmem_limit_bytes=VMEM,
            dimension_semantics=("arbitrary",),
        ),
        cost_estimate=pl.CostEstimate(flops=int(4e10), bytes_accessed=16 << 20, transcendentals=1 << 20),
    )(cot_src, n0, catt, wco, weights, gains, biases)


def exchange_in(stream, rc, encoder, weights, lines, n, line_len, dp):
    whole, p, k = plan(lines, n)
    hops = 1 + dp // 2 - 1 + p - 1 + n // p - 1
    slots, piece = k + whole, line_len // n
    most = max(k, whole, 1)

    def kernel(*refs):
        in_kernel(Exchange(lines, n, line_len), *refs)

    dma = pltpu.SemaphoreType.DMA
    return pl.pallas_call(
        kernel,
        name="exchange_in",
        in_specs=[pl.BlockSpec(memory_space=pl.ANY)] * 4,
        out_specs=[pl.BlockSpec(memory_space=pl.ANY)] * 4,
        out_shape=(
            sds((slots, line_len, D), BF),
            sds((slots, n, 1, piece), jnp.int32),
            sds((slots, line_len, D), BF),
            sds((n,) + weights.shape, BF),
        ),
        scratch_shapes=[
            dma((2, 3, most, n)), dma((2, 3, most, n)), dma((2, 3, max(p, 2))), dma((4, 2 * most)),
            dma((2, hops)),
        ],
        compiler_params=pltpu.CompilerParams(collective_id=1, has_side_effects=True),
    )(stream, rc, encoder, weights)


def flat_loop(lead, run):
    @pl.loop(0, math.prod(lead))
    def _(i):
        index = []
        for size in reversed(lead):
            index.append(i % size)
            i = i // size
        run(tuple(reversed(index)))


def add_into(dst, sources, lead):
    def run(index):
        total = dst[index].astype(F32)
        for source in sources:
            total = total + source[index].astype(F32)
        dst[index] = total.astype(dst.dtype)

    flat_loop(lead, run)


def finish_kernel(
    ex, enc_line, stream_line, ffn_grad, att_grad, co_grad, qkv_grad, norm_a, norm_b,
    enc, stream, ffn, att, norms,
    ffn_v, att_v, norm_v, ffn_bufs, att_bufs, norm_bufs, own_v, part_v,
    sem_red, sem_w, sem_p, sem_l, sem_s, sem_in,
):
    n, piece, w, k, p, me = ex.n, ex.piece, ex.whole, ex.k, ex.p, ex.me
    core, yy, xx, zz = mesh_dims(ex)
    outer = yy.size

    loads = [
        pltpu.make_async_copy(ffn_grad, ffn_v, sem_in.at[0]),
        pltpu.make_async_copy(att_grad, att_v.at[pl.ds(0, 4 * D)], sem_in.at[1]),
        pltpu.make_async_copy(co_grad, att_v.at[pl.ds(4 * D, D)], sem_in.at[2]),
        pltpu.make_async_copy(qkv_grad, att_v.at[pl.ds(5 * D, 3 * D)], sem_in.at[3]),
    ]
    lines = (enc_line, stream_line)
    mine = pl.ds(pl.multiple_of(ex.part * ex.part_len, ex.part_len), ex.part_len)
    if k:
        loads += [
            pltpu.make_async_copy(lines[a].at[pl.ds(0, k), mine], own_v.at[a], sem_in.at[4 + a])
            for a in range(2)
        ]
    start_all(loads)
    norm_v[...] = norm_a[...] + norm_b[...]
    greet(ex, core, yy)

    fl = ffn_v.shape
    rows = fl[1] // (2 * outer)
    ffn_6 = ffn_v.reshape(ex.groups, p, outer, 2, rows, fl[2])
    att_rows = att_v.shape[0] // (2 * outer * n)
    att_6 = att_v.reshape(2, outer, p, ex.groups, att_rows, D)
    ffn_o = ffn.reshape(outer, 2, rows, fl[2])
    att_o = att.reshape(2, outer, p, ex.groups, att_rows, D)
    c, y, x, z = core.index, yy.index, xx.index, zz.index
    sems = Sems(sem_red)

    def scatter(dim, view, buf, lead):
        copies = [
            send_to(view(dim.peer(v)), buf.at[v - 1], sems.next(), dim.device(v)) for v in range(1, dim.size)
        ]

        def finish():
            for copy in copies:
                copy.wait()
            add_into(view(dim.index), [buf.at[v - 1] for v in range(1, dim.size)], lead)

        return copies, finish

    def place(src, dst, sem):
        copy = pltpu.make_async_copy(src, dst, sem)
        return [copy], copy.wait

    def exchange_all(dim, buf):
        copies = [send_to(norm_v, buf.at[v - 1], sems.next(), dim.device(v)) for v in range(1, dim.size)]

        def finish():
            for copy in copies:
                copy.wait()
            norm_v[...] = sum([buf[v - 1] for v in range(1, dim.size)], norm_v[...])

        return copies, finish

    g, o = ex.groups, outer

    def att_stream(h, half):
        r = pl.ds(h * half, half)
        bufs = [buf.at[..., r, :] for buf in att_bufs]
        return [
            scatter(core, lambda t: att_6.at[t, :, :, :, r], bufs[0], (o, p, g)),
            scatter(yy, lambda t: att_6.at[c, t, :, :, r], bufs[1], (p, g)),
            scatter(xx, lambda t: att_6.at[c, y, t, :, r], bufs[2], (g,)),
            scatter(zz, lambda t: att_6.at[c, y, x, t, r], bufs[3], ()),
            place(att_6.at[c, y, x, z, r], att_o.at[c, y, x, z, r], sem_in.at[7 + h]),
            gather(zz, att_o.at[c, y, x, z, r], sems),
            gather(xx, att_o.at[c, y, x, :, r], sems),
            gather(yy, att_o.at[c, y, :, :, r], sems),
            gather(core, att_o.at[c, :, :, :, r], sems),
        ]

    halves = 2 if att_rows % 32 == 0 else 1
    streams = [att_stream(h, att_rows // halves) for h in range(halves)]
    streams += [
        [
            scatter(core, lambda t: ffn_6.at[:, :, :, t], ffn_bufs[0], (g, p, o)),
            scatter(yy, lambda t: ffn_6.at[:, :, t, c], ffn_bufs[1], (g, p)),
            scatter(xx, lambda t: ffn_6.at[:, t, y, c], ffn_bufs[2], (g,)),
            scatter(zz, lambda t: ffn_6.at[t, x, y, c], ffn_bufs[3], ()),
            place(ffn_6.at[z, x, y, c], ffn_o.at[y, c], sem_in.at[6]),
            gather(yy, ffn_o.at[y, c], sems),
            gather(core, ffn_o.at[:, c], sems),
        ],
        [exchange_all(dim, norm_bufs[i]) for i, dim in enumerate((core, yy, xx, zz))],
    ]

    lags = [0] * halves + [FFN_LAG, NORM_LAG]

    def whole_src(a, i, to):
        return lines[a].at[k + i, pl.ds(pl.multiple_of(to * piece, piece), piece)]

    outs = (enc, stream)

    def whole_copies(a, v):
        to = (me + v) % n
        result = []
        for i in range(w):
            src, dst = whole_src(a, i, to), outs[a].at[me * w + i]
            result.append(
                send_to(src, dst, (sem_w.at[0, a, i, v], sem_w.at[1, a, i, v]), {"seq": to})
                if v
                else pltpu.make_async_copy(src, dst, sem_l.at[a, i])
            )
        return result

    def shared_pair(a, i, j):
        at = pl.ds(pl.multiple_of(j * piece, piece), piece)
        src = own_v.at[a, i, at]
        return src, outs[a].at[ex.shared0 + ex.group * k + i]

    def shared_copies(a, u):
        j = (ex.group + u) % ex.chunks
        to = ex.part * ex.chunks + j
        return to, [
            send_to(*shared_pair(a, i, j), (sem_p.at[0, a, i, u], sem_p.at[1, a, i, ex.group]), {"seq": to})
            for i in range(k)
        ]

    def local_copies(a):
        return [
            pltpu.make_async_copy(*shared_pair(a, i, ex.pos_chunk), sem_l.at[a, max(w, 1) + i])
            for i in range(k)
        ]

    def each_shared(a, remote_run, local_run):
        for u in range(ex.chunks if k else 0):
            to, copies = shared_copies(a, u)

            @pl.when(to != me)
            def _():
                for copy in copies:
                    remote_run(copy)

            @pl.when(to == me)
            def _():
                for copy in local_copies(a):
                    local_run(copy)

    def sharing(a, v):
        part = (ex.part + v) % p
        theirs = pl.ds(pl.multiple_of(part * ex.part_len, ex.part_len), ex.part_len)
        return send_to(
            lines[a].at[pl.ds(0, k), theirs], part_v.at[a, v - 1], (sem_s.at[0, a, v], sem_s.at[1, a, v]),
            xx.device(v),
        )

    for copy in loads:
        copy.wait()
    for stages in streams:
        start_all(stages[0][0])
    shares = [sharing(a, v) for a in range(2) for v in range(1, p)] if k else []
    start_all(shares)

    def start_whole(a, places):
        for v in places:
            start_all(whole_copies(a, v))

    def start_shared(a):
        each_shared(a, lambda copy: copy.start(), lambda copy: copy.start())

    batches = [
        lambda: start_whole(0, range(n)),
        lambda: start_whole(1, range(n // 2)),
        lambda: start_whole(1, range(n // 2, n)),
        lambda: start_shared(0),
        lambda: start_shared(1),
    ]

    def start_batches(step):
        for at, batch in zip(ROWS_AT, batches):
            if step == at:
                batch()

    start_batches(-1)
    for step in range(max(len(stages) + lag for stages, lag in zip(streams, lags))):
        for stages, lag in zip(streams, lags):
            stage = step - lag
            if 0 <= stage < len(stages):
                stages[stage][1]()
            if 0 <= stage < len(stages) - 1:
                start_all(stages[stage + 1][0])
        if step == SHARES_AT:
            for copy in shares:
                copy.wait()
            for a in range(2 if k else 0):
                add_into(own_v.at[a], [part_v.at[a, v - 1] for v in range(1, p)], (k,))
        start_batches(step)
    norms[...] = norm_v[...]
    for a in range(2):
        for v in range(n):
            for copy in whole_copies(a, v):
                copy.wait()
        each_shared(a, lambda copy: copy.wait_send(), lambda copy: copy.wait())
        for group in range(ex.groups if k else 0):

            @pl.when(ex.owner(group) != me)
            def _():
                for i in range(k):
                    sems = (sem_p.at[0, a, i, 0], sem_p.at[1, a, i, group])
                    send_to(*shared_pair(a, i, 0), sems, {"seq": me}).wait_recv()


def finish(arrays, lines, n, line_len, dp):
    whole, p, k = plan(lines, n)
    piece, most, groups, outer = line_len // n, max(k, whole, 1), n // p, dp // 2
    cols = arrays[2].shape[2]
    rows, att_rows = 2 * D // dp, 8 * D // (dp * n)
    part_len = line_len // p
    slots = max(k, 1)

    def kernel(*refs):
        refs = list(refs)
        grouped = refs[:16] + [refs[16:20], refs[20:24], refs[24:28]] + refs[28:]
        finish_kernel(Exchange(lines, n, line_len), *grouped)

    dma = pltpu.SemaphoreType.DMA
    hops = (1, outer - 1, p - 1, groups - 1)
    hbm = pl.BlockSpec(memory_space=pl.ANY)
    vmem = pl.BlockSpec(memory_space=pltpu.VMEM)
    at_least = lambda q: max(q, 1)
    return pl.pallas_call(
        kernel,
        name="finish",
        in_specs=[hbm] * 6 + [vmem] * 2,
        out_specs=[hbm] * 2 + [vmem] * 3,
        out_shape=[sds((lines, piece, D), BF)] * 2
        + [sds((2 * D, cols), BF), sds((8 * D, D), BF), sds((8, D), F32)],
        scratch_shapes=[
            pltpu.VMEM((n, 2 * D, cols), BF),
            pltpu.VMEM((8 * D, D), BF),
            pltpu.VMEM((8, D), F32),
            pltpu.VMEM((1, groups, p, outer, rows, cols), BF),
            pltpu.VMEM((at_least(outer - 1), groups, p, rows, cols), BF),
            pltpu.VMEM((at_least(p - 1), groups, rows, cols), BF),
            pltpu.VMEM((at_least(groups - 1), rows, cols), BF),
            pltpu.VMEM((1, outer, p, groups, att_rows, D), BF),
            pltpu.VMEM((at_least(outer - 1), p, groups, att_rows, D), BF),
            pltpu.VMEM((at_least(p - 1), groups, att_rows, D), BF),
            pltpu.VMEM((at_least(groups - 1), att_rows, D), BF),
            *[pltpu.VMEM((at_least(q), 8, D), F32) for q in hops],
            pltpu.VMEM((2, slots, part_len, D), BF),
            pltpu.VMEM((2, at_least(p - 1), slots, part_len, D), BF),
            dma((2, 7 * sum(hops))),
            dma((2, 2, most, n)),
            dma((2, 2, most, n)),
            dma((2, 2 * most)),
            dma((2, 2, max(p, 2))),
            dma((9,)),
        ],
        compiler_params=pltpu.CompilerParams(
            collective_id=2, has_side_effects=True, vmem_limit_bytes=VMEM
        ),
    )(*arrays)


def assemble_kernel(
    tab, out_in, enc_in, stream_in, att, ffn, norms,
    out, stream, enc, qkv, so, cq, ckv, co, ffn_in_grad, ffn_out_grad, gain, bias,
):
    i = pl.program_id(0)
    out[...] = out_in[...]
    stream[...] = stream_in[...].astype(F32)
    enc[...] = enc_in[...].astype(F32)
    plain = {2: so, 3: cq, 4: co, 5: qkv}
    turned = {0: ckv, 1: ckv, 6: qkv, 7: qkv}
    for step, ref in plain.items():

        @pl.when(i == step)
        def _(ref=ref):
            ref[...] = att[...].astype(F32)

    for step, ref in turned.items():

        @pl.when(i == step)
        def _(ref=ref):
            ref[...] = att[...].T.astype(F32)

    @pl.when(i == 8)
    def _():
        ffn_in_grad[...] = ffn[:D, :].astype(F32)
        ffn_out_grad[...] = ffn[D:, :].T.astype(F32)
        gain[...] = norms[:3, :]
        bias[...] = norms[3:6, :]


def assemble(slot_of, output, encoder_grad, stream_grad, att, ffn, norms):
    lines, piece = output.shape[:2]
    cols = ffn.shape[1]
    most = lines - 1
    line_in = pl.BlockSpec((1, piece, D), lambda i, t: (t[jnp.minimum(i, most)], 0, 0))
    line_out = pl.BlockSpec((1, piece, D), lambda i, t: (jnp.minimum(i, most), 0, 0))
    whole = lambda *shape: pl.BlockSpec(shape, lambda i, t: (0, 0), pipeline_mode=pl.Buffered(1))
    square = lambda at: pl.BlockSpec((D, D), lambda i, t: (0, at(i)))
    f32 = lambda *shape: sds(shape, F32)
    return pl.pallas_call(
        assemble_kernel,
        name="assemble",
        grid_spec=pltpu.PrefetchScalarGridSpec(
            num_scalar_prefetch=1,
            grid=(max(lines, 9),),
            in_specs=[
                line_in, line_in, line_in, pl.BlockSpec((D, D), lambda i, t: (jnp.minimum(i, 7), 0)),
                whole(2 * D, cols), whole(8, D),
            ],
            out_specs=[
                line_out, line_out, line_out,
                square(lambda i: jnp.clip(i - 5, 0, 2)),
                whole(D, D), whole(D, D),
                square(lambda i: jnp.minimum(i, 1)),
                whole(D, D), whole(D, cols), whole(cols, D), whole(3, D), whole(3, D),
            ],
        ),
        out_shape=[
            sds((lines, piece, D), BF), f32(lines, piece, D), f32(lines, piece, D), f32(D, 3 * D), f32(D, D),
            f32(D, D), f32(D, 2 * D), f32(D, D), f32(D, cols), f32(cols, D), f32(3, D), f32(3, D),
        ],
        compiler_params=pltpu.CompilerParams(
            vmem_limit_bytes=VMEM, dimension_semantics=("arbitrary",)
        ),
    )(slot_of, output, encoder_grad, stream_grad, att, ffn, norms)


def doc_numbers(bounds, places):
    return jnp.sum((bounds[:, None, :] <= places[None, :, None]).astype(jnp.int32), axis=2)


def body(
    stream, encoder, cotangent, self_qkv, self_out, cross_q, cross_kv, cross_out, ffn_in, ffn_out,
    norm_gain, norm_bias, lengths, enc_lengths, ranks, cuts,
):
    n = lax.axis_size("seq")
    me = lax.axis_index("seq")
    lines, piece = stream.shape[0], stream.shape[1]
    line_len = piece * n
    whole, p, k = plan(lines, n)
    groups = n // p
    slots = k + whole
    part_len = line_len // p
    rows_p, rows_w = k * part_len, whole * line_len
    rows_all = rows_p + rows_w
    ff = ffn_in.shape[1] * n
    group, part = me // p, part_of(me, p)
    widths = widths_for(line_len)
    i32 = jnp.int32

    cost = jnp.sum(lengths * lengths, axis=1)
    order = jnp.arange(lines, dtype=i32)
    lighter = (cost[None, :] < cost[:, None]) | (
        (cost[None, :] == cost[:, None]) & (order[None, :] < order[:, None])
    )
    rank = jnp.sum(lighter.astype(i32), axis=1)
    slot_of = jnp.where(rank < whole * n, rank, whole * n + lines - 1 - rank)
    line_of = jnp.sum(jnp.where(slot_of[None, :] == order[:, None], order[None, :], 0), axis=1)

    rc_in = (ranks * 32 + cuts)[line_of][:, None, :]
    shard = jnp.concatenate([ffn_in, ffn_out.T])
    cot = cotangent[line_of]
    xs, rc, es, weights = exchange_in(
        stream[line_of], rc_in, encoder[line_of], shard, lines, n, line_len, lax.axis_size("dp")
    )
    rc = rc.reshape(slots, line_len)
    own_slots = jnp.concatenate([whole * n + group * k + jnp.arange(k), me * whole + jnp.arange(whole)])
    mine = line_of[own_slots.astype(i32)]
    cum_t = jnp.cumsum(lengths[mine], axis=1)
    cum_e = jnp.cumsum(enc_lengths[mine], axis=1)
    places = jnp.arange(line_len, dtype=i32)
    doc = doc_numbers(cum_t, places)
    src = doc_numbers(cum_e, places)
    zero = jnp.zeros_like(rc)
    mk = jnp.stack([doc, rc // 32, rc % 32, src, zero, zero, zero, zero], axis=1).astype(F32)

    block_line = [j for j in range(k) for _ in range(part_len // BLOCK)]
    block_line += [k + j for j in range(whole) for _ in range(line_len // BLOCK)]
    block_row = [r * BLOCK for j in range(k) for r in range(part_len // BLOCK)]
    block_row += [r * BLOCK for j in range(whole) for r in range(line_len // BLOCK)]
    blocks = len(block_line)
    begin = [int(i == 0 or block_line[i] != block_line[i - 1]) for i in range(blocks)]
    end = [int(i == blocks - 1 or block_line[i] != block_line[i + 1]) for i in range(blocks)]
    per = BLOCK // SUB
    bl = jnp.asarray(block_line, i32)
    br = jnp.asarray(block_row, i32) + jnp.where(bl < k, part * part_len, 0)
    sub_line = jnp.repeat(bl, per)
    sub_row = jnp.repeat(br, per) + jnp.tile(jnp.arange(per, dtype=i32) * SUB, blocks)
    ct, ce = cum_t[sub_line], cum_e[sub_line]
    before = ct <= sub_row[:, None]
    after = ct > sub_row[:, None] + (SUB - 1)

    def key_range(bounds):
        start = jnp.max(jnp.where(before, bounds, 0), axis=1)
        stop = jnp.min(jnp.where(after, bounds, line_len), axis=1)
        ks = start // SUB * SUB
        table = jnp.asarray([wd for wd, _ in widths], i32)
        var = jnp.sum((stop - ks)[:, None] > table[None, :], axis=1).astype(i32)
        wd = jnp.sum(jnp.where(var[:, None] == jnp.arange(len(widths)), table[None, :], 0), axis=1)
        return jnp.minimum(ks, line_len - wd), var

    sks, svar = key_range(ct)
    cks, cvar = key_range(ce)
    pad = jnp.zeros((blocks * (per - 1),), i32)
    wide = lambda v: jnp.concatenate([jnp.asarray(v, i32), pad])
    tab = jnp.stack([wide(bl), wide(br), wide(begin), wide(end), sks, svar, cks, cvar])

    output, *arrays = kernels(
        lines, n, tab, xs, es, cot, mk, self_qkv, self_out, cross_q, cross_kv, cross_out, weights, norm_gain, norm_bias
    )
    encoder_grad, stream_grad, ffn, att, norms = finish(
        arrays, lines, n, line_len, lax.axis_size("dp")
    )
    return tuple(assemble(slot_of.astype(i32), output, encoder_grad, stream_grad, att, ffn, norms))


def solution(mesh):
    lines = P("dp", "seq", None)
    in_specs = (
        lines, lines, lines, P(), P(), P(), P(), P(), P(None, "seq"), P("seq", None), P(), P(),
        P("dp", None), P("dp", None), P("dp", "seq"), P("dp", "seq"),
    )
    out_specs = (
        lines, lines, lines, P(), P(), P(), P(), P(), P(None, "seq"), P("seq", None), P(), P(),
    )
    return jax.shard_map(body, mesh=mesh, in_specs=in_specs, out_specs=out_specs, check_vma=False)
```

```python
import functools
import math

import jax
import jax.numpy as jnp
from jax import lax
from jax.experimental import pallas as pl
from jax.experimental.pallas import tpu as pltpu
from jax.sharding import PartitionSpec as P

D = 512
HEADS = 8
HEAD = 64
PAIR = 2 * HEAD
PAIRS = HEADS // 2
NEGATIVE_FILL = -1e30
EPSILON = 1e-05
SCALE = HEAD ** (-0.5)
BLOCK = 256
SUB = 256
ALIGN = 128
SUBS = BLOCK // SUB
CROSS, INV = HEADS, 2 * HEADS
BF = jnp.bfloat16
F32 = jnp.float32
NT = (((1,), (1,)), ((), ()))
GELU_C = math.sqrt(2.0 / math.pi)
VMEM = 60 * 1024 * 1024


def mm(left, right):
    return jnp.dot(left, right, preferred_element_type=F32)


def mm_nt(left, right):
    return lax.dot_general(left, right, NT, preferred_element_type=F32)


def plan(lines, n):
    whole = lines // n
    rest = lines - whole * n
    groups = math.gcd(rest, n) if rest else n
    return whole, n // groups, rest // groups


def widths_for(line_len):
    some = ((384, 4), (512, 4), (640, 4))
    return tuple(w for w in some if w[0] < line_len) + ((line_len, 2),)


def norm_stats(r):
    centred = r - jnp.mean(r, axis=-1, keepdims=True)
    inv = lax.rsqrt(jnp.mean(centred * centred, axis=-1, keepdims=True) + EPSILON)
    return centred * inv, inv


def norm_back(dy, normed, inv, gain):
    scaled = dy * gain
    inner = (
        scaled
        - jnp.mean(scaled, axis=-1, keepdims=True)
        - normed * jnp.mean(scaled * normed, axis=-1, keepdims=True)
    )
    return inner * inv


def fold8(t):
    return jnp.sum(t.reshape(t.shape[0] // 8, 8, t.shape[1]), axis=0)


def head_lanes(half):
    lane = lax.broadcasted_iota(jnp.int32, (1, PAIR), 1)
    return (lane < HEAD) if half == 0 else (lane >= HEAD)


def query_meta(mk, at):
    return mk[0, :, pl.ds(at, SUB)].T


def self_mask(mk, meta, at, ks, wd):
    doc = mk[0, 0:1, pl.ds(ks, wd)] == meta[:, 0:1]
    low = mk[0, 1:2, pl.ds(ks, wd)] < meta[:, 2:3]
    key = lax.broadcasted_iota(jnp.int32, (SUB, wd), 1) + ks
    query = lax.broadcasted_iota(jnp.int32, (SUB, wd), 0) + at
    return doc & (low | (key == query))


def cross_mask(mk, meta, at, ks, wd):
    return mk[0, 3:4, pl.ds(ks, wd)] == meta[:, 0:1]


def by_width(var, ks, widths, run):
    ks = pl.multiple_of(ks, ALIGN)
    for index, (wd, together) in enumerate(widths):

        @pl.when(var == index)
        def _(wd=wd, together=together):
            if together == PAIRS:
                run(tuple(range(PAIRS)), ks, wd)
            else:

                @pl.loop(0, PAIRS // together)
                def _(i):
                    run(tuple(i * together + j for j in range(together)), ks, wd)


def stacked(t):
    zero = jnp.zeros((), t.dtype)
    return jnp.concatenate([jnp.where(head_lanes(half), t, zero) for half in range(2)])


def unstacked(t):
    return jnp.where(head_lanes(0), t[:SUB], t[SUB:])


def pair_cols(pair, base=0):
    if isinstance(pair, int):
        return slice(base + pair * PAIR, base + (pair + 1) * PAIR)
    return pl.ds(pl.multiple_of(base + pair * PAIR, PAIR), PAIR)


def head_col(values, pair, base):
    head = base + 2 * pair
    if isinstance(pair, int):
        return jnp.concatenate([values[:, head : head + 1], values[:, head + 1 : head + 2]])
    lane = lax.broadcasted_iota(jnp.int32, values.shape, 1)
    pick = lambda at: jnp.sum(jnp.where(lane == at, values, 0.0), axis=-1, keepdims=True)
    return jnp.concatenate([pick(head), pick(head + 1)])


def attend(pairs, q, rows, kv, mask, ks, wd, out, stats, base):
    mask = jnp.concatenate([mask, mask])
    keys = pl.ds(ks, wd)
    lane = lax.broadcasted_iota(jnp.int32, (SUB, 128), 1)
    scores = [mm_nt(stacked(q[rows, pair_cols(i)]), kv[keys, pair_cols(i)]) for i in pairs]
    scores = [jnp.where(mask, s, NEGATIVE_FILL) for s in scores]
    tops = [jnp.max(s, axis=-1, keepdims=True) for s in scores]
    exps = [jnp.exp(s - top) for s, top in zip(scores, tops)]
    sums = [jnp.sum(e, axis=-1, keepdims=True) for e in exps]
    probs = [(e * (1.0 / total)).astype(BF) for e, total in zip(exps, sums)]
    outs = [mm(prob, kv[keys, pair_cols(i, D)]) for prob, i in zip(probs, pairs)]
    logs_all = stats[rows, :]
    for i, o, top, total in zip(pairs, outs, tops, sums):
        out[rows, pair_cols(i)] = unstacked(o).astype(BF)
        logs = top + jnp.log(total)
        logs_all = jnp.where(lane == base + 2 * i, logs[:SUB], logs_all)
        logs_all = jnp.where(lane == base + 2 * i + 1, logs[SUB:], logs_all)
    stats[rows, :] = logs_all


def attend_back(pairs, q, g, stats, base, rows, kv, mask, ks, wd, acc, dq):
    mask = jnp.concatenate([mask, mask])
    keys = pl.ds(ks, wd)
    logs = stats[rows, :]
    qs = [stacked(q[rows, pair_cols(i)]) for i in pairs]
    gs = [stacked(g[rows, pair_cols(i)]) for i in pairs]
    scores = [mm_nt(qi, kv[keys, pair_cols(i)]) for qi, i in zip(qs, pairs)]
    dps = [mm_nt(gi, kv[keys, pair_cols(i, D)]) for gi, i in zip(gs, pairs)]
    probs = [jnp.exp(jnp.where(mask, s, NEGATIVE_FILL) - head_col(logs, i, base)) for s, i in zip(scores, pairs)]
    sums = [jnp.sum(prob * dp, axis=-1, keepdims=True) for prob, dp in zip(probs, dps)]
    dss = [(prob * (dp - total)).astype(BF) for prob, dp, total in zip(probs, dps, sums)]
    for i, gi, prob in zip(pairs, gs, probs):
        acc[pair_cols(i, D), keys] += mm(gi.T, prob.astype(BF))
    for i, qi, ds in zip(pairs, qs, dss):
        acc[pair_cols(i), keys] += mm(qi.T, ds)
    for i, ds in zip(pairs, dss):
        dq[rows, pair_cols(i)] = (unstacked(mm(ds, kv[keys, pair_cols(i)])) * SCALE).astype(BF)


def each_sub(row0, body):
    @pl.loop(0, SUBS)
    def _(sub):
        body(sub, pl.ds(pl.multiple_of(sub * SUB, SUB), SUB), pl.multiple_of(row0 + sub * SUB, SUB))


def forward(
    widths, tab, xs, es, mk, wqkv, wso, wckv, wcq, gains, biases, kv, mkv, q, cq, att, catt, n0, stats
):
    b = pl.program_id(0)
    row0 = pl.multiple_of(tab[1, b], BLOCK)

    @pl.when(tab[2, b] == 1)
    def _():
        @pl.loop(0, kv.shape[1] // BLOCK)
        def _(i):
            rows = pl.ds(pl.multiple_of(i * BLOCK, BLOCK), BLOCK)
            kv[0, rows, :] = mm(xs[0, rows, :], wqkv[:, D:]).astype(BF)
            mkv[0, rows, :] = mm(es[0, rows, :], wckv[...]).astype(BF)

    x = xs[0, pl.ds(row0, BLOCK), :]
    q[...] = mm(x, wqkv[:, :D]).astype(BF) * jnp.asarray(SCALE, BF)
    stats[...] = jnp.zeros_like(stats)

    def self_block(sub, rows, at):
        meta = query_meta(mk, at)

        def run(pairs, ks, wd):
            mask = self_mask(mk, meta, at, ks, wd)
            attend(pairs, q, rows, kv.at[0], mask, ks, wd, att, stats, 0)

        by_width(tab[5, SUBS * b + sub], tab[4, SUBS * b + sub], widths, run)

    each_sub(row0, self_block)
    normed, inv = norm_stats(x.astype(F32) + mm(att[...], wso[...]))
    n0[...] = normed
    lane = lax.broadcasted_iota(jnp.int32, stats.shape, 1)
    stats[...] = jnp.where(lane == INV, inv, stats[...])
    first = normed * gains[0:1, :] + biases[0:1, :]
    cq[...] = mm(first.astype(BF), wcq[...]).astype(BF) * jnp.asarray(SCALE, BF)

    def cross_block(sub, rows, at):
        meta = query_meta(mk, at)

        def run(pairs, ks, wd):
            mask = cross_mask(mk, meta, at, ks, wd)
            attend(pairs, cq, rows, mkv.at[0], mask, ks, wd, catt, stats, CROSS)

        by_width(tab[7, SUBS * b + sub], tab[6, SUBS * b + sub], widths, run)

    each_sub(row0, cross_block)


def line_end(acc, inputs, weight, base, rows, gline, dwt):
    columns = 256

    @pl.loop(0, acc.shape[1] // columns)
    def _(i):
        cols = pl.ds(pl.multiple_of(i * columns, columns), columns)
        low = acc[:, cols].astype(BF)
        back = mm(weight[:, base:], low).T
        if rows is not None:
            back = back + rows[cols, :]
        gline[0, cols, :] = back.astype(BF)
        dwt[...] += mm(low, inputs[0, cols, :])


def cross_backward(
    widths, tab, es, mk, n0, stats, att, gsecond, gatt, cq, mkv, wckv, wso, wcq, params,
    gfirst, gself, eline, att_grad, norm_grad,
    acc, dq, dwckvt, dwcq, dwso, gb,
):
    b = pl.program_id(0)
    row0 = pl.multiple_of(tab[1, b], BLOCK)

    @pl.when(b == 0)
    def _():
        for ref in (dwckvt, dwcq, dwso, gb):
            ref[...] = jnp.zeros_like(ref)

    @pl.when(tab[2, b] == 1)
    def _():
        acc[...] = jnp.zeros_like(acc)

    def cross_block(sub, here, at):
        meta = query_meta(mk, at)

        def run(pairs, ks, wd):
            mask = cross_mask(mk, meta, at, ks, wd)
            attend_back(pairs, cq, gatt, stats, CROSS, here, mkv.at[0], mask, ks, wd, acc, dq)

        by_width(tab[7, SUBS * b + sub], tab[6, SUBS * b + sub], widths, run)

    each_sub(row0, cross_block)
    first = n0[...] * params[0:1, :] + params[3:4, :]
    dwcq[...] += mm(first.astype(BF).T, dq[...])
    gf = gsecond[...] + mm_nt(dq[...], wcq[...])
    gb[0] += fold8(gf * n0[...])
    gb[1] += fold8(gf)
    gf = norm_back(gf, n0[...], stats[:, INV : INV + 1], params[0:1, :])
    gfirst[...] = gf
    sg = gf.astype(BF)
    dwso[...] += mm(att[...].T, sg)
    gself[...] = mm_nt(sg, wso[...]).astype(BF)

    @pl.when(tab[3, b] == 1)
    def _():
        line_end(acc, es, wckv, 0, None, eline, dwckvt)

    @pl.when(b == pl.num_programs(0) - 1)
    def _():
        att_grad[: 2 * D, :] = dwckvt[...].astype(BF)
        att_grad[2 * D : 3 * D, :] = dwso[...].astype(BF)
        att_grad[3 * D :, :] = dwcq[...].astype(BF)
        sums = jnp.sum(gb[...], axis=1)
        none = jnp.zeros((2, D), F32)
        norm_grad[...] = jnp.concatenate([sums[0:1], none, sums[1:2], none, none])


def self_backward(widths, tab, xs, mk, stats, q, g, gf, kv, wqkv, sline, qkv_grad, acc, dq, rows, dwq, dwkvt):
    b = pl.program_id(0)
    row0 = pl.multiple_of(tab[1, b], BLOCK)

    @pl.when(b == 0)
    def _():
        dwq[...] = jnp.zeros_like(dwq)
        dwkvt[...] = jnp.zeros_like(dwkvt)

    @pl.when(tab[2, b] == 1)
    def _():
        acc[...] = jnp.zeros_like(acc)
        rows[...] = jnp.zeros_like(rows)

    def self_block(sub, here, at):
        meta = query_meta(mk, at)

        def run(pairs, ks, wd):
            mask = self_mask(mk, meta, at, ks, wd)
            attend_back(pairs, q, g, stats, 0, here, kv.at[0], mask, ks, wd, acc, dq)

        by_width(tab[5, SUBS * b + sub], tab[4, SUBS * b + sub], widths, run)

    each_sub(row0, self_block)
    own = pl.ds(row0, BLOCK)
    dwq[...] += mm(xs[0, own, :].T, dq[...])
    rows[own, :] = gf[...] + mm_nt(dq[...], wqkv[:, :D])

    @pl.when(tab[3, b] == 1)
    def _():
        line_end(acc, xs, wqkv, D, rows, sline, dwkvt)

    @pl.when(b == pl.num_programs(0) - 1)
    def _():
        qkv_grad[:D, :] = dwq[...].astype(BF)
        qkv_grad[D:, :] = dwkvt[...].astype(BF)


def const_spec(shape):
    return pl.BlockSpec(shape, lambda b, t: (0,) * len(shape), pipeline_mode=pl.Buffered(1))


def row_spec(cols):
    return pl.BlockSpec((BLOCK, cols), lambda b, t: (b, 0))


def line_spec(shape):
    return pl.BlockSpec((1,) + shape, lambda b, t: (t[0, b],) + (0,) * len(shape))


def sds(shape, dtype):
    return jax.ShapeDtypeStruct(shape, dtype)


def kernels(
    lines, n, tab, xs, es, cot, mk, self_qkv, self_out, cross_q, cross_kv, cross_out, weights, norm_gain, norm_bias
):
    slots, line_len = xs.shape[0], xs.shape[1]
    whole, p, k = plan(lines, n)
    rows_all = whole * line_len + k * line_len // p
    blocks = rows_all // BLOCK
    widths = widths_for(line_len)
    params = pltpu.CompilerParams(vmem_limit_bytes=VMEM, dimension_semantics=("arbitrary",))

    def call(kernel, name, ins, in_specs, outs, out_specs, scratch, flops):
        return pl.pallas_call(
            kernel,
            name=name,
            grid_spec=pltpu.PrefetchScalarGridSpec(
                num_scalar_prefetch=1,
                grid=(blocks,),
                in_specs=in_specs,
                out_specs=out_specs,
                scratch_shapes=scratch,
            ),
            out_shape=outs,
            compiler_params=params,
            cost_estimate=pl.CostEstimate(
                flops=int(flops), bytes_accessed=16 << 20, transcendentals=1 << 20
            ),
        )(tab, *ins)

    line2 = (line_len, 2 * D)
    rows_low, line_in, line_kv = sds((rows_all, D), BF), line_spec((line_len, D)), line_spec(line2)
    meta = line_spec((8, line_len))
    kv, mkv, q, cq, att, catt, n0, stats = call(
        functools.partial(forward, widths),
        "forward",
        (xs, es, mk, self_qkv, self_out, cross_kv, cross_q, norm_gain, norm_bias),
        [
            line_in, line_in, meta, const_spec((D, 3 * D)), const_spec((D, D)), const_spec((D, 2 * D)),
            const_spec((D, D)), const_spec((3, D)), const_spec((3, D)),
        ],
        (
            sds((slots,) + line2, BF), sds((slots,) + line2, BF), rows_low, rows_low, rows_low, rows_low,
            sds((rows_all, D), F32), sds((rows_all, 128), F32),
        ),
        (line_kv, line_kv) + (row_spec(D),) * 5 + (row_spec(128),),
        [],
        4e10,
    )

    out, gsecond, gatt, ffn_grad, co_grad, norm_a = feed(
        cot, n0, catt, cross_out, weights, norm_gain, norm_bias, lines, n, line_len
    )

    wide, tall, square = pltpu.VMEM((2 * D, line_len), F32), pltpu.VMEM((2 * D, D), F32), pltpu.VMEM((D, D), F32)
    low = pltpu.VMEM((BLOCK, D), BF)
    lines_low = sds((slots, line_len, D), BF)
    gfirst, gself, enc_line, att_grad, norm_b = call(
        functools.partial(cross_backward, widths),
        "cross_backward",
        (
            es, mk, n0, stats, att, gsecond, gatt, cq, mkv, cross_kv, self_out, cross_q,
            jnp.concatenate([norm_gain, norm_bias]),
        ),
        [line_in, meta, row_spec(D), row_spec(128)]
        + [row_spec(D)] * 4
        + [line_kv, const_spec((D, 2 * D)), const_spec((D, D)), const_spec((D, D)), const_spec((6, D))],
        (sds((rows_all, D), F32), rows_low, lines_low, sds((4 * D, D), BF), sds((8, D), F32)),
        (row_spec(D), row_spec(D), line_in, const_spec((4 * D, D)), const_spec((8, D))),
        [wide, low, tall, square, square, pltpu.VMEM((2, 8, D), F32)],
        3e10,
    )
    stream_line, qkv_grad = call(
        functools.partial(self_backward, widths),
        "self_backward",
        (xs, mk, stats, q, gself, gfirst, kv, self_qkv),
        [line_in, meta, row_spec(128)] + [row_spec(D)] * 3 + [line_kv, const_spec((D, 3 * D))],
        (lines_low, sds((3 * D, D), BF)),
        (line_in, const_spec((3 * D, D))),
        [wide, low, pltpu.VMEM((line_len, D), F32), square, tall],
        3e10,
    )
    return out, enc_line, stream_line, ffn_grad, att_grad, co_grad, qkv_grad, norm_a, norm_b


def remote(src, dst, send, recv, device):
    return pltpu.make_async_remote_copy(
        src_ref=src, dst_ref=dst, send_sem=send, recv_sem=recv, device_id={"seq": device},
        device_id_type=pl.DeviceIdType.MESH,
    )


def part_of(device, p):
    return (device % p + device // p) % p


class Exchange:
    def __init__(self, lines, n, line_len):
        self.n, self.piece = n, line_len // n
        self.whole, self.p, self.k = plan(lines, n)
        self.groups = n // self.p
        self.chunks = n // self.p
        self.part_len = line_len // self.p
        self.line_len = line_len
        self.shared0 = self.whole * n
        self.rows_p = self.k * self.part_len
        self.me = lax.axis_index("seq")
        self.group = self.me // self.p
        self.part = part_of(self.me, self.p)
        self.pos_part, self.pos_chunk = self.me // self.chunks, self.me % self.chunks

    def owner(self, group):
        return group * self.p + (self.pos_part + self.p * self.groups - group) % self.p


ROWS_AT, SHARES_AT = (-1, -1, 0, 5, 6), 1
FFN_LAG, NORM_LAG = 0, 1


class Dim:
    def __init__(self, axis, stride, size):
        self.axis, self.stride, self.size = axis, stride, size
        at = lax.axis_index(axis)
        self.index = at // stride % size
        self.rest = at - self.index * stride

    def peer(self, v):
        return (self.index + v) % self.size

    def device(self, v):
        return {self.axis: self.rest + self.peer(v) * self.stride}


def send_to(src, dst, sems, device):
    return pltpu.make_async_remote_copy(
        src_ref=src, dst_ref=dst, send_sem=sems[0], recv_sem=sems[1], device_id=device,
        device_id_type=pl.DeviceIdType.MESH,
    )


class Sems:
    def __init__(self, ref):
        self.ref, self.used = ref, 0

    def next(self):
        self.used += 1
        return self.ref.at[0, self.used - 1], self.ref.at[1, self.used - 1]


def mesh_dims(ex):
    return (
        Dim("dp", 1, 2), Dim("dp", 2, lax.axis_size("dp") // 2), Dim("seq", 1, ex.p), Dim("seq", ex.p, ex.groups),
    )


def greet(ex, core, yy):
    barrier = pltpu.get_barrier_semaphore()
    greeted = [{"seq": (ex.me + o) % ex.n} for o in range(1, ex.n)]
    greeted += [dim.device(v) for dim in (core, yy) for v in range(1, dim.size)]
    for device in greeted:
        pl.semaphore_signal(barrier, inc=1, device_id=device, device_id_type=pl.DeviceIdType.MESH)
    pl.semaphore_wait(barrier, len(greeted))


def start_all(copies):
    for copy in copies:
        copy.start()


def gather(dim, view, sems):
    copies = [send_to(view, view, sems.next(), dim.device(v)) for v in range(1, dim.size)]

    def finish():
        for copy in copies:
            copy.wait()

    return copies, finish


def in_kernel(
    ex, x_ref, rc_ref, e_ref, w_ref, xs, rc, es, weights, sem_w, sem_p, sem_f, sem_l, sem_g
):
    n, piece, w, k, me = ex.n, ex.piece, ex.whole, ex.k, ex.me
    core, yy, xx, zz = mesh_dims(ex)
    c, y, x, z = core.index, yy.index, xx.index, zz.index
    quarter = w_ref.shape[0] // (2 * yy.size)
    weights = weights.reshape(ex.groups, ex.p, yy.size, 2, quarter, w_ref.shape[1])
    own = pltpu.make_async_copy(
        w_ref.at[pl.ds(pl.multiple_of((y * 2 + c) * quarter, quarter), quarter)],
        weights.at[z, x, y, c], sem_l.at[3, 0],
    )
    own.start()
    greet(ex, core, yy)
    own.wait()
    sems = Sems(sem_g)
    stages = [
        gather(zz, weights.at[z, x, y, c], sems),
        gather(xx, weights.at[:, x, y, c], sems),
        gather(yy, weights.at[:, :, y, c], sems),
        gather(core, weights.at[:, :, :, c], sems),
    ]
    start_all(stages[0][0])

    def next_stage(i):
        stages[i][1]()
        if i + 1 < len(stages):
            start_all(stages[i + 1][0])

    spans = pl.ds(pl.multiple_of(me * piece, piece), piece)
    names = (x_ref, rc_ref, e_ref)

    def line_dst(out, slots):
        if out is rc:
            return rc.at[slots, me]
        return out.at[slots, spans]

    def whole_copies(a, o):
        to = (me + o) % n
        src = names[a]
        pairs = [(src.at[pl.ds(to * w, w)], line_dst((xs, rc, es)[a], pl.ds(k, w)))] if w else []
        return [
            remote(s, d, sem_w.at[0, a, i, o], sem_w.at[1, a, i, o], to)
            if o
            else pltpu.make_async_copy(s, d, sem_l.at[a, i])
            for i, (s, d) in enumerate(pairs)
        ]

    def shared_pairs(a, group):
        src = names[a]
        first = ex.shared0 + group * k
        return [(src.at[pl.ds(first, k)], line_dst((xs, rc, es)[a], pl.ds(0, k)))] if k else []

    def shared_send(a, u):
        group = (ex.group + u) % ex.groups
        to = ex.owner(group)
        return [
            remote(s, d, sem_p.at[0, a, i, u], sem_p.at[1, a, i, ex.pos_chunk], to)
            for i, (s, d) in enumerate(shared_pairs(a, group))
        ]

    def shared_local(a):
        return [
            pltpu.make_async_copy(s, d, sem_l.at[a, max(w, 1) + i])
            for i, (s, d) in enumerate(shared_pairs(a, ex.group))
        ]

    def shared_arrival(a, j):
        return [
            remote(s, d, sem_p.at[0, a, i, 0], sem_p.at[1, a, i, j], me)
            for i, (s, d) in enumerate(shared_pairs(a, ex.group))
        ]

    def forwards(a):
        out = (xs, rc, es)[a]
        mine = ex.part * ex.part_len
        if a == 1:
            view = rc.at[pl.ds(0, k), pl.ds(ex.part * ex.chunks, ex.chunks)]
        else:
            view = out.at[pl.ds(0, k), pl.ds(pl.multiple_of(mine, ex.part_len), ex.part_len)]
        return [
            remote(view, view, sem_f.at[0, a, v], sem_f.at[1, a, v], ex.group * ex.p + (me % ex.p + v) % ex.p)
            for v in range(1, ex.p)
        ]

    here = ex.pos_part == ex.part
    for a in range(3):
        for u in range(ex.groups if k else 0):
            if u == 0:

                @pl.when(here)
                def _():
                    for copy in shared_local(a):
                        copy.start()

                @pl.when(jnp.logical_not(here))
                def _():
                    for copy in shared_send(a, 0):
                        copy.start()

            else:
                for copy in shared_send(a, u):
                    copy.start()
        for o in range(n):
            for copy in whole_copies(a, o):
                copy.start()
    next_stage(0)
    for a in range(3):
        next_stage(a + 1)
        for j in range(ex.chunks if k else 0):
            own = ex.part * ex.chunks + j == me

            @pl.when(own)
            def _():
                for copy in shared_local(a):
                    copy.wait()

            @pl.when(jnp.logical_not(own))
            def _():
                for copy in shared_arrival(a, j):
                    copy.wait_recv()

        if k:
            for copy in forwards(a):
                copy.start()
    for a in range(3):
        for o in range(n):
            for copy in whole_copies(a, o):
                copy.wait()
        for u in range(ex.groups if k else 0):
            if u == 0:

                @pl.when(jnp.logical_not(here))
                def _():
                    for copy in shared_send(a, 0):
                        copy.wait_send()

            else:
                for copy in shared_send(a, u):
                    copy.wait_send()
        if k:
            for copy in forwards(a):
                copy.wait()


def feed_kernel(
    ex, cot_src, n0, catt, wco, wff, gains, biases,
    out, gsecond_out, gatt, ffn_grad, co_grad, norm_grad,
    cot, out_v, hid, gprime, dw1, dw2t, dwco, gb, sem_cs, sem_cw, sem_os, sem_ow,
):
    b, last = pl.program_id(0), pl.num_programs(0) - 1
    n, piece, w, k, me = ex.n, ex.piece, ex.whole, ex.k, ex.me

    def rows_at(row):
        return pl.ds(pl.multiple_of(row, piece), piece)

    def cot_copy(i, slot, row, sems, at, to):
        src, dst = cot_src.at[slot], cot.at[rows_at(row)]
        local = lambda: pltpu.make_async_copy(src, dst, sems.at[1, i, at])
        return local, lambda sent: send_to(src, dst, (sems.at[0, i, sent], sems.at[1, i, at]), {"seq": to})

    def cot_sends():
        for u in range(ex.groups if k else 0):
            group = (ex.group + u) % ex.groups
            to = ex.owner(group)
            for i in range(k):
                row = i * ex.part_len + ex.pos_chunk * piece
                local, far = cot_copy(i, ex.shared0 + group * k + i, row, sem_cs, ex.pos_chunk, to)
                yield to, local, functools.partial(far, u)
        for v in range(n):
            to = (me + v) % n
            for i in range(w):
                row = ex.rows_p + i * ex.line_len + me * piece
                local, far = cot_copy(i, to * w + i, row, sem_cw, me, to)
                yield to, local, functools.partial(far, v)

    def out_copy(row, slot, i, sems, sent, at, to):
        src, dst = out_v.at[rows_at(row)], out.at[slot]
        return (
            to,
            lambda: pltpu.make_async_copy(src, dst, sems.at[1, i, at]),
            lambda: send_to(src, dst, (sems.at[0, i, sent], sems.at[1, i, at]), {"seq": to}),
        )

    def out_shared(row):
        i, j = row // ex.part_len, row % ex.part_len // piece
        return out_copy(
            row, ex.shared0 + ex.group * k + i, i, sem_os, j, ex.group, ex.part * ex.chunks + j
        )

    def out_whole(row):
        at = row - ex.rows_p
        i, s = at // ex.line_len, at % ex.line_len // piece
        return out_copy(row, me * w + i, i, sem_ow, s, me, s)

    def either(to, here, there):
        @pl.when(to == me)
        def _():
            here()

        @pl.when(to != me)
        def _():
            there()

    @pl.when(b == 0)
    def _():
        for ref in (dw1, dw2t, dwco, gb):
            ref[...] = jnp.zeros_like(ref)
        core, yy = mesh_dims(ex)[:2]
        greet(ex, core, yy)
        for to, local, far in cot_sends():
            either(to, lambda: local().start(), lambda: far().start())

    first = n0[...] * gains[0:1, :] + biases[0:1, :]
    n1, s1 = norm_stats(first + mm(catt[...], wco[...]))
    second = n1 * gains[1:2, :] + biases[1:2, :]
    second_low = second.astype(BF)
    chunks, chunk = wff.shape[0], wff.shape[2]
    total = second
    for c in range(chunks):
        cols = slice(c * chunk, (c + 1) * chunk)
        v = mm(second_low, wff[c, :D, :])
        v2 = v * v
        t = jnp.tanh(GELU_C * (v + 0.044715 * (v2 * v)))
        half = 0.5 * (1.0 + t)
        h = (v * half).astype(BF)
        hid[:, cols] = h
        gprime[:, cols] = half + (0.5 * v) * (1.0 - t * t) * (GELU_C + (3 * 0.044715 * GELU_C) * v2)
        total = total + mm_nt(h, wff[c, D:, :])
    n2, s2 = norm_stats(total)
    here = pl.ds(pl.multiple_of(b * BLOCK, BLOCK), BLOCK)
    out_v[here, :] = (n2 * gains[2:3, :] + biases[2:3, :]).astype(BF)

    for q in range(BLOCK // piece):
        row = b * BLOCK + q * piece

        @pl.when(row < ex.rows_p)
        def _():
            i, j = row // ex.part_len, row % ex.part_len // piece
            local, far = cot_copy(i, 0, row, sem_cs, j, me)
            either(ex.part * ex.chunks + j, lambda: local().wait(), lambda: far(0).wait_recv())
            to, local, far = out_shared(row)
            either(to, lambda: local().start(), lambda: far().start())

        @pl.when(row >= ex.rows_p)
        def _():
            at = row - ex.rows_p
            i, s = at // ex.line_len, at % ex.line_len // piece
            local, far = cot_copy(i, 0, row, sem_cw, s, me)
            either(s, lambda: local().wait(), lambda: far(0).wait_recv())
            to, local, far = out_whole(row)
            either(to, lambda: local().start(), lambda: far().start())

    dy = cot[here, :].astype(F32)
    gb[1] += fold8(dy * n2)
    gb[3] += fold8(dy)
    gthird = norm_back(dy, n2, s2, gains[2:3, :])
    fg = gthird.astype(BF)
    fgt, sect = fg.T, second_low.T
    back = gthird
    for c in range(chunks):
        cols = slice(c * chunk, (c + 1) * chunk)
        pg = (mm(fg, wff[c, D:, :]) * gprime[:, cols]).astype(BF)
        dw2t[:, cols] += mm(fgt, hid[:, cols])
        dw1[:, cols] += mm(sect, pg)
        back = back + mm_nt(pg, wff[c, :D, :])
    gb[0] += fold8(back * n1)
    gb[2] += fold8(back)
    gsecond = norm_back(back, n1, s1, gains[1:2, :])
    gsecond_out[...] = gsecond
    cg = gsecond.astype(BF)
    dwco[...] += mm(catt[...].T, cg)
    gatt[...] = mm_nt(cg, wco[...]).astype(BF)

    @pl.when(b == last)
    def _():
        for c in range(chunks):
            cols = slice(c * chunk, (c + 1) * chunk)
            ffn_grad[c, :D, :] = dw1[:, cols].astype(BF)
            ffn_grad[c, D:, :] = dw2t[:, cols].astype(BF)
        co_grad[...] = dwco[...].astype(BF)
        sums = jnp.sum(gb[...], axis=1)
        none = jnp.zeros((1, D), F32)
        norm_grad[...] = jnp.concatenate([none, sums[:2], none, sums[2:], none, none])
        for to, local, far in cot_sends():
            either(to, lambda: None, lambda: far().wait_send())
        for row in range(0, ex.rows_p, piece):
            to, local, far = out_shared(row)
            either(to, lambda: local().wait(), lambda: far().wait_send())
        for row in range(ex.rows_p, cot.shape[0], piece):
            to, local, far = out_whole(row)
            either(to, lambda: local().wait(), lambda: far().wait_send())
        for i in range(k):
            for group in range(ex.groups):
                arrival = out_copy(0, ex.shared0 + group * k + i, i, sem_os, 0, group, me)[2]
                either(ex.owner(group), lambda: None, lambda: arrival().wait_recv())
        for i in range(w):
            for s in range(n):
                arrival = out_copy(0, s * w + i, i, sem_ow, 0, s, me)[2]
                either(s, lambda: None, lambda: arrival().wait_recv())


def feed(cot_src, n0, catt, wco, weights, gains, biases, lines, n, line_len):
    whole, p, k = plan(lines, n)
    most = max(k, whole, 1)
    rows_all, cols = n0.shape[0], weights.shape[2]
    ff = n * cols

    def kernel(*refs):
        feed_kernel(Exchange(lines, n, line_len), *refs)

    row = lambda c: pl.BlockSpec((BLOCK, c), lambda b: (b, 0))
    const = lambda *shape: pl.BlockSpec(shape, lambda b: (0,) * len(shape), pipeline_mode=pl.Buffered(1))
    hbm = pl.BlockSpec(memory_space=pl.ANY)
    dma = pltpu.SemaphoreType.DMA
    return pl.pallas_call(
        kernel,
        name="feed",
        grid=(rows_all // BLOCK,),
        in_specs=[hbm, row(D), row(D), const(D, D), const(n, 2 * D, cols), const(3, D), const(3, D)],
        out_specs=[hbm, row(D), row(D), const(n, 2 * D, cols), const(D, D), const(8, D)],
        out_shape=(
            sds((lines, line_len // n, D), BF),
            sds((rows_all, D), F32),
            sds((rows_all, D), BF),
            sds((n, 2 * D, cols), BF),
            sds((D, D), BF),
            sds((8, D), F32),
        ),
        scratch_shapes=[
            pltpu.VMEM((rows_all, D), BF),
            pltpu.VMEM((rows_all, D), BF),
            pltpu.VMEM((BLOCK, ff), BF),
            pltpu.VMEM((BLOCK, ff), F32),
            pltpu.VMEM((D, ff), F32),
            pltpu.VMEM((D, ff), F32),
            pltpu.VMEM((D, D), F32),
            pltpu.VMEM((4, 8, D), F32),
            dma((2, most, n)),
            dma((2, most, n)),
            dma((2, most, n)),
            dma((2, most, n)),
        ],
        compiler_params=pltpu.CompilerParams(
            collective_id=3, has_side_effects=True, vmem_limit_bytes=VMEM,
            dimension_semantics=("arbitrary",),
        ),
        cost_estimate=pl.CostEstimate(flops=int(4e10), bytes_accessed=16 << 20, transcendentals=1 << 20),
    )(cot_src, n0, catt, wco, weights, gains, biases)


def exchange_in(stream, rc, encoder, weights, lines, n, line_len, dp):
    whole, p, k = plan(lines, n)
    hops = 1 + dp // 2 - 1 + p - 1 + n // p - 1
    slots, piece = k + whole, line_len // n
    most = max(k, whole, 1)

    def kernel(*refs):
        in_kernel(Exchange(lines, n, line_len), *refs)

    dma = pltpu.SemaphoreType.DMA
    return pl.pallas_call(
        kernel,
        name="exchange_in",
        in_specs=[pl.BlockSpec(memory_space=pl.ANY)] * 4,
        out_specs=[pl.BlockSpec(memory_space=pl.ANY)] * 4,
        out_shape=(
            sds((slots, line_len, D), BF),
            sds((slots, n, 1, piece), jnp.int32),
            sds((slots, line_len, D), BF),
            sds((n,) + weights.shape, BF),
        ),
        scratch_shapes=[
            dma((2, 3, most, n)), dma((2, 3, most, n)), dma((2, 3, max(p, 2))), dma((4, 2 * most)),
            dma((2, hops)),
        ],
        compiler_params=pltpu.CompilerParams(collective_id=1, has_side_effects=True),
    )(stream, rc, encoder, weights)


def flat_loop(lead, run):
    @pl.loop(0, math.prod(lead))
    def _(i):
        index = []
        for size in reversed(lead):
            index.append(i % size)
            i = i // size
        run(tuple(reversed(index)))


def add_into(dst, sources, lead):
    def run(index):
        total = dst[index].astype(F32)
        for source in sources:
            total = total + source[index].astype(F32)
        dst[index] = total.astype(dst.dtype)

    flat_loop(lead, run)


def finish_kernel(
    ex, enc_line, stream_line, ffn_grad, att_grad, co_grad, qkv_grad, norm_a, norm_b,
    enc, stream, ffn, att, norms,
    ffn_v, att_v, norm_v, ffn_bufs, att_bufs, norm_bufs, own_v, part_v,
    sem_red, sem_w, sem_p, sem_l, sem_s, sem_in,
):
    n, piece, w, k, p, me = ex.n, ex.piece, ex.whole, ex.k, ex.p, ex.me
    core, yy, xx, zz = mesh_dims(ex)
    outer = yy.size

    loads = [
        pltpu.make_async_copy(ffn_grad, ffn_v, sem_in.at[0]),
        pltpu.make_async_copy(att_grad, att_v.at[pl.ds(0, 4 * D)], sem_in.at[1]),
        pltpu.make_async_copy(co_grad, att_v.at[pl.ds(4 * D, D)], sem_in.at[2]),
        pltpu.make_async_copy(qkv_grad, att_v.at[pl.ds(5 * D, 3 * D)], sem_in.at[3]),
    ]
    lines = (enc_line, stream_line)
    mine = pl.ds(pl.multiple_of(ex.part * ex.part_len, ex.part_len), ex.part_len)
    if k:
        loads += [
            pltpu.make_async_copy(lines[a].at[pl.ds(0, k), mine], own_v.at[a], sem_in.at[4 + a])
            for a in range(2)
        ]
    start_all(loads)
    norm_v[...] = norm_a[...] + norm_b[...]
    greet(ex, core, yy)

    fl = ffn_v.shape
    rows = fl[1] // (2 * outer)
    ffn_6 = ffn_v.reshape(ex.groups, p, outer, 2, rows, fl[2])
    att_rows = att_v.shape[0] // (2 * outer * n)
    att_6 = att_v.reshape(2, outer, p, ex.groups, att_rows, D)
    ffn_o = ffn.reshape(outer, 2, rows, fl[2])
    att_o = att.reshape(2, outer, p, ex.groups, att_rows, D)
    c, y, x, z = core.index, yy.index, xx.index, zz.index
    sems = Sems(sem_red)

    def scatter(dim, view, buf, lead):
        copies = [
            send_to(view(dim.peer(v)), buf.at[v - 1], sems.next(), dim.device(v)) for v in range(1, dim.size)
        ]

        def finish():
            for copy in copies:
                copy.wait()
            add_into(view(dim.index), [buf.at[v - 1] for v in range(1, dim.size)], lead)

        return copies, finish

    def place(src, dst, sem):
        copy = pltpu.make_async_copy(src, dst, sem)
        return [copy], copy.wait

    def exchange_all(dim, buf):
        copies = [send_to(norm_v, buf.at[v - 1], sems.next(), dim.device(v)) for v in range(1, dim.size)]

        def finish():
            for copy in copies:
                copy.wait()
            norm_v[...] = sum([buf[v - 1] for v in range(1, dim.size)], norm_v[...])

        return copies, finish

    g, o = ex.groups, outer

    def att_stream(h, half):
        r = pl.ds(h * half, half)
        bufs = [buf.at[..., r, :] for buf in att_bufs]
        return [
            scatter(core, lambda t: att_6.at[t, :, :, :, r], bufs[0], (o, p, g)),
            scatter(yy, lambda t: att_6.at[c, t, :, :, r], bufs[1], (p, g)),
            scatter(xx, lambda t: att_6.at[c, y, t, :, r], bufs[2], (g,)),
            scatter(zz, lambda t: att_6.at[c, y, x, t, r], bufs[3], ()),
            place(att_6.at[c, y, x, z, r], att_o.at[c, y, x, z, r], sem_in.at[7 + h]),
            gather(zz, att_o.at[c, y, x, z, r], sems),
            gather(xx, att_o.at[c, y, x, :, r], sems),
            gather(yy, att_o.at[c, y, :, :, r], sems),
            gather(core, att_o.at[c, :, :, :, r], sems),
        ]

    halves = 2 if att_rows % 32 == 0 else 1
    streams = [att_stream(h, att_rows // halves) for h in range(halves)]
    streams += [
        [
            scatter(core, lambda t: ffn_6.at[:, :, :, t], ffn_bufs[0], (g, p, o)),
            scatter(yy, lambda t: ffn_6.at[:, :, t, c], ffn_bufs[1], (g, p)),
            scatter(xx, lambda t: ffn_6.at[:, t, y, c], ffn_bufs[2], (g,)),
            scatter(zz, lambda t: ffn_6.at[t, x, y, c], ffn_bufs[3], ()),
            place(ffn_6.at[z, x, y, c], ffn_o.at[y, c], sem_in.at[6]),
            gather(yy, ffn_o.at[y, c], sems),
            gather(core, ffn_o.at[:, c], sems),
        ],
        [exchange_all(dim, norm_bufs[i]) for i, dim in enumerate((core, yy, xx, zz))],
    ]

    lags = [0] * halves + [FFN_LAG, NORM_LAG]

    def whole_src(a, i, to):
        return lines[a].at[k + i, pl.ds(pl.multiple_of(to * piece, piece), piece)]

    outs = (enc, stream)

    def whole_copies(a, v):
        to = (me + v) % n
        result = []
        for i in range(w):
            src, dst = whole_src(a, i, to), outs[a].at[me * w + i]
            result.append(
                send_to(src, dst, (sem_w.at[0, a, i, v], sem_w.at[1, a, i, v]), {"seq": to})
                if v
                else pltpu.make_async_copy(src, dst, sem_l.at[a, i])
            )
        return result

    def shared_pair(a, i, j):
        at = pl.ds(pl.multiple_of(j * piece, piece), piece)
        src = own_v.at[a, i, at]
        return src, outs[a].at[ex.shared0 + ex.group * k + i]

    def shared_copies(a, u):
        j = (ex.group + u) % ex.chunks
        to = ex.part * ex.chunks + j
        return to, [
            send_to(*shared_pair(a, i, j), (sem_p.at[0, a, i, u], sem_p.at[1, a, i, ex.group]), {"seq": to})
            for i in range(k)
        ]

    def local_copies(a):
        return [
            pltpu.make_async_copy(*shared_pair(a, i, ex.pos_chunk), sem_l.at[a, max(w, 1) + i])
            for i in range(k)
        ]

    def each_shared(a, remote_run, local_run):
        for u in range(ex.chunks if k else 0):
            to, copies = shared_copies(a, u)

            @pl.when(to != me)
            def _():
                for copy in copies:
                    remote_run(copy)

            @pl.when(to == me)
            def _():
                for copy in local_copies(a):
                    local_run(copy)

    def sharing(a, v):
        part = (ex.part + v) % p
        theirs = pl.ds(pl.multiple_of(part * ex.part_len, ex.part_len), ex.part_len)
        return send_to(
            lines[a].at[pl.ds(0, k), theirs], part_v.at[a, v - 1], (sem_s.at[0, a, v], sem_s.at[1, a, v]),
            xx.device(v),
        )

    for copy in loads:
        copy.wait()
    for stages in streams:
        start_all(stages[0][0])
    shares = [sharing(a, v) for a in range(2) for v in range(1, p)] if k else []
    start_all(shares)

    def start_whole(a, places):
        for v in places:
            start_all(whole_copies(a, v))

    def start_shared(a):
        each_shared(a, lambda copy: copy.start(), lambda copy: copy.start())

    batches = [
        lambda: start_whole(0, range(n)),
        lambda: start_whole(1, range(n // 2)),
        lambda: start_whole(1, range(n // 2, n)),
        lambda: start_shared(0),
        lambda: start_shared(1),
    ]

    def start_batches(step):
        for at, batch in zip(ROWS_AT, batches):
            if step == at:
                batch()

    start_batches(-1)
    for step in range(max(len(stages) + lag for stages, lag in zip(streams, lags))):
        for stages, lag in zip(streams, lags):
            stage = step - lag
            if 0 <= stage < len(stages):
                stages[stage][1]()
            if 0 <= stage < len(stages) - 1:
                start_all(stages[stage + 1][0])
        if step == SHARES_AT:
            for copy in shares:
                copy.wait()
            for a in range(2 if k else 0):
                add_into(own_v.at[a], [part_v.at[a, v - 1] for v in range(1, p)], (k,))
        start_batches(step)
    norms[...] = norm_v[...]
    for a in range(2):
        for v in range(n):
            for copy in whole_copies(a, v):
                copy.wait()
        each_shared(a, lambda copy: copy.wait_send(), lambda copy: copy.wait())
        for group in range(ex.groups if k else 0):

            @pl.when(ex.owner(group) != me)
            def _():
                for i in range(k):
                    sems = (sem_p.at[0, a, i, 0], sem_p.at[1, a, i, group])
                    send_to(*shared_pair(a, i, 0), sems, {"seq": me}).wait_recv()


def finish(arrays, lines, n, line_len, dp):
    whole, p, k = plan(lines, n)
    piece, most, groups, outer = line_len // n, max(k, whole, 1), n // p, dp // 2
    cols = arrays[2].shape[2]
    rows, att_rows = 2 * D // dp, 8 * D // (dp * n)
    part_len = line_len // p
    slots = max(k, 1)

    def kernel(*refs):
        refs = list(refs)
        grouped = refs[:16] + [refs[16:20], refs[20:24], refs[24:28]] + refs[28:]
        finish_kernel(Exchange(lines, n, line_len), *grouped)

    dma = pltpu.SemaphoreType.DMA
    hops = (1, outer - 1, p - 1, groups - 1)
    hbm = pl.BlockSpec(memory_space=pl.ANY)
    vmem = pl.BlockSpec(memory_space=pltpu.VMEM)
    at_least = lambda q: max(q, 1)
    return pl.pallas_call(
        kernel,
        name="finish",
        in_specs=[hbm] * 6 + [vmem] * 2,
        out_specs=[hbm] * 2 + [vmem] * 3,
        out_shape=[sds((lines, piece, D), BF)] * 2
        + [sds((2 * D, cols), BF), sds((8 * D, D), BF), sds((8, D), F32)],
        scratch_shapes=[
            pltpu.VMEM((n, 2 * D, cols), BF),
            pltpu.VMEM((8 * D, D), BF),
            pltpu.VMEM((8, D), F32),
            pltpu.VMEM((1, groups, p, outer, rows, cols), BF),
            pltpu.VMEM((at_least(outer - 1), groups, p, rows, cols), BF),
            pltpu.VMEM((at_least(p - 1), groups, rows, cols), BF),
            pltpu.VMEM((at_least(groups - 1), rows, cols), BF),
            pltpu.VMEM((1, outer, p, groups, att_rows, D), BF),
            pltpu.VMEM((at_least(outer - 1), p, groups, att_rows, D), BF),
            pltpu.VMEM((at_least(p - 1), groups, att_rows, D), BF),
            pltpu.VMEM((at_least(groups - 1), att_rows, D), BF),
            *[pltpu.VMEM((at_least(q), 8, D), F32) for q in hops],
            pltpu.VMEM((2, slots, part_len, D), BF),
            pltpu.VMEM((2, at_least(p - 1), slots, part_len, D), BF),
            dma((2, 7 * sum(hops))),
            dma((2, 2, most, n)),
            dma((2, 2, most, n)),
            dma((2, 2 * most)),
            dma((2, 2, max(p, 2))),
            dma((9,)),
        ],
        compiler_params=pltpu.CompilerParams(
            collective_id=2, has_side_effects=True, vmem_limit_bytes=VMEM
        ),
    )(*arrays)


def assemble_kernel(
    tab, out_in, enc_in, stream_in, att, ffn, norms,
    out, stream, enc, qkv, so, cq, ckv, co, ffn_in_grad, ffn_out_grad, gain, bias,
):
    i = pl.program_id(0)
    out[...] = out_in[...]
    stream[...] = stream_in[...].astype(F32)
    enc[...] = enc_in[...].astype(F32)
    plain = {2: so, 3: cq, 4: co, 5: qkv}
    turned = {0: ckv, 1: ckv, 6: qkv, 7: qkv}
    for step, ref in plain.items():

        @pl.when(i == step)
        def _(ref=ref):
            ref[...] = att[...].astype(F32)

    for step, ref in turned.items():

        @pl.when(i == step)
        def _(ref=ref):
            ref[...] = att[...].T.astype(F32)

    @pl.when(i == 8)
    def _():
        ffn_in_grad[...] = ffn[:D, :].astype(F32)
        ffn_out_grad[...] = ffn[D:, :].T.astype(F32)
        gain[...] = norms[:3, :]
        bias[...] = norms[3:6, :]


def assemble(slot_of, output, encoder_grad, stream_grad, att, ffn, norms):
    lines, piece = output.shape[:2]
    cols = ffn.shape[1]
    most = lines - 1
    line_in = pl.BlockSpec((1, piece, D), lambda i, t: (t[jnp.minimum(i, most)], 0, 0))
    line_out = pl.BlockSpec((1, piece, D), lambda i, t: (jnp.minimum(i, most), 0, 0))
    whole = lambda *shape: pl.BlockSpec(shape, lambda i, t: (0, 0), pipeline_mode=pl.Buffered(1))
    square = lambda at: pl.BlockSpec((D, D), lambda i, t: (0, at(i)))
    f32 = lambda *shape: sds(shape, F32)
    return pl.pallas_call(
        assemble_kernel,
        name="assemble",
        grid_spec=pltpu.PrefetchScalarGridSpec(
            num_scalar_prefetch=1,
            grid=(max(lines, 9),),
            in_specs=[
                line_in, line_in, line_in, pl.BlockSpec((D, D), lambda i, t: (jnp.minimum(i, 7), 0)),
                whole(2 * D, cols), whole(8, D),
            ],
            out_specs=[
                line_out, line_out, line_out,
                square(lambda i: jnp.clip(i - 5, 0, 2)),
                whole(D, D), whole(D, D),
                square(lambda i: jnp.minimum(i, 1)),
                whole(D, D), whole(D, cols), whole(cols, D), whole(3, D), whole(3, D),
            ],
        ),
        out_shape=[
            sds((lines, piece, D), BF), f32(lines, piece, D), f32(lines, piece, D), f32(D, 3 * D), f32(D, D),
            f32(D, D), f32(D, 2 * D), f32(D, D), f32(D, cols), f32(cols, D), f32(3, D), f32(3, D),
        ],
        compiler_params=pltpu.CompilerParams(
            vmem_limit_bytes=VMEM, dimension_semantics=("arbitrary",)
        ),
    )(slot_of, output, encoder_grad, stream_grad, att, ffn, norms)


def doc_numbers(bounds, places):
    return jnp.sum((bounds[:, None, :] <= places[None, :, None]).astype(jnp.int32), axis=2)


def body(
    stream, encoder, cotangent, self_qkv, self_out, cross_q, cross_kv, cross_out, ffn_in, ffn_out,
    norm_gain, norm_bias, lengths, enc_lengths, ranks, cuts,
):
    n = lax.axis_size("seq")
    me = lax.axis_index("seq")
    lines, piece = stream.shape[0], stream.shape[1]
    line_len = piece * n
    whole, p, k = plan(lines, n)
    groups = n // p
    slots = k + whole
    part_len = line_len // p
    rows_p, rows_w = k * part_len, whole * line_len
    rows_all = rows_p + rows_w
    ff = ffn_in.shape[1] * n
    group, part = me // p, part_of(me, p)
    widths = widths_for(line_len)
    i32 = jnp.int32

    cost = jnp.sum(lengths * lengths, axis=1)
    order = jnp.arange(lines, dtype=i32)
    lighter = (cost[None, :] < cost[:, None]) | (
        (cost[None, :] == cost[:, None]) & (order[None, :] < order[:, None])
    )
    rank = jnp.sum(lighter.astype(i32), axis=1)
    slot_of = jnp.where(rank < whole * n, rank, whole * n + lines - 1 - rank)
    line_of = jnp.sum(jnp.where(slot_of[None, :] == order[:, None], order[None, :], 0), axis=1)

    rc_in = (ranks * 32 + cuts)[line_of][:, None, :]
    shard = jnp.concatenate([ffn_in, ffn_out.T])
    cot = cotangent[line_of]
    xs, rc, es, weights = exchange_in(
        stream[line_of], rc_in, encoder[line_of], shard, lines, n, line_len, lax.axis_size("dp")
    )
    rc = rc.reshape(slots, line_len)
    own_slots = jnp.concatenate([whole * n + group * k + jnp.arange(k), me * whole + jnp.arange(whole)])
    mine = line_of[own_slots.astype(i32)]
    cum_t = jnp.cumsum(lengths[mine], axis=1)
    cum_e = jnp.cumsum(enc_lengths[mine], axis=1)
    places = jnp.arange(line_len, dtype=i32)
    doc = doc_numbers(cum_t, places)
    src = doc_numbers(cum_e, places)
    zero = jnp.zeros_like(rc)
    mk = jnp.stack([doc, rc // 32, rc % 32, src, zero, zero, zero, zero], axis=1).astype(F32)

    block_line = [j for j in range(k) for _ in range(part_len // BLOCK)]
    block_line += [k + j for j in range(whole) for _ in range(line_len // BLOCK)]
    block_row = [r * BLOCK for j in range(k) for r in range(part_len // BLOCK)]
    block_row += [r * BLOCK for j in range(whole) for r in range(line_len // BLOCK)]
    blocks = len(block_line)
    begin = [int(i == 0 or block_line[i] != block_line[i - 1]) for i in range(blocks)]
    end = [int(i == blocks - 1 or block_line[i] != block_line[i + 1]) for i in range(blocks)]
    per = SUBS
    bl = jnp.asarray(block_line, i32)
    br = jnp.asarray(block_row, i32) + jnp.where(bl < k, part * part_len, 0)
    sub_line = jnp.repeat(bl, per)
    sub_row = jnp.repeat(br, per) + jnp.tile(jnp.arange(per, dtype=i32) * SUB, blocks)
    ct, ce = cum_t[sub_line], cum_e[sub_line]
    before = ct <= sub_row[:, None]
    after = ct > sub_row[:, None] + (SUB - 1)

    def key_range(bounds):
        start = jnp.max(jnp.where(before, bounds, 0), axis=1)
        stop = jnp.min(jnp.where(after, bounds, line_len), axis=1)
        ks = start // ALIGN * ALIGN
        table = jnp.asarray([wd for wd, _ in widths], i32)
        var = jnp.sum((stop - ks)[:, None] > table[None, :], axis=1).astype(i32)
        wd = jnp.sum(jnp.where(var[:, None] == jnp.arange(len(widths)), table[None, :], 0), axis=1)
        return jnp.minimum(ks, line_len - wd), var

    sks, svar = key_range(ct)
    cks, cvar = key_range(ce)
    pad = jnp.zeros((blocks * (per - 1),), i32)
    wide = lambda v: jnp.concatenate([jnp.asarray(v, i32), pad])
    tab = jnp.stack([wide(bl), wide(br), wide(begin), wide(end), sks, svar, cks, cvar])

    output, *arrays = kernels(
        lines, n, tab, xs, es, cot, mk, self_qkv, self_out, cross_q, cross_kv, cross_out, weights, norm_gain, norm_bias
    )
    encoder_grad, stream_grad, ffn, att, norms = finish(
        arrays, lines, n, line_len, lax.axis_size("dp")
    )
    return tuple(assemble(slot_of.astype(i32), output, encoder_grad, stream_grad, att, ffn, norms))


def solution(mesh):
    lines = P("dp", "seq", None)
    in_specs = (
        lines, lines, lines, P(), P(), P(), P(), P(), P(None, "seq"), P("seq", None), P(), P(),
        P("dp", None), P("dp", None), P("dp", "seq"), P("dp", "seq"),
    )
    out_specs = (
        lines, lines, lines, P(), P(), P(), P(), P(), P(None, "seq"), P("seq", None), P(), P(),
    )
    return jax.shard_map(body, mesh=mesh, in_specs=in_specs, out_specs=out_specs, check_vma=False)
```

```python
import functools
import math

import jax
import jax.numpy as jnp
from jax import lax
from jax.experimental import pallas as pl
from jax.experimental.pallas import tpu as pltpu
from jax.sharding import PartitionSpec as P

D = 512
HEADS = 8
HEAD = 64
PAIR = 2 * HEAD
PAIRS = HEADS // 2
NEGATIVE_FILL = -1e30
EPSILON = 1e-05
SCALE = HEAD ** (-0.5)
BLOCK = 256
SUB = 256
ALIGN = 128
SUBS = BLOCK // SUB
CROSS, INV = HEADS, 2 * HEADS
BF = jnp.bfloat16
F32 = jnp.float32
NT = (((1,), (1,)), ((), ()))
GELU_C = math.sqrt(2.0 / math.pi)
VMEM = 60 * 1024 * 1024


def mm(left, right):
    return jnp.dot(left, right, preferred_element_type=F32)


def mm_nt(left, right):
    return lax.dot_general(left, right, NT, preferred_element_type=F32)


def plan(lines, n):
    whole = lines // n
    rest = lines - whole * n
    groups = math.gcd(rest, n) if rest else n
    return whole, n // groups, rest // groups


def widths_for(line_len):
    some = ((384, 4), (512, 4), (640, 4))
    return tuple(w for w in some if w[0] < line_len) + ((line_len, 2),)


def norm_stats(r):
    centred = r - jnp.mean(r, axis=-1, keepdims=True)
    inv = lax.rsqrt(jnp.mean(centred * centred, axis=-1, keepdims=True) + EPSILON)
    return centred * inv, inv


def norm_back(dy, normed, inv, gain):
    scaled = dy * gain
    inner = (
        scaled
        - jnp.mean(scaled, axis=-1, keepdims=True)
        - normed * jnp.mean(scaled * normed, axis=-1, keepdims=True)
    )
    return inner * inv


def fold8(t):
    return jnp.sum(t.reshape(t.shape[0] // 8, 8, t.shape[1]), axis=0)


def head_lanes(half):
    lane = lax.broadcasted_iota(jnp.int32, (1, PAIR), 1)
    return (lane < HEAD) if half == 0 else (lane >= HEAD)


def query_meta(mk, at):
    return mk[0, :, pl.ds(at, SUB)].T


def self_mask(mk, meta, at, ks, wd):
    doc = mk[0, 0:1, pl.ds(ks, wd)] == meta[:, 0:1]
    low = mk[0, 1:2, pl.ds(ks, wd)] < meta[:, 2:3]
    key = lax.broadcasted_iota(jnp.int32, (SUB, wd), 1) + ks
    query = lax.broadcasted_iota(jnp.int32, (SUB, wd), 0) + at
    return doc & (low | (key == query))


def cross_mask(mk, meta, at, ks, wd):
    return mk[0, 3:4, pl.ds(ks, wd)] == meta[:, 0:1]


def by_width(var, ks, widths, run):
    ks = pl.multiple_of(ks, ALIGN)
    for index, (wd, together) in enumerate(widths):

        @pl.when(var == index)
        def _(wd=wd, together=together):
            if together == PAIRS:
                run(tuple(range(PAIRS)), ks, wd)
            else:

                @pl.loop(0, PAIRS // together)
                def _(i):
                    run(tuple(i * together + j for j in range(together)), ks, wd)


def stacked(t):
    zero = jnp.zeros((), t.dtype)
    return jnp.concatenate([jnp.where(head_lanes(half), t, zero) for half in range(2)])


def unstacked(t):
    return jnp.where(head_lanes(0), t[:SUB], t[SUB:])


def pair_cols(pair, base=0):
    if isinstance(pair, int):
        return slice(base + pair * PAIR, base + (pair + 1) * PAIR)
    return pl.ds(pl.multiple_of(base + pair * PAIR, PAIR), PAIR)


def head_col(values, pair, base):
    head = base + 2 * pair
    if isinstance(pair, int):
        return jnp.concatenate([values[:, head : head + 1], values[:, head + 1 : head + 2]])
    lane = lax.broadcasted_iota(jnp.int32, values.shape, 1)
    pick = lambda at: jnp.sum(jnp.where(lane == at, values, 0.0), axis=-1, keepdims=True)
    return jnp.concatenate([pick(head), pick(head + 1)])


def attend(pairs, q, rows, kv, mask, ks, wd, out, stats, base):
    mask = jnp.concatenate([mask, mask])
    keys = pl.ds(ks, wd)
    lane = lax.broadcasted_iota(jnp.int32, (SUB, 128), 1)
    scores = [mm_nt(stacked(q[rows, pair_cols(i)]), kv[keys, pair_cols(i)]) for i in pairs]
    scores = [jnp.where(mask, s, NEGATIVE_FILL) for s in scores]
    tops = [jnp.max(s, axis=-1, keepdims=True) for s in scores]
    exps = [jnp.exp(s - top) for s, top in zip(scores, tops)]
    sums = [jnp.sum(e, axis=-1, keepdims=True) for e in exps]
    probs = [(e * (1.0 / total)).astype(BF) for e, total in zip(exps, sums)]
    outs = [mm(prob, kv[keys, pair_cols(i, D)]) for prob, i in zip(probs, pairs)]
    logs_all = stats[rows, :]
    for i, o, top, total in zip(pairs, outs, tops, sums):
        out[rows, pair_cols(i)] = unstacked(o).astype(BF)
        logs = top + jnp.log(total)
        logs_all = jnp.where(lane == base + 2 * i, logs[:SUB], logs_all)
        logs_all = jnp.where(lane == base + 2 * i + 1, logs[SUB:], logs_all)
    stats[rows, :] = logs_all


def attend_back(pairs, q, g, stats, base, rows, kv, mask, ks, wd, acc, dq):
    mask = jnp.concatenate([mask, mask])
    keys = pl.ds(ks, wd)
    logs = stats[rows, :]
    qs = [stacked(q[rows, pair_cols(i)]) for i in pairs]
    gs = [stacked(g[rows, pair_cols(i)]) for i in pairs]
    scores = [mm_nt(qi, kv[keys, pair_cols(i)]) for qi, i in zip(qs, pairs)]
    dps = [mm_nt(gi, kv[keys, pair_cols(i, D)]) for gi, i in zip(gs, pairs)]
    probs = [jnp.exp(jnp.where(mask, s, NEGATIVE_FILL) - head_col(logs, i, base)) for s, i in zip(scores, pairs)]
    sums = [jnp.sum(prob * dp, axis=-1, keepdims=True) for prob, dp in zip(probs, dps)]
    dss = [(prob * (dp - total)).astype(BF) for prob, dp, total in zip(probs, dps, sums)]
    for i, gi, prob in zip(pairs, gs, probs):
        acc[pair_cols(i, D), keys] += mm(gi.T, prob.astype(BF))
    for i, qi, ds in zip(pairs, qs, dss):
        acc[pair_cols(i), keys] += mm(qi.T, ds)
    for i, ds in zip(pairs, dss):
        dq[rows, pair_cols(i)] = (unstacked(mm(ds, kv[keys, pair_cols(i)])) * SCALE).astype(BF)


def each_sub(row0, body):
    @pl.loop(0, SUBS)
    def _(sub):
        body(sub, pl.ds(pl.multiple_of(sub * SUB, SUB), SUB), pl.multiple_of(row0 + sub * SUB, SUB))


def forward(
    widths, tab, xs, es, mk, wqkv, wso, wckv, wcq, gains, biases, kv, mkv, q, cq, att, catt, n0, stats
):
    b = pl.program_id(0)
    row0 = pl.multiple_of(tab[1, b], BLOCK)

    @pl.when(tab[2, b] == 1)
    def _():
        @pl.loop(0, kv.shape[1] // BLOCK)
        def _(i):
            rows = pl.ds(pl.multiple_of(i * BLOCK, BLOCK), BLOCK)
            kv[0, rows, :] = mm(xs[0, rows, :], wqkv[:, D:]).astype(BF)
            mkv[0, rows, :] = mm(es[0, rows, :], wckv[...]).astype(BF)

    x = xs[0, pl.ds(row0, BLOCK), :]
    q[...] = mm(x, wqkv[:, :D]).astype(BF) * jnp.asarray(SCALE, BF)
    stats[...] = jnp.zeros_like(stats)

    def self_block(sub, rows, at):
        meta = query_meta(mk, at)

        def run(pairs, ks, wd):
            mask = self_mask(mk, meta, at, ks, wd)
            attend(pairs, q, rows, kv.at[0], mask, ks, wd, att, stats, 0)

        by_width(tab[5, SUBS * b + sub], tab[4, SUBS * b + sub], widths, run)

    each_sub(row0, self_block)
    normed, inv = norm_stats(x.astype(F32) + mm(att[...], wso[...]))
    n0[...] = normed
    lane = lax.broadcasted_iota(jnp.int32, stats.shape, 1)
    stats[...] = jnp.where(lane == INV, inv, stats[...])
    first = normed * gains[0:1, :] + biases[0:1, :]
    cq[...] = mm(first.astype(BF), wcq[...]).astype(BF) * jnp.asarray(SCALE, BF)

    def cross_block(sub, rows, at):
        meta = query_meta(mk, at)

        def run(pairs, ks, wd):
            mask = cross_mask(mk, meta, at, ks, wd)
            attend(pairs, cq, rows, mkv.at[0], mask, ks, wd, catt, stats, CROSS)

        by_width(tab[7, SUBS * b + sub], tab[6, SUBS * b + sub], widths, run)

    each_sub(row0, cross_block)


def line_end(acc, inputs, weight, base, rows, gline, dwt):
    columns = 256

    @pl.loop(0, acc.shape[1] // columns)
    def _(i):
        cols = pl.ds(pl.multiple_of(i * columns, columns), columns)
        low = acc[:, cols].astype(BF)
        back = mm(weight[:, base:], low).T
        if rows is not None:
            back = back + rows[cols, :]
        gline[0, cols, :] = back.astype(BF)
        dwt[...] += mm(low, inputs[0, cols, :])


def cross_backward(
    widths, tab, es, mk, n0, stats, att, gsecond, gatt, cq, mkv, wckv, wso, wcq, params,
    gfirst, gself, eline, att_grad, norm_grad,
    acc, dq, dwckvt, dwcq, dwso, gb,
):
    b = pl.program_id(0)
    row0 = pl.multiple_of(tab[1, b], BLOCK)

    @pl.when(b == 0)
    def _():
        for ref in (dwckvt, dwcq, dwso, gb):
            ref[...] = jnp.zeros_like(ref)

    @pl.when(tab[2, b] == 1)
    def _():
        acc[...] = jnp.zeros_like(acc)

    def cross_block(sub, here, at):
        meta = query_meta(mk, at)

        def run(pairs, ks, wd):
            mask = cross_mask(mk, meta, at, ks, wd)
            attend_back(pairs, cq, gatt, stats, CROSS, here, mkv.at[0], mask, ks, wd, acc, dq)

        by_width(tab[7, SUBS * b + sub], tab[6, SUBS * b + sub], widths, run)

    each_sub(row0, cross_block)
    first = n0[...] * params[0:1, :] + params[3:4, :]
    dwcq[...] += mm(first.astype(BF).T, dq[...])
    gf = gsecond[...] + mm_nt(dq[...], wcq[...])
    gb[0] += fold8(gf * n0[...])
    gb[1] += fold8(gf)
    gf = norm_back(gf, n0[...], stats[:, INV : INV + 1], params[0:1, :])
    gfirst[...] = gf
    sg = gf.astype(BF)
    dwso[...] += mm(att[...].T, sg)
    gself[...] = mm_nt(sg, wso[...]).astype(BF)

    @pl.when(tab[3, b] == 1)
    def _():
        line_end(acc, es, wckv, 0, None, eline, dwckvt)

    @pl.when(b == pl.num_programs(0) - 1)
    def _():
        att_grad[: 2 * D, :] = dwckvt[...].astype(BF)
        att_grad[2 * D : 3 * D, :] = dwso[...].astype(BF)
        att_grad[3 * D :, :] = dwcq[...].astype(BF)
        sums = jnp.sum(gb[...], axis=1)
        none = jnp.zeros((2, D), F32)
        norm_grad[...] = jnp.concatenate([sums[0:1], none, sums[1:2], none, none])


def self_backward(widths, tab, xs, mk, stats, q, g, gf, kv, wqkv, sline, qkv_grad, acc, dq, rows, dwq, dwkvt):
    b = pl.program_id(0)
    row0 = pl.multiple_of(tab[1, b], BLOCK)

    @pl.when(b == 0)
    def _():
        dwq[...] = jnp.zeros_like(dwq)
        dwkvt[...] = jnp.zeros_like(dwkvt)

    @pl.when(tab[2, b] == 1)
    def _():
        acc[...] = jnp.zeros_like(acc)
        rows[...] = jnp.zeros_like(rows)

    def self_block(sub, here, at):
        meta = query_meta(mk, at)

        def run(pairs, ks, wd):
            mask = self_mask(mk, meta, at, ks, wd)
            attend_back(pairs, q, g, stats, 0, here, kv.at[0], mask, ks, wd, acc, dq)

        by_width(tab[5, SUBS * b + sub], tab[4, SUBS * b + sub], widths, run)

    each_sub(row0, self_block)
    own = pl.ds(row0, BLOCK)
    dwq[...] += mm(xs[0, own, :].T, dq[...])
    rows[own, :] = gf[...] + mm_nt(dq[...], wqkv[:, :D])

    @pl.when(tab[3, b] == 1)
    def _():
        line_end(acc, xs, wqkv, D, rows, sline, dwkvt)

    @pl.when(b == pl.num_programs(0) - 1)
    def _():
        qkv_grad[:D, :] = dwq[...].astype(BF)
        qkv_grad[D:, :] = dwkvt[...].astype(BF)


def const_spec(shape):
    return pl.BlockSpec(shape, lambda b, t: (0,) * len(shape), pipeline_mode=pl.Buffered(1))


def row_spec(cols):
    return pl.BlockSpec((BLOCK, cols), lambda b, t: (b, 0))


def line_spec(shape):
    return pl.BlockSpec((1,) + shape, lambda b, t: (t[0, b],) + (0,) * len(shape))


def sds(shape, dtype):
    return jax.ShapeDtypeStruct(shape, dtype)


def kernels(
    lines, n, tab, xs, es, cot, mk, self_qkv, self_out, cross_q, cross_kv, cross_out, weights, norm_gain, norm_bias
):
    slots, line_len = xs.shape[0], xs.shape[1]
    whole, p, k = plan(lines, n)
    rows_all = whole * line_len + k * line_len // p
    blocks = rows_all // BLOCK
    widths = widths_for(line_len)
    params = pltpu.CompilerParams(vmem_limit_bytes=VMEM, dimension_semantics=("arbitrary",))

    def call(kernel, name, ins, in_specs, outs, out_specs, scratch, flops):
        return pl.pallas_call(
            kernel,
            name=name,
            grid_spec=pltpu.PrefetchScalarGridSpec(
                num_scalar_prefetch=1,
                grid=(blocks,),
                in_specs=in_specs,
                out_specs=out_specs,
                scratch_shapes=scratch,
            ),
            out_shape=outs,
            compiler_params=params,
            cost_estimate=pl.CostEstimate(
                flops=int(flops), bytes_accessed=16 << 20, transcendentals=1 << 20
            ),
        )(tab, *ins)

    line2 = (line_len, 2 * D)
    rows_low, line_in, line_kv = sds((rows_all, D), BF), line_spec((line_len, D)), line_spec(line2)
    meta = line_spec((8, line_len))
    kv, mkv, q, cq, att, catt, n0, stats = call(
        functools.partial(forward, widths),
        "forward",
        (xs, es, mk, self_qkv, self_out, cross_kv, cross_q, norm_gain, norm_bias),
        [
            line_in, line_in, meta, const_spec((D, 3 * D)), const_spec((D, D)), const_spec((D, 2 * D)),
            const_spec((D, D)), const_spec((3, D)), const_spec((3, D)),
        ],
        (
            sds((slots,) + line2, BF), sds((slots,) + line2, BF), rows_low, rows_low, rows_low, rows_low,
            sds((rows_all, D), F32), sds((rows_all, 128), F32),
        ),
        (line_kv, line_kv) + (row_spec(D),) * 5 + (row_spec(128),),
        [],
        4e10,
    )

    out, gsecond, gatt, ffn_grad, co_grad, norm_a = feed(
        cot, n0, catt, cross_out, weights, norm_gain, norm_bias, lines, n, line_len
    )

    wide, tall, square = pltpu.VMEM((2 * D, line_len), F32), pltpu.VMEM((2 * D, D), F32), pltpu.VMEM((D, D), F32)
    low = pltpu.VMEM((BLOCK, D), BF)
    lines_low = sds((slots, line_len, D), BF)
    gfirst, gself, enc_line, att_grad, norm_b = call(
        functools.partial(cross_backward, widths),
        "cross_backward",
        (
            es, mk, n0, stats, att, gsecond, gatt, cq, mkv, cross_kv, self_out, cross_q,
            jnp.concatenate([norm_gain, norm_bias]),
        ),
        [line_in, meta, row_spec(D), row_spec(128)]
        + [row_spec(D)] * 4
        + [line_kv, const_spec((D, 2 * D)), const_spec((D, D)), const_spec((D, D)), const_spec((6, D))],
        (sds((rows_all, D), F32), rows_low, lines_low, sds((4 * D, D), BF), sds((8, D), F32)),
        (row_spec(D), row_spec(D), line_in, const_spec((4 * D, D)), const_spec((8, D))),
        [wide, low, tall, square, square, pltpu.VMEM((2, 8, D), F32)],
        3e10,
    )
    stream_line, qkv_grad = call(
        functools.partial(self_backward, widths),
        "self_backward",
        (xs, mk, stats, q, gself, gfirst, kv, self_qkv),
        [line_in, meta, row_spec(128)] + [row_spec(D)] * 3 + [line_kv, const_spec((D, 3 * D))],
        (lines_low, sds((3 * D, D), BF)),
        (line_in, const_spec((3 * D, D))),
        [wide, low, pltpu.VMEM((line_len, D), F32), square, tall],
        3e10,
    )
    return out, enc_line, stream_line, ffn_grad, att_grad, co_grad, qkv_grad, norm_a, norm_b


def remote(src, dst, send, recv, device):
    return pltpu.make_async_remote_copy(
        src_ref=src, dst_ref=dst, send_sem=send, recv_sem=recv, device_id={"seq": device},
        device_id_type=pl.DeviceIdType.MESH,
    )


def part_of(device, p):
    return (device % p + device // p) % p


class Exchange:
    def __init__(self, lines, n, line_len):
        self.n, self.piece = n, line_len // n
        self.whole, self.p, self.k = plan(lines, n)
        self.groups = n // self.p
        self.chunks = n // self.p
        self.part_len = line_len // self.p
        self.line_len = line_len
        self.shared0 = self.whole * n
        self.rows_p = self.k * self.part_len
        self.me = lax.axis_index("seq")
        self.group = self.me // self.p
        self.part = part_of(self.me, self.p)
        self.pos_part, self.pos_chunk = self.me // self.chunks, self.me % self.chunks

    def owner(self, group):
        return group * self.p + (self.pos_part + self.p * self.groups - group) % self.p


ROWS_AT, SHARES_AT = (-1, -1, 0, 5, 6), 1
FFN_LAG, NORM_LAG = 0, 1


class Dim:
    def __init__(self, axis, stride, size):
        self.axis, self.stride, self.size = axis, stride, size
        at = lax.axis_index(axis)
        self.index = at // stride % size
        self.rest = at - self.index * stride

    def peer(self, v):
        return (self.index + v) % self.size

    def device(self, v):
        return {self.axis: self.rest + self.peer(v) * self.stride}


def send_to(src, dst, sems, device):
    return pltpu.make_async_remote_copy(
        src_ref=src, dst_ref=dst, send_sem=sems[0], recv_sem=sems[1], device_id=device,
        device_id_type=pl.DeviceIdType.MESH,
    )


class Sems:
    def __init__(self, ref):
        self.ref, self.used = ref, 0

    def next(self):
        self.used += 1
        return self.ref.at[0, self.used - 1], self.ref.at[1, self.used - 1]


def mesh_dims(ex):
    return (
        Dim("dp", 1, 2), Dim("dp", 2, lax.axis_size("dp") // 2), Dim("seq", 1, ex.p), Dim("seq", ex.p, ex.groups),
    )


def greet(ex, *dims):
    barrier = pltpu.get_barrier_semaphore()
    greeted = [{"seq": (ex.me + o) % ex.n} for o in range(1, ex.n)]
    greeted += [dim.device(v) for dim in dims for v in range(1, dim.size)]
    for device in greeted:
        pl.semaphore_signal(barrier, inc=1, device_id=device, device_id_type=pl.DeviceIdType.MESH)
    pl.semaphore_wait(barrier, len(greeted))


def start_all(copies):
    for copy in copies:
        copy.start()


def gather(dim, view, sems):
    copies = [send_to(view, view, sems.next(), dim.device(v)) for v in range(1, dim.size)]

    def finish():
        for copy in copies:
            copy.wait()

    return copies, finish


def in_kernel(
    ex, x_ref, rc_ref, e_ref, w_ref, xs, rc, es, weights, sem_w, sem_p, sem_f, sem_l, sem_g
):
    n, piece, w, k, me = ex.n, ex.piece, ex.whole, ex.k, ex.me
    core, yy, xx, zz = mesh_dims(ex)
    c, y, x, z = core.index, yy.index, xx.index, zz.index
    quarter = w_ref.shape[0] // (2 * yy.size)
    weights = weights.reshape(ex.groups, ex.p, yy.size, 2, quarter, w_ref.shape[1])
    own = pltpu.make_async_copy(
        w_ref.at[pl.ds(pl.multiple_of((y * 2 + c) * quarter, quarter), quarter)],
        weights.at[z, x, y, c], sem_l.at[3, 0],
    )
    own.start()
    greet(ex, core, yy)
    own.wait()
    sems = Sems(sem_g)
    stages = [
        gather(zz, weights.at[z, x, y, c], sems),
        gather(xx, weights.at[:, x, y, c], sems),
        gather(yy, weights.at[:, :, y, c], sems),
        gather(core, weights.at[:, :, :, c], sems),
    ]
    start_all(stages[0][0])

    def next_stage(i):
        stages[i][1]()
        if i + 1 < len(stages):
            start_all(stages[i + 1][0])

    spans = pl.ds(pl.multiple_of(me * piece, piece), piece)
    names = (x_ref, rc_ref, e_ref)

    def line_dst(out, slots):
        if out is rc:
            return rc.at[slots, me]
        return out.at[slots, spans]

    def whole_copies(a, o):
        to = (me + o) % n
        src = names[a]
        pairs = [(src.at[pl.ds(to * w, w)], line_dst((xs, rc, es)[a], pl.ds(k, w)))] if w else []
        return [
            remote(s, d, sem_w.at[0, a, i, o], sem_w.at[1, a, i, o], to)
            if o
            else pltpu.make_async_copy(s, d, sem_l.at[a, i])
            for i, (s, d) in enumerate(pairs)
        ]

    def shared_pairs(a, group):
        src = names[a]
        first = ex.shared0 + group * k
        return [(src.at[pl.ds(first, k)], line_dst((xs, rc, es)[a], pl.ds(0, k)))] if k else []

    def shared_send(a, u):
        group = (ex.group + u) % ex.groups
        to = ex.owner(group)
        return [
            remote(s, d, sem_p.at[0, a, i, u], sem_p.at[1, a, i, ex.pos_chunk], to)
            for i, (s, d) in enumerate(shared_pairs(a, group))
        ]

    def shared_local(a):
        return [
            pltpu.make_async_copy(s, d, sem_l.at[a, max(w, 1) + i])
            for i, (s, d) in enumerate(shared_pairs(a, ex.group))
        ]

    def shared_arrival(a, j):
        return [
            remote(s, d, sem_p.at[0, a, i, 0], sem_p.at[1, a, i, j], me)
            for i, (s, d) in enumerate(shared_pairs(a, ex.group))
        ]

    def forwards(a):
        out = (xs, rc, es)[a]
        mine = ex.part * ex.part_len
        if a == 1:
            view = rc.at[pl.ds(0, k), pl.ds(ex.part * ex.chunks, ex.chunks)]
        else:
            view = out.at[pl.ds(0, k), pl.ds(pl.multiple_of(mine, ex.part_len), ex.part_len)]
        return [
            remote(view, view, sem_f.at[0, a, v], sem_f.at[1, a, v], ex.group * ex.p + (me % ex.p + v) % ex.p)
            for v in range(1, ex.p)
        ]

    here = ex.pos_part == ex.part
    for a in range(3):
        for u in range(ex.groups if k else 0):
            if u == 0:

                @pl.when(here)
                def _():
                    for copy in shared_local(a):
                        copy.start()

                @pl.when(jnp.logical_not(here))
                def _():
                    for copy in shared_send(a, 0):
                        copy.start()

            else:
                for copy in shared_send(a, u):
                    copy.start()
        for o in range(n):
            for copy in whole_copies(a, o):
                copy.start()
    next_stage(0)
    for a in range(3):
        next_stage(a + 1)
        for j in range(ex.chunks if k else 0):
            own = ex.part * ex.chunks + j == me

            @pl.when(own)
            def _():
                for copy in shared_local(a):
                    copy.wait()

            @pl.when(jnp.logical_not(own))
            def _():
                for copy in shared_arrival(a, j):
                    copy.wait_recv()

        if k:
            for copy in forwards(a):
                copy.start()
    for a in range(3):
        for o in range(n):
            for copy in whole_copies(a, o):
                copy.wait()
        for u in range(ex.groups if k else 0):
            if u == 0:

                @pl.when(jnp.logical_not(here))
                def _():
                    for copy in shared_send(a, 0):
                        copy.wait_send()

            else:
                for copy in shared_send(a, u):
                    copy.wait_send()
        if k:
            for copy in forwards(a):
                copy.wait()


def feed_kernel(
    ex, cot_src, n0, catt, wco, wff, gains, biases,
    out, gsecond_out, gatt, ffn_grad, co_grad, norm_grad,
    cot, out_v, hid, gprime, dw1, dw2t, dwco, gb, sem_cs, sem_cw, sem_os, sem_ow,
):
    b, last = pl.program_id(0), pl.num_programs(0) - 1
    n, piece, w, k, me = ex.n, ex.piece, ex.whole, ex.k, ex.me

    def rows_at(row):
        return pl.ds(pl.multiple_of(row, piece), piece)

    def cot_copy(i, slot, row, sems, at, to):
        src, dst = cot_src.at[slot], cot.at[rows_at(row)]
        local = lambda: pltpu.make_async_copy(src, dst, sems.at[1, i, at])
        return local, lambda sent: send_to(src, dst, (sems.at[0, i, sent], sems.at[1, i, at]), {"seq": to})

    def cot_sends():
        for u in range(ex.groups if k else 0):
            group = (ex.group + u) % ex.groups
            to = ex.owner(group)
            for i in range(k):
                row = i * ex.part_len + ex.pos_chunk * piece
                local, far = cot_copy(i, ex.shared0 + group * k + i, row, sem_cs, ex.pos_chunk, to)
                yield to, local, functools.partial(far, u)
        for v in range(n):
            to = (me + v) % n
            for i in range(w):
                row = ex.rows_p + i * ex.line_len + me * piece
                local, far = cot_copy(i, to * w + i, row, sem_cw, me, to)
                yield to, local, functools.partial(far, v)

    def out_copy(row, slot, i, sems, sent, at, to):
        src, dst = out_v.at[rows_at(row)], out.at[slot]
        return (
            to,
            lambda: pltpu.make_async_copy(src, dst, sems.at[1, i, at]),
            lambda: send_to(src, dst, (sems.at[0, i, sent], sems.at[1, i, at]), {"seq": to}),
        )

    def out_shared(row):
        i, j = row // ex.part_len, row % ex.part_len // piece
        return out_copy(
            row, ex.shared0 + ex.group * k + i, i, sem_os, j, ex.group, ex.part * ex.chunks + j
        )

    def out_whole(row):
        at = row - ex.rows_p
        i, s = at // ex.line_len, at % ex.line_len // piece
        return out_copy(row, me * w + i, i, sem_ow, s, me, s)

    def either(to, here, there):
        @pl.when(to == me)
        def _():
            here()

        @pl.when(to != me)
        def _():
            there()

    @pl.when(b == 0)
    def _():
        for ref in (dw1, dw2t, dwco, gb):
            ref[...] = jnp.zeros_like(ref)
        greet(ex)
        for to, local, far in cot_sends():
            either(to, lambda: local().start(), lambda: far().start())

    first = n0[...] * gains[0:1, :] + biases[0:1, :]
    n1, s1 = norm_stats(first + mm(catt[...], wco[...]))
    second = n1 * gains[1:2, :] + biases[1:2, :]
    second_low = second.astype(BF)
    chunks, chunk = wff.shape[0], wff.shape[2]
    total = second
    for c in range(chunks):
        cols = slice(c * chunk, (c + 1) * chunk)
        v = mm(second_low, wff[c, :D, :])
        v2 = v * v
        t = jnp.tanh(GELU_C * (v + 0.044715 * (v2 * v)))
        half = 0.5 * (1.0 + t)
        h = (v * half).astype(BF)
        hid[:, cols] = h
        gprime[:, cols] = half + (0.5 * v) * (1.0 - t * t) * (GELU_C + (3 * 0.044715 * GELU_C) * v2)
        total = total + mm_nt(h, wff[c, D:, :])
    n2, s2 = norm_stats(total)
    here = pl.ds(pl.multiple_of(b * BLOCK, BLOCK), BLOCK)
    out_v[here, :] = (n2 * gains[2:3, :] + biases[2:3, :]).astype(BF)

    for q in range(BLOCK // piece):
        row = b * BLOCK + q * piece

        @pl.when(row < ex.rows_p)
        def _():
            i, j = row // ex.part_len, row % ex.part_len // piece
            local, far = cot_copy(i, 0, row, sem_cs, j, me)
            either(ex.part * ex.chunks + j, lambda: local().wait(), lambda: far(0).wait_recv())
            to, local, far = out_shared(row)
            either(to, lambda: local().start(), lambda: far().start())

        @pl.when(row >= ex.rows_p)
        def _():
            at = row - ex.rows_p
            i, s = at // ex.line_len, at % ex.line_len // piece
            local, far = cot_copy(i, 0, row, sem_cw, s, me)
            either(s, lambda: local().wait(), lambda: far(0).wait_recv())
            to, local, far = out_whole(row)
            either(to, lambda: local().start(), lambda: far().start())

    dy = cot[here, :].astype(F32)
    gb[1] += fold8(dy * n2)
    gb[3] += fold8(dy)
    gthird = norm_back(dy, n2, s2, gains[2:3, :])
    fg = gthird.astype(BF)
    fgt, sect = fg.T, second_low.T
    back = gthird
    for c in range(chunks):
        cols = slice(c * chunk, (c + 1) * chunk)
        pg = (mm(fg, wff[c, D:, :]) * gprime[:, cols]).astype(BF)
        dw2t[:, cols] += mm(fgt, hid[:, cols])
        dw1[:, cols] += mm(sect, pg)
        back = back + mm_nt(pg, wff[c, :D, :])
    gb[0] += fold8(back * n1)
    gb[2] += fold8(back)
    gsecond = norm_back(back, n1, s1, gains[1:2, :])
    gsecond_out[...] = gsecond
    cg = gsecond.astype(BF)
    dwco[...] += mm(catt[...].T, cg)
    gatt[...] = mm_nt(cg, wco[...]).astype(BF)

    @pl.when(b == last)
    def _():
        for c in range(chunks):
            cols = slice(c * chunk, (c + 1) * chunk)
            ffn_grad[c, :D, :] = dw1[:, cols].astype(BF)
            ffn_grad[c, D:, :] = dw2t[:, cols].astype(BF)
        co_grad[...] = dwco[...].astype(BF)
        sums = jnp.sum(gb[...], axis=1)
        none = jnp.zeros((1, D), F32)
        norm_grad[...] = jnp.concatenate([none, sums[:2], none, sums[2:], none, none])
        for to, local, far in cot_sends():
            either(to, lambda: None, lambda: far().wait_send())
        for row in range(0, ex.rows_p, piece):
            to, local, far = out_shared(row)
            either(to, lambda: local().wait(), lambda: far().wait_send())
        for row in range(ex.rows_p, cot.shape[0], piece):
            to, local, far = out_whole(row)
            either(to, lambda: local().wait(), lambda: far().wait_send())
        for i in range(k):
            for group in range(ex.groups):
                arrival = out_copy(0, ex.shared0 + group * k + i, i, sem_os, 0, group, me)[2]
                either(ex.owner(group), lambda: None, lambda: arrival().wait_recv())
        for i in range(w):
            for s in range(n):
                arrival = out_copy(0, s * w + i, i, sem_ow, 0, s, me)[2]
                either(s, lambda: None, lambda: arrival().wait_recv())


def feed(cot_src, n0, catt, wco, weights, gains, biases, lines, n, line_len):
    whole, p, k = plan(lines, n)
    most = max(k, whole, 1)
    rows_all, cols = n0.shape[0], weights.shape[2]
    ff = n * cols

    def kernel(*refs):
        feed_kernel(Exchange(lines, n, line_len), *refs)

    row = lambda c: pl.BlockSpec((BLOCK, c), lambda b: (b, 0))
    const = lambda *shape: pl.BlockSpec(shape, lambda b: (0,) * len(shape), pipeline_mode=pl.Buffered(1))
    hbm = pl.BlockSpec(memory_space=pl.ANY)
    dma = pltpu.SemaphoreType.DMA
    return pl.pallas_call(
        kernel,
        name="feed",
        grid=(rows_all // BLOCK,),
        in_specs=[hbm, row(D), row(D), const(D, D), const(n, 2 * D, cols), const(3, D), const(3, D)],
        out_specs=[hbm, row(D), row(D), const(n, 2 * D, cols), const(D, D), const(8, D)],
        out_shape=(
            sds((lines, line_len // n, D), BF),
            sds((rows_all, D), F32),
            sds((rows_all, D), BF),
            sds((n, 2 * D, cols), BF),
            sds((D, D), BF),
            sds((8, D), F32),
        ),
        scratch_shapes=[
            pltpu.VMEM((rows_all, D), BF),
            pltpu.VMEM((rows_all, D), BF),
            pltpu.VMEM((BLOCK, ff), BF),
            pltpu.VMEM((BLOCK, ff), F32),
            pltpu.VMEM((D, ff), F32),
            pltpu.VMEM((D, ff), F32),
            pltpu.VMEM((D, D), F32),
            pltpu.VMEM((4, 8, D), F32),
            dma((2, most, n)),
            dma((2, most, n)),
            dma((2, most, n)),
            dma((2, most, n)),
        ],
        compiler_params=pltpu.CompilerParams(
            collective_id=3, has_side_effects=True, vmem_limit_bytes=VMEM,
            dimension_semantics=("arbitrary",),
        ),
        cost_estimate=pl.CostEstimate(flops=int(4e10), bytes_accessed=16 << 20, transcendentals=1 << 20),
    )(cot_src, n0, catt, wco, weights, gains, biases)


def exchange_in(stream, rc, encoder, weights, lines, n, line_len, dp):
    whole, p, k = plan(lines, n)
    hops = 1 + dp // 2 - 1 + p - 1 + n // p - 1
    slots, piece = k + whole, line_len // n
    most = max(k, whole, 1)

    def kernel(*refs):
        in_kernel(Exchange(lines, n, line_len), *refs)

    dma = pltpu.SemaphoreType.DMA
    return pl.pallas_call(
        kernel,
        name="exchange_in",
        in_specs=[pl.BlockSpec(memory_space=pl.ANY)] * 4,
        out_specs=[pl.BlockSpec(memory_space=pl.ANY)] * 4,
        out_shape=(
            sds((slots, line_len, D), BF),
            sds((slots, n, 1, piece), jnp.int32),
            sds((slots, line_len, D), BF),
            sds((n,) + weights.shape, BF),
        ),
        scratch_shapes=[
            dma((2, 3, most, n)), dma((2, 3, most, n)), dma((2, 3, max(p, 2))), dma((4, 2 * most)),
            dma((2, hops)),
        ],
        compiler_params=pltpu.CompilerParams(collective_id=1, has_side_effects=True),
    )(stream, rc, encoder, weights)


def flat_loop(lead, run):
    @pl.loop(0, math.prod(lead))
    def _(i):
        index = []
        for size in reversed(lead):
            index.append(i % size)
            i = i // size
        run(tuple(reversed(index)))


def add_into(dst, sources, lead):
    def run(index):
        total = dst[index].astype(F32)
        for source in sources:
            total = total + source[index].astype(F32)
        dst[index] = total.astype(dst.dtype)

    flat_loop(lead, run)


def finish_kernel(
    ex, enc_line, stream_line, ffn_grad, att_grad, co_grad, qkv_grad, norm_a, norm_b,
    enc, stream, ffn, att, norms,
    ffn_v, att_v, norm_v, ffn_bufs, att_bufs, norm_bufs, own_v, part_v,
    sem_red, sem_w, sem_p, sem_l, sem_s, sem_in,
):
    n, piece, w, k, p, me = ex.n, ex.piece, ex.whole, ex.k, ex.p, ex.me
    core, yy, xx, zz = mesh_dims(ex)
    outer = yy.size

    loads = [
        pltpu.make_async_copy(ffn_grad, ffn_v, sem_in.at[0]),
        pltpu.make_async_copy(att_grad, att_v.at[pl.ds(0, 4 * D)], sem_in.at[1]),
        pltpu.make_async_copy(co_grad, att_v.at[pl.ds(4 * D, D)], sem_in.at[2]),
        pltpu.make_async_copy(qkv_grad, att_v.at[pl.ds(5 * D, 3 * D)], sem_in.at[3]),
    ]
    lines = (enc_line, stream_line)
    mine = pl.ds(pl.multiple_of(ex.part * ex.part_len, ex.part_len), ex.part_len)
    if k:
        loads += [
            pltpu.make_async_copy(lines[a].at[pl.ds(0, k), mine], own_v.at[a], sem_in.at[4 + a])
            for a in range(2)
        ]
    start_all(loads)
    norm_v[...] = norm_a[...] + norm_b[...]
    greet(ex, core, yy)

    fl = ffn_v.shape
    rows = fl[1] // (2 * outer)
    ffn_6 = ffn_v.reshape(ex.groups, p, outer, 2, rows, fl[2])
    att_rows = att_v.shape[0] // (2 * outer * n)
    att_6 = att_v.reshape(2, outer, p, ex.groups, att_rows, D)
    ffn_o = ffn.reshape(outer, 2, rows, fl[2])
    att_o = att.reshape(2, outer, p, ex.groups, att_rows, D)
    c, y, x, z = core.index, yy.index, xx.index, zz.index
    sems = Sems(sem_red)

    def scatter(dim, view, buf, lead):
        copies = [
            send_to(view(dim.peer(v)), buf.at[v - 1], sems.next(), dim.device(v)) for v in range(1, dim.size)
        ]

        def finish():
            for copy in copies:
                copy.wait()
            add_into(view(dim.index), [buf.at[v - 1] for v in range(1, dim.size)], lead)

        return copies, finish

    def place(src, dst, sem):
        copy = pltpu.make_async_copy(src, dst, sem)
        return [copy], copy.wait

    def exchange_all(dim, buf):
        copies = [send_to(norm_v, buf.at[v - 1], sems.next(), dim.device(v)) for v in range(1, dim.size)]

        def finish():
            for copy in copies:
                copy.wait()
            norm_v[...] = sum([buf[v - 1] for v in range(1, dim.size)], norm_v[...])

        return copies, finish

    g, o = ex.groups, outer

    def att_stream(h, half):
        r = pl.ds(h * half, half)
        bufs = [buf.at[..., r, :] for buf in att_bufs]
        return [
            scatter(core, lambda t: att_6.at[t, :, :, :, r], bufs[0], (o, p, g)),
            scatter(yy, lambda t: att_6.at[c, t, :, :, r], bufs[1], (p, g)),
            scatter(xx, lambda t: att_6.at[c, y, t, :, r], bufs[2], (g,)),
            scatter(zz, lambda t: att_6.at[c, y, x, t, r], bufs[3], ()),
            place(att_6.at[c, y, x, z, r], att_o.at[c, y, x, z, r], sem_in.at[7 + h]),
            gather(zz, att_o.at[c, y, x, z, r], sems),
            gather(xx, att_o.at[c, y, x, :, r], sems),
            gather(yy, att_o.at[c, y, :, :, r], sems),
            gather(core, att_o.at[c, :, :, :, r], sems),
        ]

    halves = 2 if att_rows % 32 == 0 else 1
    streams = [att_stream(h, att_rows // halves) for h in range(halves)]
    streams += [
        [
            scatter(core, lambda t: ffn_6.at[:, :, :, t], ffn_bufs[0], (g, p, o)),
            scatter(yy, lambda t: ffn_6.at[:, :, t, c], ffn_bufs[1], (g, p)),
            scatter(xx, lambda t: ffn_6.at[:, t, y, c], ffn_bufs[2], (g,)),
            scatter(zz, lambda t: ffn_6.at[t, x, y, c], ffn_bufs[3], ()),
            place(ffn_6.at[z, x, y, c], ffn_o.at[y, c], sem_in.at[6]),
            gather(yy, ffn_o.at[y, c], sems),
            gather(core, ffn_o.at[:, c], sems),
        ],
        [exchange_all(dim, norm_bufs[i]) for i, dim in enumerate((core, yy, xx, zz))],
    ]

    lags = [0] * halves + [FFN_LAG, NORM_LAG]

    def whole_src(a, i, to):
        return lines[a].at[k + i, pl.ds(pl.multiple_of(to * piece, piece), piece)]

    outs = (enc, stream)

    def whole_copies(a, v):
        to = (me + v) % n
        result = []
        for i in range(w):
            src, dst = whole_src(a, i, to), outs[a].at[me * w + i]
            result.append(
                send_to(src, dst, (sem_w.at[0, a, i, v], sem_w.at[1, a, i, v]), {"seq": to})
                if v
                else pltpu.make_async_copy(src, dst, sem_l.at[a, i])
            )
        return result

    def shared_pair(a, i, j):
        at = pl.ds(pl.multiple_of(j * piece, piece), piece)
        src = own_v.at[a, i, at]
        return src, outs[a].at[ex.shared0 + ex.group * k + i]

    def shared_copies(a, u):
        j = (ex.group + u) % ex.chunks
        to = ex.part * ex.chunks + j
        return to, [
            send_to(*shared_pair(a, i, j), (sem_p.at[0, a, i, u], sem_p.at[1, a, i, ex.group]), {"seq": to})
            for i in range(k)
        ]

    def local_copies(a):
        return [
            pltpu.make_async_copy(*shared_pair(a, i, ex.pos_chunk), sem_l.at[a, max(w, 1) + i])
            for i in range(k)
        ]

    def each_shared(a, remote_run, local_run):
        for u in range(ex.chunks if k else 0):
            to, copies = shared_copies(a, u)

            @pl.when(to != me)
            def _():
                for copy in copies:
                    remote_run(copy)

            @pl.when(to == me)
            def _():
                for copy in local_copies(a):
                    local_run(copy)

    def sharing(a, v):
        part = (ex.part + v) % p
        theirs = pl.ds(pl.multiple_of(part * ex.part_len, ex.part_len), ex.part_len)
        return send_to(
            lines[a].at[pl.ds(0, k), theirs], part_v.at[a, v - 1], (sem_s.at[0, a, v], sem_s.at[1, a, v]),
            xx.device(v),
        )

    for copy in loads:
        copy.wait()
    for stages in streams:
        start_all(stages[0][0])
    shares = [sharing(a, v) for a in range(2) for v in range(1, p)] if k else []
    start_all(shares)

    def start_whole(a, places):
        for v in places:
            start_all(whole_copies(a, v))

    def start_shared(a):
        each_shared(a, lambda copy: copy.start(), lambda copy: copy.start())

    batches = [
        lambda: start_whole(0, range(n)),
        lambda: start_whole(1, range(n // 2)),
        lambda: start_whole(1, range(n // 2, n)),
        lambda: start_shared(0),
        lambda: start_shared(1),
    ]

    def start_batches(step):
        for at, batch in zip(ROWS_AT, batches):
            if step == at:
                batch()

    start_batches(-1)
    for step in range(max(len(stages) + lag for stages, lag in zip(streams, lags))):
        for stages, lag in zip(streams, lags):
            stage = step - lag
            if 0 <= stage < len(stages):
                stages[stage][1]()
            if 0 <= stage < len(stages) - 1:
                start_all(stages[stage + 1][0])
        if step == SHARES_AT:
            for copy in shares:
                copy.wait()
            for a in range(2 if k else 0):
                add_into(own_v.at[a], [part_v.at[a, v - 1] for v in range(1, p)], (k,))
        start_batches(step)
    norms[...] = norm_v[...]
    for a in range(2):
        for v in range(n):
            for copy in whole_copies(a, v):
                copy.wait()
        each_shared(a, lambda copy: copy.wait_send(), lambda copy: copy.wait())
        for group in range(ex.groups if k else 0):

            @pl.when(ex.owner(group) != me)
            def _():
                for i in range(k):
                    sems = (sem_p.at[0, a, i, 0], sem_p.at[1, a, i, group])
                    send_to(*shared_pair(a, i, 0), sems, {"seq": me}).wait_recv()


def finish(arrays, lines, n, line_len, dp):
    whole, p, k = plan(lines, n)
    piece, most, groups, outer = line_len // n, max(k, whole, 1), n // p, dp // 2
    cols = arrays[2].shape[2]
    rows, att_rows = 2 * D // dp, 8 * D // (dp * n)
    part_len = line_len // p
    slots = max(k, 1)

    def kernel(*refs):
        refs = list(refs)
        grouped = refs[:16] + [refs[16:20], refs[20:24], refs[24:28]] + refs[28:]
        finish_kernel(Exchange(lines, n, line_len), *grouped)

    dma = pltpu.SemaphoreType.DMA
    hops = (1, outer - 1, p - 1, groups - 1)
    hbm = pl.BlockSpec(memory_space=pl.ANY)
    vmem = pl.BlockSpec(memory_space=pltpu.VMEM)
    at_least = lambda q: max(q, 1)
    return pl.pallas_call(
        kernel,
        name="finish",
        in_specs=[hbm] * 6 + [vmem] * 2,
        out_specs=[hbm] * 2 + [vmem] * 3,
        out_shape=[sds((lines, piece, D), BF)] * 2
        + [sds((2 * D, cols), BF), sds((8 * D, D), BF), sds((8, D), F32)],
        scratch_shapes=[
            pltpu.VMEM((n, 2 * D, cols), BF),
            pltpu.VMEM((8 * D, D), BF),
            pltpu.VMEM((8, D), F32),
            pltpu.VMEM((1, groups, p, outer, rows, cols), BF),
            pltpu.VMEM((at_least(outer - 1), groups, p, rows, cols), BF),
            pltpu.VMEM((at_least(p - 1), groups, rows, cols), BF),
            pltpu.VMEM((at_least(groups - 1), rows, cols), BF),
            pltpu.VMEM((1, outer, p, groups, att_rows, D), BF),
            pltpu.VMEM((at_least(outer - 1), p, groups, att_rows, D), BF),
            pltpu.VMEM((at_least(p - 1), groups, att_rows, D), BF),
            pltpu.VMEM((at_least(groups - 1), att_rows, D), BF),
            *[pltpu.VMEM((at_least(q), 8, D), F32) for q in hops],
            pltpu.VMEM((2, slots, part_len, D), BF),
            pltpu.VMEM((2, at_least(p - 1), slots, part_len, D), BF),
            dma((2, 7 * sum(hops))),
            dma((2, 2, most, n)),
            dma((2, 2, most, n)),
            dma((2, 2 * most)),
            dma((2, 2, max(p, 2))),
            dma((9,)),
        ],
        compiler_params=pltpu.CompilerParams(
            collective_id=2, has_side_effects=True, vmem_limit_bytes=VMEM
        ),
    )(*arrays)


def assemble_kernel(
    tab, out_in, enc_in, stream_in, att, ffn, norms,
    out, stream, enc, qkv, so, cq, ckv, co, ffn_in_grad, ffn_out_grad, gain, bias,
):
    i = pl.program_id(0)
    out[...] = out_in[...]
    stream[...] = stream_in[...].astype(F32)
    enc[...] = enc_in[...].astype(F32)
    plain = {2: so, 3: cq, 4: co, 5: qkv}
    turned = {0: ckv, 1: ckv, 6: qkv, 7: qkv}
    for step, ref in plain.items():

        @pl.when(i == step)
        def _(ref=ref):
            ref[...] = att[...].astype(F32)

    for step, ref in turned.items():

        @pl.when(i == step)
        def _(ref=ref):
            ref[...] = att[...].T.astype(F32)

    @pl.when(i == 8)
    def _():
        ffn_in_grad[...] = ffn[:D, :].astype(F32)
        ffn_out_grad[...] = ffn[D:, :].T.astype(F32)
        gain[...] = norms[:3, :]
        bias[...] = norms[3:6, :]


def assemble(slot_of, output, encoder_grad, stream_grad, att, ffn, norms):
    lines, piece = output.shape[:2]
    cols = ffn.shape[1]
    most = lines - 1
    line_in = pl.BlockSpec((1, piece, D), lambda i, t: (t[jnp.minimum(i, most)], 0, 0))
    line_out = pl.BlockSpec((1, piece, D), lambda i, t: (jnp.minimum(i, most), 0, 0))
    whole = lambda *shape: pl.BlockSpec(shape, lambda i, t: (0, 0), pipeline_mode=pl.Buffered(1))
    square = lambda at: pl.BlockSpec((D, D), lambda i, t: (0, at(i)))
    f32 = lambda *shape: sds(shape, F32)
    return pl.pallas_call(
        assemble_kernel,
        name="assemble",
        grid_spec=pltpu.PrefetchScalarGridSpec(
            num_scalar_prefetch=1,
            grid=(max(lines, 9),),
            in_specs=[
                line_in, line_in, line_in, pl.BlockSpec((D, D), lambda i, t: (jnp.minimum(i, 7), 0)),
                whole(2 * D, cols), whole(8, D),
            ],
            out_specs=[
                line_out, line_out, line_out,
                square(lambda i: jnp.clip(i - 5, 0, 2)),
                whole(D, D), whole(D, D),
                square(lambda i: jnp.minimum(i, 1)),
                whole(D, D), whole(D, cols), whole(cols, D), whole(3, D), whole(3, D),
            ],
        ),
        out_shape=[
            sds((lines, piece, D), BF), f32(lines, piece, D), f32(lines, piece, D), f32(D, 3 * D), f32(D, D),
            f32(D, D), f32(D, 2 * D), f32(D, D), f32(D, cols), f32(cols, D), f32(3, D), f32(3, D),
        ],
        compiler_params=pltpu.CompilerParams(
            vmem_limit_bytes=VMEM, dimension_semantics=("arbitrary",)
        ),
    )(slot_of, output, encoder_grad, stream_grad, att, ffn, norms)


def tables_kernel(lines, n, line_len, me_ref, len_ref, enc_ref, order, tab, docs):
    whole, p, k = plan(lines, n)
    part_len, slots, half = line_len // p, whole + k, 4
    widths = [wd for wd, _ in widths_for(line_len)]
    me = me_ref[0]
    group, part = me // p, part_of(me, p)
    size = (lines + 7) // 8 * 8
    fill = jnp.zeros((size - lines, len_ref.shape[1]), F32)
    pad = (lambda t: jnp.concatenate([t, fill])) if size > lines else (lambda t: t)
    target, source = pad(len_ref[...].astype(F32)), pad(enc_ref[...].astype(F32))

    row = lax.broadcasted_iota(jnp.int32, (size, 128), 0).astype(F32)
    lane = lax.broadcasted_iota(jnp.int32, (size, 128), 1).astype(F32)
    cost = jnp.broadcast_to(jnp.sum(target * target, axis=-1, keepdims=True), (size, 128))
    own = row == lane
    cost_lane = jnp.sum(jnp.where(own, cost, 0.0), axis=0, keepdims=True)
    lighter = (cost_lane < cost) | ((cost_lane == cost) & (lane < row))
    rank = jnp.sum(jnp.where(lighter & (lane < lines), 1.0, 0.0), axis=-1, keepdims=True)
    slot = jnp.where(rank < whole * n, rank, whole * n + lines - 1.0 - rank)
    slot = jnp.broadcast_to(slot, (size, 128))
    real = row < lines
    line_of = jnp.sum(jnp.where((slot == lane) & real, row, 0.0), axis=0, keepdims=True)
    slot_of = jnp.sum(jnp.where(own & real, slot, 0.0), axis=0, keepdims=True)
    order[...] = jnp.concatenate([line_of, slot_of, jnp.zeros((6, 128), F32)]).astype(jnp.int32)

    def lengths_of(table, j):
        at = whole * n + group * k + j if j < k else me * whole + (j - k)
        return jnp.sum(jnp.where((slot == at.astype(F32)) & real, table, 0.0), axis=0, keepdims=True)

    none = [jnp.zeros((1, 128), F32)] * (half - slots)
    sums = jnp.concatenate(
        [lengths_of(target, j) for j in range(slots)] + none + [lengths_of(source, j) for j in range(slots)] + none
    )
    lane8 = lax.broadcasted_iota(jnp.int32, (8, 128), 1)
    shift = 1
    while shift < 128:
        sums = sums + jnp.where(lane8 >= shift, pltpu.roll(sums, shift, 1), 0.0)
        shift *= 2
    columns = sums.T
    places = lax.broadcasted_iota(jnp.int32, (1, line_len), 1).astype(F32)
    zero = jnp.zeros((1, line_len), F32)
    for j in range(slots):
        count = lambda at: jnp.sum(
            jnp.where(columns[:, at : at + 1] <= places, 1.0, 0.0), axis=0, keepdims=True
        )
        docs[j] = jnp.concatenate([count(j), zero, zero, count(half + j), zero, zero, zero, zero])

    block_line = [j for j in range(k) for _ in range(part_len // BLOCK)]
    block_line += [k + j for j in range(whole) for _ in range(line_len // BLOCK)]
    block_row = [r * BLOCK for j in range(k) for r in range(part_len // BLOCK)]
    block_row += [r * BLOCK for j in range(whole) for r in range(line_len // BLOCK)]
    blocks = len(block_line)
    lane1 = lax.broadcasted_iota(jnp.int32, (1, 128), 1)
    rows = [jnp.zeros((1, 128), F32)] * 8
    for b in range(blocks):
        j = block_line[b]
        first = (jnp.int32(block_row[b]) + (part * part_len if j < k else 0)).astype(F32)
        bounds = sums[j : j + 1]
        before, after = bounds <= first, bounds > first + (BLOCK - 1.0)

        def key_range(ends):
            start = jnp.max(jnp.where(before, ends, 0.0), axis=-1, keepdims=True)
            stop = jnp.min(jnp.where(after, ends, float(line_len)), axis=-1, keepdims=True)
            ks = jnp.floor(start * (1.0 / ALIGN)) * ALIGN
            var, wd = jnp.zeros_like(ks), jnp.full_like(ks, widths[0])
            for at, width in enumerate(widths[:-1]):
                wider = stop - ks > width
                var = jnp.where(wider, at + 1.0, var)
                wd = jnp.where(wider, float(widths[at + 1]), wd)
            return jnp.minimum(ks, line_len - wd), var

        values = [
            float(j), first, float(b == 0 or block_line[b - 1] != j),
            float(b == blocks - 1 or block_line[b + 1] != j),
            *key_range(bounds), *key_range(sums[half + j : half + j + 1]),
        ]
        rows = [jnp.where(lane1 == b, value, r) for r, value in zip(rows, values)]
    tab[...] = jnp.concatenate(rows).astype(jnp.int32)


def tables(me, lengths, enc_lengths, lines, n, line_len):
    whole, _, k = plan(lines, n)
    vmem = pl.BlockSpec(memory_space=pltpu.VMEM)
    return pl.pallas_call(
        functools.partial(tables_kernel, lines, n, line_len),
        name="tables",
        in_specs=[pl.BlockSpec(memory_space=pltpu.SMEM), vmem, vmem],
        out_specs=[vmem] * 3,
        out_shape=[
            sds((8, 128), jnp.int32), sds((8, 128), jnp.int32), sds((whole + k, 8, line_len), F32),
        ],
    )(me.reshape(1).astype(jnp.int32), lengths, enc_lengths)


def body(
    stream, encoder, cotangent, self_qkv, self_out, cross_q, cross_kv, cross_out, ffn_in, ffn_out,
    norm_gain, norm_bias, lengths, enc_lengths, ranks, cuts,
):
    n = lax.axis_size("seq")
    lines, piece = stream.shape[0], stream.shape[1]
    line_len = piece * n
    order, tab, docs = tables(lax.axis_index("seq"), lengths, enc_lengths, lines, n, line_len)
    line_of, slot_of = order[0, :lines], order[1, :lines]

    rc_in = (ranks * 32 + cuts)[line_of][:, None, :]
    shard = jnp.concatenate([ffn_in, ffn_out.T])
    cot = cotangent[line_of]
    xs, rc, es, weights = exchange_in(
        stream[line_of], rc_in, encoder[line_of], shard, lines, n, line_len, lax.axis_size("dp")
    )
    rc = rc.reshape(rc.shape[0], 1, line_len)
    row = jnp.arange(8)[None, :, None]
    mk = jnp.where(row == 1, (rc // 32).astype(F32), jnp.where(row == 2, (rc % 32).astype(F32), docs))

    output, *arrays = kernels(
        lines, n, tab, xs, es, cot, mk, self_qkv, self_out, cross_q, cross_kv, cross_out, weights, norm_gain, norm_bias
    )
    encoder_grad, stream_grad, ffn, att, norms = finish(
        arrays, lines, n, line_len, lax.axis_size("dp")
    )
    return tuple(assemble(slot_of, output, encoder_grad, stream_grad, att, ffn, norms))


def solution(mesh):
    lines = P("dp", "seq", None)
    in_specs = (
        lines, lines, lines, P(), P(), P(), P(), P(), P(None, "seq"), P("seq", None), P(), P(),
        P("dp", None), P("dp", None), P("dp", "seq"), P("dp", "seq"),
    )
    out_specs = (
        lines, lines, lines, P(), P(), P(), P(), P(), P(None, "seq"), P("seq", None), P(), P(),
    )
    return jax.shard_map(body, mesh=mesh, in_specs=in_specs, out_specs=out_specs, check_vma=False)
```

```python
import functools
import math

import jax
import jax.numpy as jnp
from jax import lax
from jax.experimental import pallas as pl
from jax.experimental.pallas import tpu as pltpu
from jax.sharding import PartitionSpec as P

D = 512
HEADS = 8
HEAD = 64
PAIR = 2 * HEAD
PAIRS = HEADS // 2
NEGATIVE_FILL = -1e30
EPSILON = 1e-05
SCALE = HEAD ** (-0.5)
BLOCK = 256
SUB = 256
ALIGN = 128
SUBS = BLOCK // SUB
CROSS, INV = HEADS, 2 * HEADS
BF = jnp.bfloat16
F32 = jnp.float32
NT = (((1,), (1,)), ((), ()))
GELU_C = math.sqrt(2.0 / math.pi)
VMEM = 60 * 1024 * 1024


def mm(left, right):
    return jnp.dot(left, right, preferred_element_type=F32)


def mm_nt(left, right):
    return lax.dot_general(left, right, NT, preferred_element_type=F32)


def plan(lines, n):
    whole = lines // n
    rest = lines - whole * n
    groups = math.gcd(rest, n) if rest else n
    return whole, n // groups, rest // groups


def widths_for(line_len):
    some = ((384, 4), (512, 4), (640, 4))
    return tuple(w for w in some if w[0] < line_len) + ((line_len, 2),)


def norm_stats(r):
    centred = r - jnp.mean(r, axis=-1, keepdims=True)
    inv = lax.rsqrt(jnp.mean(centred * centred, axis=-1, keepdims=True) + EPSILON)
    return centred * inv, inv


def norm_back(dy, normed, inv, gain):
    scaled = dy * gain
    inner = (
        scaled
        - jnp.mean(scaled, axis=-1, keepdims=True)
        - normed * jnp.mean(scaled * normed, axis=-1, keepdims=True)
    )
    return inner * inv


def fold8(t):
    return jnp.sum(t.reshape(t.shape[0] // 8, 8, t.shape[1]), axis=0)


def head_lanes(half):
    lane = lax.broadcasted_iota(jnp.int32, (1, PAIR), 1)
    return (lane < HEAD) if half == 0 else (lane >= HEAD)


def query_meta(mk, at):
    return mk[0, :, pl.ds(at, SUB)].T


def self_mask(mk, meta, at, ks, wd):
    doc = mk[0, 0:1, pl.ds(ks, wd)] == meta[:, 0:1]
    low = mk[0, 1:2, pl.ds(ks, wd)] < meta[:, 2:3]
    key = lax.broadcasted_iota(jnp.int32, (SUB, wd), 1) + ks
    query = lax.broadcasted_iota(jnp.int32, (SUB, wd), 0) + at
    return doc & (low | (key == query))


def cross_mask(mk, meta, at, ks, wd):
    return mk[0, 3:4, pl.ds(ks, wd)] == meta[:, 0:1]


def by_width(var, ks, widths, run):
    ks = pl.multiple_of(ks, ALIGN)
    for index, (wd, together) in enumerate(widths):

        @pl.when(var == index)
        def _(wd=wd, together=together):
            if together == PAIRS:
                run(tuple(range(PAIRS)), ks, wd)
            else:

                @pl.loop(0, PAIRS // together)
                def _(i):
                    run(tuple(i * together + j for j in range(together)), ks, wd)


def stacked(t):
    zero = jnp.zeros((), t.dtype)
    return jnp.concatenate([jnp.where(head_lanes(half), t, zero) for half in range(2)])


def unstacked(t):
    return jnp.where(head_lanes(0), t[:SUB], t[SUB:])


def pair_cols(pair, base=0):
    if isinstance(pair, int):
        return slice(base + pair * PAIR, base + (pair + 1) * PAIR)
    return pl.ds(pl.multiple_of(base + pair * PAIR, PAIR), PAIR)


def head_col(values, pair, base):
    head = base + 2 * pair
    if isinstance(pair, int):
        return jnp.concatenate([values[:, head : head + 1], values[:, head + 1 : head + 2]])
    lane = lax.broadcasted_iota(jnp.int32, values.shape, 1)
    pick = lambda at: jnp.sum(jnp.where(lane == at, values, 0.0), axis=-1, keepdims=True)
    return jnp.concatenate([pick(head), pick(head + 1)])


def attend(pairs, q, rows, kv, mask, ks, wd, out, stats, base):
    mask = jnp.concatenate([mask, mask])
    keys = pl.ds(ks, wd)
    lane = lax.broadcasted_iota(jnp.int32, (SUB, 128), 1)
    scores = [mm_nt(stacked(q[rows, pair_cols(i)]), kv[keys, pair_cols(i)]) for i in pairs]
    scores = [jnp.where(mask, s, NEGATIVE_FILL) for s in scores]
    tops = [jnp.max(s, axis=-1, keepdims=True) for s in scores]
    exps = [jnp.exp(s - top) for s, top in zip(scores, tops)]
    sums = [jnp.sum(e, axis=-1, keepdims=True) for e in exps]
    probs = [(e * (1.0 / total)).astype(BF) for e, total in zip(exps, sums)]
    outs = [mm(prob, kv[keys, pair_cols(i, D)]) for prob, i in zip(probs, pairs)]
    logs_all = stats[rows, :]
    for i, o, top, total in zip(pairs, outs, tops, sums):
        out[rows, pair_cols(i)] = unstacked(o).astype(BF)
        logs = top + jnp.log(total)
        logs_all = jnp.where(lane == base + 2 * i, logs[:SUB], logs_all)
        logs_all = jnp.where(lane == base + 2 * i + 1, logs[SUB:], logs_all)
    stats[rows, :] = logs_all


def attend_back(pairs, q, g, stats, base, rows, kv, mask, ks, wd, acc, dq):
    mask = jnp.concatenate([mask, mask])
    keys = pl.ds(ks, wd)
    logs = stats[rows, :]
    qs = [stacked(q[rows, pair_cols(i)]) for i in pairs]
    gs = [stacked(g[rows, pair_cols(i)]) for i in pairs]
    scores = [mm_nt(qi, kv[keys, pair_cols(i)]) for qi, i in zip(qs, pairs)]
    dps = [mm_nt(gi, kv[keys, pair_cols(i, D)]) for gi, i in zip(gs, pairs)]
    probs = [jnp.exp(jnp.where(mask, s, NEGATIVE_FILL) - head_col(logs, i, base)) for s, i in zip(scores, pairs)]
    sums = [jnp.sum(prob * dp, axis=-1, keepdims=True) for prob, dp in zip(probs, dps)]
    dss = [(prob * (dp - total)).astype(BF) for prob, dp, total in zip(probs, dps, sums)]
    for i, gi, prob in zip(pairs, gs, probs):
        acc[pair_cols(i, D), keys] += mm(gi.T, prob.astype(BF))
    for i, qi, ds in zip(pairs, qs, dss):
        acc[pair_cols(i), keys] += mm(qi.T, ds)
    for i, ds in zip(pairs, dss):
        dq[rows, pair_cols(i)] = (unstacked(mm(ds, kv[keys, pair_cols(i)])) * SCALE).astype(BF)


def each_sub(row0, body):
    @pl.loop(0, SUBS)
    def _(sub):
        body(sub, pl.ds(pl.multiple_of(sub * SUB, SUB), SUB), pl.multiple_of(row0 + sub * SUB, SUB))


def forward(
    widths, tab, xs, es, mk, wqkv, wso, wckv, wcq, gains, biases, kv, mkv, q, cq, att, catt, n0, stats
):
    b = pl.program_id(0)
    row0 = pl.multiple_of(tab[1, b], BLOCK)

    @pl.when(tab[2, b] == 1)
    def _():
        @pl.loop(0, kv.shape[1] // BLOCK)
        def _(i):
            rows = pl.ds(pl.multiple_of(i * BLOCK, BLOCK), BLOCK)
            kv[0, rows, :] = mm(xs[0, rows, :], wqkv[:, D:]).astype(BF)
            mkv[0, rows, :] = mm(es[0, rows, :], wckv[...]).astype(BF)

    x = xs[0, pl.ds(row0, BLOCK), :]
    q[...] = mm(x, wqkv[:, :D]).astype(BF) * jnp.asarray(SCALE, BF)
    stats[...] = jnp.zeros_like(stats)

    def self_block(sub, rows, at):
        meta = query_meta(mk, at)

        def run(pairs, ks, wd):
            mask = self_mask(mk, meta, at, ks, wd)
            attend(pairs, q, rows, kv.at[0], mask, ks, wd, att, stats, 0)

        by_width(tab[5, SUBS * b + sub], tab[4, SUBS * b + sub], widths, run)

    each_sub(row0, self_block)
    normed, inv = norm_stats(x.astype(F32) + mm(att[...], wso[...]))
    n0[...] = normed
    lane = lax.broadcasted_iota(jnp.int32, stats.shape, 1)
    stats[...] = jnp.where(lane == INV, inv, stats[...])
    first = normed * gains[0:1, :] + biases[0:1, :]
    cq[...] = mm(first.astype(BF), wcq[...]).astype(BF) * jnp.asarray(SCALE, BF)

    def cross_block(sub, rows, at):
        meta = query_meta(mk, at)

        def run(pairs, ks, wd):
            mask = cross_mask(mk, meta, at, ks, wd)
            attend(pairs, cq, rows, mkv.at[0], mask, ks, wd, catt, stats, CROSS)

        by_width(tab[7, SUBS * b + sub], tab[6, SUBS * b + sub], widths, run)

    each_sub(row0, cross_block)


def line_end(acc, inputs, weight, base, rows, gline, dwt):
    columns = 256

    @pl.loop(0, acc.shape[1] // columns)
    def _(i):
        cols = pl.ds(pl.multiple_of(i * columns, columns), columns)
        low = acc[:, cols].astype(BF)
        back = mm(weight[:, base:], low).T
        if rows is not None:
            back = back + rows[cols, :]
        gline[0, cols, :] = back.astype(BF)
        dwt[...] += mm(low, inputs[0, cols, :])


def cross_backward(
    widths, tab, es, mk, n0, stats, att, gsecond, gatt, cq, mkv, wckv, wso, wcq, gains, biases,
    gfirst, gself, eline, att_grad, norm_grad,
    acc, dq, dwckvt, dwcq, dwso, gb,
):
    b = pl.program_id(0)
    row0 = pl.multiple_of(tab[1, b], BLOCK)

    @pl.when(b == 0)
    def _():
        for ref in (dwckvt, dwcq, dwso, gb):
            ref[...] = jnp.zeros_like(ref)

    @pl.when(tab[2, b] == 1)
    def _():
        acc[...] = jnp.zeros_like(acc)

    def cross_block(sub, here, at):
        meta = query_meta(mk, at)

        def run(pairs, ks, wd):
            mask = cross_mask(mk, meta, at, ks, wd)
            attend_back(pairs, cq, gatt, stats, CROSS, here, mkv.at[0], mask, ks, wd, acc, dq)

        by_width(tab[7, SUBS * b + sub], tab[6, SUBS * b + sub], widths, run)

    each_sub(row0, cross_block)
    first = n0[...] * gains[0:1, :] + biases[0:1, :]
    dwcq[...] += mm(first.astype(BF).T, dq[...])
    gf = gsecond[...] + mm_nt(dq[...], wcq[...])
    gb[0] += fold8(gf * n0[...])
    gb[1] += fold8(gf)
    gf = norm_back(gf, n0[...], stats[:, INV : INV + 1], gains[0:1, :])
    gfirst[...] = gf
    sg = gf.astype(BF)
    dwso[...] += mm(att[...].T, sg)
    gself[...] = mm_nt(sg, wso[...]).astype(BF)

    @pl.when(tab[3, b] == 1)
    def _():
        line_end(acc, es, wckv, 0, None, eline, dwckvt)

    @pl.when(b == pl.num_programs(0) - 1)
    def _():
        att_grad[: 2 * D, :] = dwckvt[...].astype(BF)
        att_grad[2 * D : 3 * D, :] = dwso[...].astype(BF)
        att_grad[3 * D :, :] = dwcq[...].astype(BF)
        sums = jnp.sum(gb[...], axis=1)
        none = jnp.zeros((2, D), F32)
        norm_grad[...] = jnp.concatenate([sums[0:1], none, sums[1:2], none, none])


def self_backward(widths, tab, xs, mk, stats, q, g, gf, kv, wqkv, sline, qkv_grad, acc, dq, rows, dwq, dwkvt):
    b = pl.program_id(0)
    row0 = pl.multiple_of(tab[1, b], BLOCK)

    @pl.when(b == 0)
    def _():
        dwq[...] = jnp.zeros_like(dwq)
        dwkvt[...] = jnp.zeros_like(dwkvt)

    @pl.when(tab[2, b] == 1)
    def _():
        acc[...] = jnp.zeros_like(acc)
        rows[...] = jnp.zeros_like(rows)

    def self_block(sub, here, at):
        meta = query_meta(mk, at)

        def run(pairs, ks, wd):
            mask = self_mask(mk, meta, at, ks, wd)
            attend_back(pairs, q, g, stats, 0, here, kv.at[0], mask, ks, wd, acc, dq)

        by_width(tab[5, SUBS * b + sub], tab[4, SUBS * b + sub], widths, run)

    each_sub(row0, self_block)
    own = pl.ds(row0, BLOCK)
    dwq[...] += mm(xs[0, own, :].T, dq[...])
    rows[own, :] = gf[...] + mm_nt(dq[...], wqkv[:, :D])

    @pl.when(tab[3, b] == 1)
    def _():
        line_end(acc, xs, wqkv, D, rows, sline, dwkvt)

    @pl.when(b == pl.num_programs(0) - 1)
    def _():
        qkv_grad[:D, :] = dwq[...].astype(BF)
        qkv_grad[D:, :] = dwkvt[...].astype(BF)


def const_spec(shape):
    return pl.BlockSpec(shape, lambda b, t: (0,) * len(shape), pipeline_mode=pl.Buffered(1))


def row_spec(cols):
    return pl.BlockSpec((BLOCK, cols), lambda b, t: (b, 0))


def line_spec(shape):
    return pl.BlockSpec((1,) + shape, lambda b, t: (t[0, b],) + (0,) * len(shape))


def sds(shape, dtype):
    return jax.ShapeDtypeStruct(shape, dtype)


def kernels(
    lines, n, tab, xs, es, cot, mk, self_qkv, self_out, cross_q, cross_kv, cross_out, weights, norm_gain, norm_bias
):
    slots, line_len = xs.shape[0], xs.shape[1]
    whole, p, k = plan(lines, n)
    rows_all = whole * line_len + k * line_len // p
    blocks = rows_all // BLOCK
    widths = widths_for(line_len)
    params = pltpu.CompilerParams(vmem_limit_bytes=VMEM, dimension_semantics=("arbitrary",))

    def call(kernel, name, ins, in_specs, outs, out_specs, scratch, flops):
        return pl.pallas_call(
            kernel,
            name=name,
            grid_spec=pltpu.PrefetchScalarGridSpec(
                num_scalar_prefetch=1,
                grid=(blocks,),
                in_specs=in_specs,
                out_specs=out_specs,
                scratch_shapes=scratch,
            ),
            out_shape=outs,
            compiler_params=params,
            cost_estimate=pl.CostEstimate(
                flops=int(flops), bytes_accessed=16 << 20, transcendentals=1 << 20
            ),
        )(tab, *ins)

    line2 = (line_len, 2 * D)
    rows_low, line_in, line_kv = sds((rows_all, D), BF), line_spec((line_len, D)), line_spec(line2)
    meta = line_spec((8, line_len))
    kv, mkv, q, cq, att, catt, n0, stats = call(
        functools.partial(forward, widths),
        "forward",
        (xs, es, mk, self_qkv, self_out, cross_kv, cross_q, norm_gain, norm_bias),
        [
            line_in, line_in, meta, const_spec((D, 3 * D)), const_spec((D, D)), const_spec((D, 2 * D)),
            const_spec((D, D)), const_spec((3, D)), const_spec((3, D)),
        ],
        (
            sds((slots,) + line2, BF), sds((slots,) + line2, BF), rows_low, rows_low, rows_low, rows_low,
            sds((rows_all, D), F32), sds((rows_all, 128), F32),
        ),
        (line_kv, line_kv) + (row_spec(D),) * 5 + (row_spec(128),),
        [],
        4e10,
    )

    out, gsecond, gatt, ffn_grad, co_grad, norm_a = feed(
        cot, n0, catt, cross_out, weights, norm_gain, norm_bias, lines, n, line_len
    )

    wide, tall, square = pltpu.VMEM((2 * D, line_len), F32), pltpu.VMEM((2 * D, D), F32), pltpu.VMEM((D, D), F32)
    low = pltpu.VMEM((BLOCK, D), BF)
    lines_low = sds((slots, line_len, D), BF)
    gfirst, gself, enc_line, att_grad, norm_b = call(
        functools.partial(cross_backward, widths),
        "cross_backward",
        (
            es, mk, n0, stats, att, gsecond, gatt, cq, mkv, cross_kv, self_out, cross_q,
            norm_gain, norm_bias,
        ),
        [line_in, meta, row_spec(D), row_spec(128)]
        + [row_spec(D)] * 4
        + [line_kv, const_spec((D, 2 * D)), const_spec((D, D)), const_spec((D, D)), const_spec((3, D)), const_spec((3, D))],
        (sds((rows_all, D), F32), rows_low, lines_low, sds((4 * D, D), BF), sds((8, D), F32)),
        (row_spec(D), row_spec(D), line_in, const_spec((4 * D, D)), const_spec((8, D))),
        [wide, low, tall, square, square, pltpu.VMEM((2, 8, D), F32)],
        3e10,
    )
    stream_line, qkv_grad = call(
        functools.partial(self_backward, widths),
        "self_backward",
        (xs, mk, stats, q, gself, gfirst, kv, self_qkv),
        [line_in, meta, row_spec(128)] + [row_spec(D)] * 3 + [line_kv, const_spec((D, 3 * D))],
        (lines_low, sds((3 * D, D), BF)),
        (line_in, const_spec((3 * D, D))),
        [wide, low, pltpu.VMEM((line_len, D), F32), square, tall],
        3e10,
    )
    return out, enc_line, stream_line, ffn_grad, att_grad, co_grad, qkv_grad, norm_a, norm_b


def remote(src, dst, send, recv, device):
    return pltpu.make_async_remote_copy(
        src_ref=src, dst_ref=dst, send_sem=send, recv_sem=recv, device_id={"seq": device},
        device_id_type=pl.DeviceIdType.MESH,
    )


def part_of(device, p):
    return (device % p + device // p) % p


class Exchange:
    def __init__(self, lines, n, line_len):
        self.n, self.piece = n, line_len // n
        self.whole, self.p, self.k = plan(lines, n)
        self.groups = n // self.p
        self.chunks = n // self.p
        self.part_len = line_len // self.p
        self.line_len = line_len
        self.shared0 = self.whole * n
        self.rows_p = self.k * self.part_len
        self.me = lax.axis_index("seq")
        self.group = self.me // self.p
        self.part = part_of(self.me, self.p)
        self.pos_part, self.pos_chunk = self.me // self.chunks, self.me % self.chunks

    def owner(self, group):
        return group * self.p + (self.pos_part + self.p * self.groups - group) % self.p


ROWS_AT, SHARES_AT = (-1, -1, 0, 5, 6), 1
FFN_LAG, NORM_LAG = 0, 1


class Dim:
    def __init__(self, axis, stride, size):
        self.axis, self.stride, self.size = axis, stride, size
        at = lax.axis_index(axis)
        self.index = at // stride % size
        self.rest = at - self.index * stride

    def peer(self, v):
        return (self.index + v) % self.size

    def device(self, v):
        return {self.axis: self.rest + self.peer(v) * self.stride}


def send_to(src, dst, sems, device):
    return pltpu.make_async_remote_copy(
        src_ref=src, dst_ref=dst, send_sem=sems[0], recv_sem=sems[1], device_id=device,
        device_id_type=pl.DeviceIdType.MESH,
    )


class Sems:
    def __init__(self, ref):
        self.ref, self.used = ref, 0

    def next(self):
        self.used += 1
        return self.ref.at[0, self.used - 1], self.ref.at[1, self.used - 1]


def mesh_dims(ex):
    return (
        Dim("dp", 1, 2), Dim("dp", 2, lax.axis_size("dp") // 2), Dim("seq", 1, ex.p), Dim("seq", ex.p, ex.groups),
    )


def greet(ex, *dims):
    barrier = pltpu.get_barrier_semaphore()
    greeted = [{"seq": (ex.me + o) % ex.n} for o in range(1, ex.n)]
    greeted += [dim.device(v) for dim in dims for v in range(1, dim.size)]
    for device in greeted:
        pl.semaphore_signal(barrier, inc=1, device_id=device, device_id_type=pl.DeviceIdType.MESH)
    pl.semaphore_wait(barrier, len(greeted))


def start_all(copies):
    for copy in copies:
        copy.start()


def gather(dim, view, sems):
    copies = [send_to(view, view, sems.next(), dim.device(v)) for v in range(1, dim.size)]

    def finish():
        for copy in copies:
            copy.wait()

    return copies, finish


def in_kernel(
    ex, x_ref, rc_ref, e_ref, w_in, w_out, xs, rc, es, weights, sem_w, sem_p, sem_f, sem_l, sem_g
):
    n, piece, w, k, me = ex.n, ex.piece, ex.whole, ex.k, ex.me
    core, yy, xx, zz = mesh_dims(ex)
    c, y, x, z = core.index, yy.index, xx.index, zz.index
    quarter = 2 * D // (2 * yy.size)
    weights = weights.reshape(ex.groups, ex.p, yy.size, 2, quarter, w_in.shape[1])
    index, each = y * 2 + c, D // quarter

    def own_quarter(src, at):
        rows = pl.ds(pl.multiple_of(at * quarter, quarter), quarter)
        return pltpu.make_async_copy(src.at[rows], weights.at[z, x, y, c], sem_l.at[3, 0])

    @pl.when(index < each)
    def _():
        own_quarter(w_in, index).start()

    @pl.when(index >= each)
    def _():
        own_quarter(w_out, index - each).start()

    greet(ex, core, yy)
    own_quarter(w_in, 0).wait()
    sems = Sems(sem_g)
    stages = [
        gather(zz, weights.at[z, x, y, c], sems),
        gather(xx, weights.at[:, x, y, c], sems),
        gather(yy, weights.at[:, :, y, c], sems),
        gather(core, weights.at[:, :, :, c], sems),
    ]
    start_all(stages[0][0])

    def next_stage(i):
        stages[i][1]()
        if i + 1 < len(stages):
            start_all(stages[i + 1][0])

    spans = pl.ds(pl.multiple_of(me * piece, piece), piece)
    names = (x_ref, rc_ref, e_ref)

    def line_dst(out, slots):
        if out is rc:
            return rc.at[slots, me]
        return out.at[slots, spans]

    def whole_copies(a, o):
        to = (me + o) % n
        src = names[a]
        pairs = [(src.at[pl.ds(to * w, w)], line_dst((xs, rc, es)[a], pl.ds(k, w)))] if w else []
        return [
            remote(s, d, sem_w.at[0, a, i, o], sem_w.at[1, a, i, o], to)
            if o
            else pltpu.make_async_copy(s, d, sem_l.at[a, i])
            for i, (s, d) in enumerate(pairs)
        ]

    def shared_pairs(a, group):
        src = names[a]
        first = ex.shared0 + group * k
        return [(src.at[pl.ds(first, k)], line_dst((xs, rc, es)[a], pl.ds(0, k)))] if k else []

    def shared_send(a, u):
        group = (ex.group + u) % ex.groups
        to = ex.owner(group)
        return [
            remote(s, d, sem_p.at[0, a, i, u], sem_p.at[1, a, i, ex.pos_chunk], to)
            for i, (s, d) in enumerate(shared_pairs(a, group))
        ]

    def shared_local(a):
        return [
            pltpu.make_async_copy(s, d, sem_l.at[a, max(w, 1) + i])
            for i, (s, d) in enumerate(shared_pairs(a, ex.group))
        ]

    def shared_arrival(a, j):
        return [
            remote(s, d, sem_p.at[0, a, i, 0], sem_p.at[1, a, i, j], me)
            for i, (s, d) in enumerate(shared_pairs(a, ex.group))
        ]

    def forwards(a):
        out = (xs, rc, es)[a]
        mine = ex.part * ex.part_len
        if a == 1:
            view = rc.at[pl.ds(0, k), pl.ds(ex.part * ex.chunks, ex.chunks)]
        else:
            view = out.at[pl.ds(0, k), pl.ds(pl.multiple_of(mine, ex.part_len), ex.part_len)]
        return [
            remote(view, view, sem_f.at[0, a, v], sem_f.at[1, a, v], ex.group * ex.p + (me % ex.p + v) % ex.p)
            for v in range(1, ex.p)
        ]

    here = ex.pos_part == ex.part
    for a in range(3):
        for u in range(ex.groups if k else 0):
            if u == 0:

                @pl.when(here)
                def _():
                    for copy in shared_local(a):
                        copy.start()

                @pl.when(jnp.logical_not(here))
                def _():
                    for copy in shared_send(a, 0):
                        copy.start()

            else:
                for copy in shared_send(a, u):
                    copy.start()
        for o in range(n):
            for copy in whole_copies(a, o):
                copy.start()
    next_stage(0)
    for a in range(3):
        next_stage(a + 1)
        for j in range(ex.chunks if k else 0):
            own = ex.part * ex.chunks + j == me

            @pl.when(own)
            def _():
                for copy in shared_local(a):
                    copy.wait()

            @pl.when(jnp.logical_not(own))
            def _():
                for copy in shared_arrival(a, j):
                    copy.wait_recv()

        if k:
            for copy in forwards(a):
                copy.start()
    for a in range(3):
        for o in range(n):
            for copy in whole_copies(a, o):
                copy.wait()
        for u in range(ex.groups if k else 0):
            if u == 0:

                @pl.when(jnp.logical_not(here))
                def _():
                    for copy in shared_send(a, 0):
                        copy.wait_send()

            else:
                for copy in shared_send(a, u):
                    copy.wait_send()
        if k:
            for copy in forwards(a):
                copy.wait()


def feed_kernel(
    ex, cot_src, n0, catt, wco, wff, gains, biases,
    out, gsecond_out, gatt, ffn_grad, co_grad, norm_grad,
    cot, out_v, hid, gprime, dw1, dw2t, dwco, gb, sem_cs, sem_cw, sem_os, sem_ow,
):
    b, last = pl.program_id(0), pl.num_programs(0) - 1
    n, piece, w, k, me = ex.n, ex.piece, ex.whole, ex.k, ex.me

    def rows_at(row):
        return pl.ds(pl.multiple_of(row, piece), piece)

    def cot_copy(i, slot, row, sems, at, to):
        src, dst = cot_src.at[slot], cot.at[rows_at(row)]
        local = lambda: pltpu.make_async_copy(src, dst, sems.at[1, i, at])
        return local, lambda sent: send_to(src, dst, (sems.at[0, i, sent], sems.at[1, i, at]), {"seq": to})

    def cot_sends():
        for u in range(ex.groups if k else 0):
            group = (ex.group + u) % ex.groups
            to = ex.owner(group)
            for i in range(k):
                row = i * ex.part_len + ex.pos_chunk * piece
                local, far = cot_copy(i, ex.shared0 + group * k + i, row, sem_cs, ex.pos_chunk, to)
                yield to, local, functools.partial(far, u)
        for v in range(n):
            to = (me + v) % n
            for i in range(w):
                row = ex.rows_p + i * ex.line_len + me * piece
                local, far = cot_copy(i, to * w + i, row, sem_cw, me, to)
                yield to, local, functools.partial(far, v)

    def out_copy(row, slot, i, sems, sent, at, to):
        src, dst = out_v.at[rows_at(row)], out.at[slot]
        return (
            to,
            lambda: pltpu.make_async_copy(src, dst, sems.at[1, i, at]),
            lambda: send_to(src, dst, (sems.at[0, i, sent], sems.at[1, i, at]), {"seq": to}),
        )

    def out_shared(row):
        i, j = row // ex.part_len, row % ex.part_len // piece
        return out_copy(
            row, ex.shared0 + ex.group * k + i, i, sem_os, j, ex.group, ex.part * ex.chunks + j
        )

    def out_whole(row):
        at = row - ex.rows_p
        i, s = at // ex.line_len, at % ex.line_len // piece
        return out_copy(row, me * w + i, i, sem_ow, s, me, s)

    def either(to, here, there):
        @pl.when(to == me)
        def _():
            here()

        @pl.when(to != me)
        def _():
            there()

    @pl.when(b == 0)
    def _():
        for ref in (dw1, dw2t, dwco, gb):
            ref[...] = jnp.zeros_like(ref)
        greet(ex)
        for to, local, far in cot_sends():
            either(to, lambda: local().start(), lambda: far().start())

    first = n0[...] * gains[0:1, :] + biases[0:1, :]
    n1, s1 = norm_stats(first + mm(catt[...], wco[...]))
    second = n1 * gains[1:2, :] + biases[1:2, :]
    second_low = second.astype(BF)
    chunks, chunk = wff.shape[0], wff.shape[2]
    total = second
    for c in range(chunks):
        cols = slice(c * chunk, (c + 1) * chunk)
        v = mm(second_low, wff[c, :D, :])
        v2 = v * v
        t = jnp.tanh(GELU_C * (v + 0.044715 * (v2 * v)))
        half = 0.5 * (1.0 + t)
        h = (v * half).astype(BF)
        hid[:, cols] = h
        gprime[:, cols] = half + (0.5 * v) * (1.0 - t * t) * (GELU_C + (3 * 0.044715 * GELU_C) * v2)
        total = total + mm_nt(h, wff[c, D:, :])
    n2, s2 = norm_stats(total)
    here = pl.ds(pl.multiple_of(b * BLOCK, BLOCK), BLOCK)
    out_v[here, :] = (n2 * gains[2:3, :] + biases[2:3, :]).astype(BF)

    for q in range(BLOCK // piece):
        row = b * BLOCK + q * piece

        @pl.when(row < ex.rows_p)
        def _():
            i, j = row // ex.part_len, row % ex.part_len // piece
            local, far = cot_copy(i, 0, row, sem_cs, j, me)
            either(ex.part * ex.chunks + j, lambda: local().wait(), lambda: far(0).wait_recv())
            to, local, far = out_shared(row)
            either(to, lambda: local().start(), lambda: far().start())

        @pl.when(row >= ex.rows_p)
        def _():
            at = row - ex.rows_p
            i, s = at // ex.line_len, at % ex.line_len // piece
            local, far = cot_copy(i, 0, row, sem_cw, s, me)
            either(s, lambda: local().wait(), lambda: far(0).wait_recv())
            to, local, far = out_whole(row)
            either(to, lambda: local().start(), lambda: far().start())

    dy = cot[here, :].astype(F32)
    gb[1] += fold8(dy * n2)
    gb[3] += fold8(dy)
    gthird = norm_back(dy, n2, s2, gains[2:3, :])
    fg = gthird.astype(BF)
    fgt, sect = fg.T, second_low.T
    back = gthird
    for c in range(chunks):
        cols = slice(c * chunk, (c + 1) * chunk)
        pg = (mm(fg, wff[c, D:, :]) * gprime[:, cols]).astype(BF)
        dw2t[:, cols] += mm(fgt, hid[:, cols])
        dw1[:, cols] += mm(sect, pg)
        back = back + mm_nt(pg, wff[c, :D, :])
    gb[0] += fold8(back * n1)
    gb[2] += fold8(back)
    gsecond = norm_back(back, n1, s1, gains[1:2, :])
    gsecond_out[...] = gsecond
    cg = gsecond.astype(BF)
    dwco[...] += mm(catt[...].T, cg)
    gatt[...] = mm_nt(cg, wco[...]).astype(BF)

    @pl.when(b == last)
    def _():
        for c in range(chunks):
            cols = slice(c * chunk, (c + 1) * chunk)
            ffn_grad[c, :D, :] = dw1[:, cols].astype(BF)
            ffn_grad[c, D:, :] = dw2t[:, cols].astype(BF)
        co_grad[...] = dwco[...].astype(BF)
        sums = jnp.sum(gb[...], axis=1)
        none = jnp.zeros((1, D), F32)
        norm_grad[...] = jnp.concatenate([none, sums[:2], none, sums[2:], none, none])
        for to, local, far in cot_sends():
            either(to, lambda: None, lambda: far().wait_send())
        for row in range(0, ex.rows_p, piece):
            to, local, far = out_shared(row)
            either(to, lambda: local().wait(), lambda: far().wait_send())
        for row in range(ex.rows_p, cot.shape[0], piece):
            to, local, far = out_whole(row)
            either(to, lambda: local().wait(), lambda: far().wait_send())
        for i in range(k):
            for group in range(ex.groups):
                arrival = out_copy(0, ex.shared0 + group * k + i, i, sem_os, 0, group, me)[2]
                either(ex.owner(group), lambda: None, lambda: arrival().wait_recv())
        for i in range(w):
            for s in range(n):
                arrival = out_copy(0, s * w + i, i, sem_ow, 0, s, me)[2]
                either(s, lambda: None, lambda: arrival().wait_recv())


def feed(cot_src, n0, catt, wco, weights, gains, biases, lines, n, line_len):
    whole, p, k = plan(lines, n)
    most = max(k, whole, 1)
    rows_all, cols = n0.shape[0], weights.shape[2]
    ff = n * cols

    def kernel(*refs):
        feed_kernel(Exchange(lines, n, line_len), *refs)

    row = lambda c: pl.BlockSpec((BLOCK, c), lambda b: (b, 0))
    const = lambda *shape: pl.BlockSpec(shape, lambda b: (0,) * len(shape), pipeline_mode=pl.Buffered(1))
    hbm = pl.BlockSpec(memory_space=pl.ANY)
    dma = pltpu.SemaphoreType.DMA
    return pl.pallas_call(
        kernel,
        name="feed",
        grid=(rows_all // BLOCK,),
        in_specs=[hbm, row(D), row(D), const(D, D), const(n, 2 * D, cols), const(3, D), const(3, D)],
        out_specs=[hbm, row(D), row(D), const(n, 2 * D, cols), const(D, D), const(8, D)],
        out_shape=(
            sds((lines, line_len // n, D), BF),
            sds((rows_all, D), F32),
            sds((rows_all, D), BF),
            sds((n, 2 * D, cols), BF),
            sds((D, D), BF),
            sds((8, D), F32),
        ),
        scratch_shapes=[
            pltpu.VMEM((rows_all, D), BF),
            pltpu.VMEM((rows_all, D), BF),
            pltpu.VMEM((BLOCK, ff), BF),
            pltpu.VMEM((BLOCK, ff), F32),
            pltpu.VMEM((D, ff), F32),
            pltpu.VMEM((D, ff), F32),
            pltpu.VMEM((D, D), F32),
            pltpu.VMEM((4, 8, D), F32),
            dma((2, most, n)),
            dma((2, most, n)),
            dma((2, most, n)),
            dma((2, most, n)),
        ],
        compiler_params=pltpu.CompilerParams(
            collective_id=3, has_side_effects=True, vmem_limit_bytes=VMEM,
            dimension_semantics=("arbitrary",),
        ),
        cost_estimate=pl.CostEstimate(flops=int(4e10), bytes_accessed=16 << 20, transcendentals=1 << 20),
    )(cot_src, n0, catt, wco, weights, gains, biases)


def exchange_in(stream, rc, encoder, w_in, w_out, lines, n, line_len, dp):
    whole, p, k = plan(lines, n)
    hops = 1 + dp // 2 - 1 + p - 1 + n // p - 1
    slots, piece = k + whole, line_len // n
    most = max(k, whole, 1)

    def kernel(*refs):
        in_kernel(Exchange(lines, n, line_len), *refs)

    dma = pltpu.SemaphoreType.DMA
    return pl.pallas_call(
        kernel,
        name="exchange_in",
        in_specs=[pl.BlockSpec(memory_space=pl.ANY)] * 5,
        out_specs=[pl.BlockSpec(memory_space=pl.ANY)] * 4,
        out_shape=(
            sds((slots, line_len, D), BF),
            sds((slots, n, 1, piece), jnp.int32),
            sds((slots, line_len, D), BF),
            sds((n, 2 * D, w_in.shape[1]), BF),
        ),
        scratch_shapes=[
            dma((2, 3, most, n)), dma((2, 3, most, n)), dma((2, 3, max(p, 2))), dma((4, 2 * most)),
            dma((2, hops)),
        ],
        compiler_params=pltpu.CompilerParams(collective_id=1, has_side_effects=True),
    )(stream, rc, encoder, w_in, w_out)


def flat_loop(lead, run):
    @pl.loop(0, math.prod(lead))
    def _(i):
        index = []
        for size in reversed(lead):
            index.append(i % size)
            i = i // size
        run(tuple(reversed(index)))


def add_into(dst, sources, lead):
    def run(index):
        total = dst[index].astype(F32)
        for source in sources:
            total = total + source[index].astype(F32)
        dst[index] = total.astype(dst.dtype)

    flat_loop(lead, run)


def finish_kernel(
    ex, enc_line, stream_line, ffn_grad, att_grad, co_grad, qkv_grad, norm_a, norm_b,
    enc, stream, ffn, att, norms,
    ffn_v, att_v, norm_v, ffn_bufs, att_bufs, norm_bufs, own_v, part_v,
    sem_red, sem_w, sem_p, sem_l, sem_s, sem_in,
):
    n, piece, w, k, p, me = ex.n, ex.piece, ex.whole, ex.k, ex.p, ex.me
    core, yy, xx, zz = mesh_dims(ex)
    outer = yy.size

    loads = [
        pltpu.make_async_copy(ffn_grad, ffn_v, sem_in.at[0]),
        pltpu.make_async_copy(att_grad, att_v.at[pl.ds(0, 4 * D)], sem_in.at[1]),
        pltpu.make_async_copy(co_grad, att_v.at[pl.ds(4 * D, D)], sem_in.at[2]),
        pltpu.make_async_copy(qkv_grad, att_v.at[pl.ds(5 * D, 3 * D)], sem_in.at[3]),
    ]
    lines = (enc_line, stream_line)
    mine = pl.ds(pl.multiple_of(ex.part * ex.part_len, ex.part_len), ex.part_len)
    if k:
        loads += [
            pltpu.make_async_copy(lines[a].at[pl.ds(0, k), mine], own_v.at[a], sem_in.at[4 + a])
            for a in range(2)
        ]
    start_all(loads)
    norm_v[...] = norm_a[...] + norm_b[...]
    greet(ex, core, yy)

    fl = ffn_v.shape
    rows = fl[1] // (2 * outer)
    ffn_6 = ffn_v.reshape(ex.groups, p, outer, 2, rows, fl[2])
    att_rows = att_v.shape[0] // (2 * outer * n)
    att_6 = att_v.reshape(2, outer, p, ex.groups, att_rows, D)
    ffn_o = ffn.reshape(outer, 2, rows, fl[2])
    att_o = att.reshape(2, outer, p, ex.groups, att_rows, D)
    c, y, x, z = core.index, yy.index, xx.index, zz.index
    sems = Sems(sem_red)

    def scatter(dim, view, buf, lead):
        copies = [
            send_to(view(dim.peer(v)), buf.at[v - 1], sems.next(), dim.device(v)) for v in range(1, dim.size)
        ]

        def finish():
            for copy in copies:
                copy.wait()
            add_into(view(dim.index), [buf.at[v - 1] for v in range(1, dim.size)], lead)

        return copies, finish

    def place(src, dst, sem):
        copy = pltpu.make_async_copy(src, dst, sem)
        return [copy], copy.wait

    def exchange_all(dim, buf):
        copies = [send_to(norm_v, buf.at[v - 1], sems.next(), dim.device(v)) for v in range(1, dim.size)]

        def finish():
            for copy in copies:
                copy.wait()
            norm_v[...] = sum([buf[v - 1] for v in range(1, dim.size)], norm_v[...])

        return copies, finish

    g, o = ex.groups, outer

    def att_stream(h, half):
        r = pl.ds(h * half, half)
        bufs = [buf.at[..., r, :] for buf in att_bufs]
        return [
            scatter(core, lambda t: att_6.at[t, :, :, :, r], bufs[0], (o, p, g)),
            scatter(yy, lambda t: att_6.at[c, t, :, :, r], bufs[1], (p, g)),
            scatter(xx, lambda t: att_6.at[c, y, t, :, r], bufs[2], (g,)),
            scatter(zz, lambda t: att_6.at[c, y, x, t, r], bufs[3], ()),
            place(att_6.at[c, y, x, z, r], att_o.at[c, y, x, z, r], sem_in.at[7 + h]),
            gather(zz, att_o.at[c, y, x, z, r], sems),
            gather(xx, att_o.at[c, y, x, :, r], sems),
            gather(yy, att_o.at[c, y, :, :, r], sems),
            gather(core, att_o.at[c, :, :, :, r], sems),
        ]

    halves = 2 if att_rows % 32 == 0 else 1
    streams = [att_stream(h, att_rows // halves) for h in range(halves)]
    streams += [
        [
            scatter(core, lambda t: ffn_6.at[:, :, :, t], ffn_bufs[0], (g, p, o)),
            scatter(yy, lambda t: ffn_6.at[:, :, t, c], ffn_bufs[1], (g, p)),
            scatter(xx, lambda t: ffn_6.at[:, t, y, c], ffn_bufs[2], (g,)),
            scatter(zz, lambda t: ffn_6.at[t, x, y, c], ffn_bufs[3], ()),
            place(ffn_6.at[z, x, y, c], ffn_o.at[y, c], sem_in.at[6]),
            gather(yy, ffn_o.at[y, c], sems),
            gather(core, ffn_o.at[:, c], sems),
        ],
        [exchange_all(dim, norm_bufs[i]) for i, dim in enumerate((core, yy, xx, zz))],
    ]

    lags = [0] * halves + [FFN_LAG, NORM_LAG]

    def whole_src(a, i, to):
        return lines[a].at[k + i, pl.ds(pl.multiple_of(to * piece, piece), piece)]

    outs = (enc, stream)

    def whole_copies(a, v):
        to = (me + v) % n
        result = []
        for i in range(w):
            src, dst = whole_src(a, i, to), outs[a].at[me * w + i]
            result.append(
                send_to(src, dst, (sem_w.at[0, a, i, v], sem_w.at[1, a, i, v]), {"seq": to})
                if v
                else pltpu.make_async_copy(src, dst, sem_l.at[a, i])
            )
        return result

    def shared_pair(a, i, j):
        at = pl.ds(pl.multiple_of(j * piece, piece), piece)
        src = own_v.at[a, i, at]
        return src, outs[a].at[ex.shared0 + ex.group * k + i]

    def shared_copies(a, u):
        j = (ex.group + u) % ex.chunks
        to = ex.part * ex.chunks + j
        return to, [
            send_to(*shared_pair(a, i, j), (sem_p.at[0, a, i, u], sem_p.at[1, a, i, ex.group]), {"seq": to})
            for i in range(k)
        ]

    def local_copies(a):
        return [
            pltpu.make_async_copy(*shared_pair(a, i, ex.pos_chunk), sem_l.at[a, max(w, 1) + i])
            for i in range(k)
        ]

    def each_shared(a, remote_run, local_run):
        for u in range(ex.chunks if k else 0):
            to, copies = shared_copies(a, u)

            @pl.when(to != me)
            def _():
                for copy in copies:
                    remote_run(copy)

            @pl.when(to == me)
            def _():
                for copy in local_copies(a):
                    local_run(copy)

    def sharing(a, v):
        part = (ex.part + v) % p
        theirs = pl.ds(pl.multiple_of(part * ex.part_len, ex.part_len), ex.part_len)
        return send_to(
            lines[a].at[pl.ds(0, k), theirs], part_v.at[a, v - 1], (sem_s.at[0, a, v], sem_s.at[1, a, v]),
            xx.device(v),
        )

    for copy in loads:
        copy.wait()
    for stages in streams:
        start_all(stages[0][0])
    shares = [sharing(a, v) for a in range(2) for v in range(1, p)] if k else []
    start_all(shares)

    def start_whole(a, places):
        for v in places:
            start_all(whole_copies(a, v))

    def start_shared(a):
        each_shared(a, lambda copy: copy.start(), lambda copy: copy.start())

    batches = [
        lambda: start_whole(0, range(n)),
        lambda: start_whole(1, range(n // 2)),
        lambda: start_whole(1, range(n // 2, n)),
        lambda: start_shared(0),
        lambda: start_shared(1),
    ]

    def start_batches(step):
        for at, batch in zip(ROWS_AT, batches):
            if step == at:
                batch()

    start_batches(-1)
    for step in range(max(len(stages) + lag for stages, lag in zip(streams, lags))):
        for stages, lag in zip(streams, lags):
            stage = step - lag
            if 0 <= stage < len(stages):
                stages[stage][1]()
            if 0 <= stage < len(stages) - 1:
                start_all(stages[stage + 1][0])
        if step == SHARES_AT:
            for copy in shares:
                copy.wait()
            for a in range(2 if k else 0):
                add_into(own_v.at[a], [part_v.at[a, v - 1] for v in range(1, p)], (k,))
        start_batches(step)
    norms[...] = norm_v[...]
    for a in range(2):
        for v in range(n):
            for copy in whole_copies(a, v):
                copy.wait()
        each_shared(a, lambda copy: copy.wait_send(), lambda copy: copy.wait())
        for group in range(ex.groups if k else 0):

            @pl.when(ex.owner(group) != me)
            def _():
                for i in range(k):
                    sems = (sem_p.at[0, a, i, 0], sem_p.at[1, a, i, group])
                    send_to(*shared_pair(a, i, 0), sems, {"seq": me}).wait_recv()


def finish(arrays, lines, n, line_len, dp):
    whole, p, k = plan(lines, n)
    piece, most, groups, outer = line_len // n, max(k, whole, 1), n // p, dp // 2
    cols = arrays[2].shape[2]
    rows, att_rows = 2 * D // dp, 8 * D // (dp * n)
    part_len = line_len // p
    slots = max(k, 1)

    def kernel(*refs):
        refs = list(refs)
        grouped = refs[:16] + [refs[16:20], refs[20:24], refs[24:28]] + refs[28:]
        finish_kernel(Exchange(lines, n, line_len), *grouped)

    dma = pltpu.SemaphoreType.DMA
    hops = (1, outer - 1, p - 1, groups - 1)
    hbm = pl.BlockSpec(memory_space=pl.ANY)
    vmem = pl.BlockSpec(memory_space=pltpu.VMEM)
    at_least = lambda q: max(q, 1)
    return pl.pallas_call(
        kernel,
        name="finish",
        in_specs=[hbm] * 6 + [vmem] * 2,
        out_specs=[hbm] * 2 + [vmem] * 3,
        out_shape=[sds((lines, piece, D), BF)] * 2
        + [sds((2 * D, cols), BF), sds((8 * D, D), BF), sds((8, D), F32)],
        scratch_shapes=[
            pltpu.VMEM((n, 2 * D, cols), BF),
            pltpu.VMEM((8 * D, D), BF),
            pltpu.VMEM((8, D), F32),
            pltpu.VMEM((1, groups, p, outer, rows, cols), BF),
            pltpu.VMEM((at_least(outer - 1), groups, p, rows, cols), BF),
            pltpu.VMEM((at_least(p - 1), groups, rows, cols), BF),
            pltpu.VMEM((at_least(groups - 1), rows, cols), BF),
            pltpu.VMEM((1, outer, p, groups, att_rows, D), BF),
            pltpu.VMEM((at_least(outer - 1), p, groups, att_rows, D), BF),
            pltpu.VMEM((at_least(p - 1), groups, att_rows, D), BF),
            pltpu.VMEM((at_least(groups - 1), att_rows, D), BF),
            *[pltpu.VMEM((at_least(q), 8, D), F32) for q in hops],
            pltpu.VMEM((2, slots, part_len, D), BF),
            pltpu.VMEM((2, at_least(p - 1), slots, part_len, D), BF),
            dma((2, 7 * sum(hops))),
            dma((2, 2, most, n)),
            dma((2, 2, most, n)),
            dma((2, 2 * most)),
            dma((2, 2, max(p, 2))),
            dma((9,)),
        ],
        compiler_params=pltpu.CompilerParams(
            collective_id=2, has_side_effects=True, vmem_limit_bytes=VMEM
        ),
    )(*arrays)


def assemble_kernel(
    tab, out_in, enc_in, stream_in, att, ffn, norms,
    out, stream, enc, qkv, so, cq, ckv, co, ffn_in_grad, ffn_out_grad, gain, bias,
):
    i = pl.program_id(0)
    out[...] = out_in[...]
    stream[...] = stream_in[...].astype(F32)
    enc[...] = enc_in[...].astype(F32)
    plain = {2: so, 3: cq, 4: co, 5: qkv}
    turned = {0: ckv, 1: ckv, 6: qkv, 7: qkv}
    for step, ref in plain.items():

        @pl.when(i == step)
        def _(ref=ref):
            ref[...] = att[...].astype(F32)

    for step, ref in turned.items():

        @pl.when(i == step)
        def _(ref=ref):
            ref[...] = att[...].T.astype(F32)

    @pl.when(i == 8)
    def _():
        ffn_in_grad[...] = ffn[:D, :].astype(F32)
        ffn_out_grad[...] = ffn[D:, :].T.astype(F32)
        gain[...] = norms[:3, :]
        bias[...] = norms[3:6, :]


def assemble(slot_of, output, encoder_grad, stream_grad, att, ffn, norms):
    lines, piece = output.shape[:2]
    cols = ffn.shape[1]
    most = lines - 1
    line_in = pl.BlockSpec((1, piece, D), lambda i, t: (t[jnp.minimum(i, most)], 0, 0))
    line_out = pl.BlockSpec((1, piece, D), lambda i, t: (jnp.minimum(i, most), 0, 0))
    whole = lambda *shape: pl.BlockSpec(shape, lambda i, t: (0, 0), pipeline_mode=pl.Buffered(1))
    square = lambda at: pl.BlockSpec((D, D), lambda i, t: (0, at(i)))
    f32 = lambda *shape: sds(shape, F32)
    return pl.pallas_call(
        assemble_kernel,
        name="assemble",
        grid_spec=pltpu.PrefetchScalarGridSpec(
            num_scalar_prefetch=1,
            grid=(max(lines, 9),),
            in_specs=[
                line_in, line_in, line_in, pl.BlockSpec((D, D), lambda i, t: (jnp.minimum(i, 7), 0)),
                whole(2 * D, cols), whole(8, D),
            ],
            out_specs=[
                line_out, line_out, line_out,
                square(lambda i: jnp.clip(i - 5, 0, 2)),
                whole(D, D), whole(D, D),
                square(lambda i: jnp.minimum(i, 1)),
                whole(D, D), whole(D, cols), whole(cols, D), whole(3, D), whole(3, D),
            ],
        ),
        out_shape=[
            sds((lines, piece, D), BF), f32(lines, piece, D), f32(lines, piece, D), f32(D, 3 * D), f32(D, D),
            f32(D, D), f32(D, 2 * D), f32(D, D), f32(D, cols), f32(cols, D), f32(3, D), f32(3, D),
        ],
        compiler_params=pltpu.CompilerParams(
            vmem_limit_bytes=VMEM, dimension_semantics=("arbitrary",)
        ),
    )(slot_of, output, encoder_grad, stream_grad, att, ffn, norms)


def tables_kernel(lines, n, line_len, me_ref, len_ref, enc_ref, order, tab, docs):
    whole, p, k = plan(lines, n)
    part_len, slots, half = line_len // p, whole + k, 4
    widths = [wd for wd, _ in widths_for(line_len)]
    me = me_ref[0]
    group, part = me // p, part_of(me, p)
    size = (lines + 7) // 8 * 8
    fill = jnp.zeros((size - lines, len_ref.shape[1]), F32)
    pad = (lambda t: jnp.concatenate([t, fill])) if size > lines else (lambda t: t)
    target, source = pad(len_ref[...].astype(F32)), pad(enc_ref[...].astype(F32))

    row = lax.broadcasted_iota(jnp.int32, (size, 128), 0).astype(F32)
    lane = lax.broadcasted_iota(jnp.int32, (size, 128), 1).astype(F32)
    cost = jnp.broadcast_to(jnp.sum(target * target, axis=-1, keepdims=True), (size, 128))
    own = row == lane
    cost_lane = jnp.sum(jnp.where(own, cost, 0.0), axis=0, keepdims=True)
    lighter = (cost_lane < cost) | ((cost_lane == cost) & (lane < row))
    rank = jnp.sum(jnp.where(lighter & (lane < lines), 1.0, 0.0), axis=-1, keepdims=True)
    slot = jnp.where(rank < whole * n, rank, whole * n + lines - 1.0 - rank)
    slot = jnp.broadcast_to(slot, (size, 128))
    real = row < lines
    line_of = jnp.sum(jnp.where((slot == lane) & real, row, 0.0), axis=0, keepdims=True)
    slot_of = jnp.sum(jnp.where(own & real, slot, 0.0), axis=0, keepdims=True)
    order[...] = jnp.concatenate([line_of, slot_of, jnp.zeros((6, 128), F32)]).astype(jnp.int32)

    def lengths_of(table, j):
        at = whole * n + group * k + j if j < k else me * whole + (j - k)
        return jnp.sum(jnp.where((slot == at.astype(F32)) & real, table, 0.0), axis=0, keepdims=True)

    none = [jnp.zeros((1, 128), F32)] * (half - slots)
    sums = jnp.concatenate(
        [lengths_of(target, j) for j in range(slots)] + none + [lengths_of(source, j) for j in range(slots)] + none
    )
    lane8 = lax.broadcasted_iota(jnp.int32, (8, 128), 1)
    shift = 1
    while shift < 128:
        sums = sums + jnp.where(lane8 >= shift, pltpu.roll(sums, shift, 1), 0.0)
        shift *= 2
    columns = sums.T
    places = lax.broadcasted_iota(jnp.int32, (1, line_len), 1).astype(F32)
    zero = jnp.zeros((1, line_len), F32)
    for j in range(slots):
        count = lambda at: jnp.sum(
            jnp.where(columns[:, at : at + 1] <= places, 1.0, 0.0), axis=0, keepdims=True
        )
        docs[j] = jnp.concatenate([count(j), zero, zero, count(half + j), zero, zero, zero, zero])

    block_line = [j for j in range(k) for _ in range(part_len // BLOCK)]
    block_line += [k + j for j in range(whole) for _ in range(line_len // BLOCK)]
    block_row = [r * BLOCK for j in range(k) for r in range(part_len // BLOCK)]
    block_row += [r * BLOCK for j in range(whole) for r in range(line_len // BLOCK)]
    blocks = len(block_line)
    lane1 = lax.broadcasted_iota(jnp.int32, (1, 128), 1)
    rows = [jnp.zeros((1, 128), F32)] * 8
    for b in range(blocks):
        j = block_line[b]
        first = (jnp.int32(block_row[b]) + (part * part_len if j < k else 0)).astype(F32)
        bounds = sums[j : j + 1]
        before, after = bounds <= first, bounds > first + (BLOCK - 1.0)

        def key_range(ends):
            start = jnp.max(jnp.where(before, ends, 0.0), axis=-1, keepdims=True)
            stop = jnp.min(jnp.where(after, ends, float(line_len)), axis=-1, keepdims=True)
            ks = jnp.floor(start * (1.0 / ALIGN)) * ALIGN
            var, wd = jnp.zeros_like(ks), jnp.full_like(ks, widths[0])
            for at, width in enumerate(widths[:-1]):
                wider = stop - ks > width
                var = jnp.where(wider, at + 1.0, var)
                wd = jnp.where(wider, float(widths[at + 1]), wd)
            return jnp.minimum(ks, line_len - wd), var

        values = [
            float(j), first, float(b == 0 or block_line[b - 1] != j),
            float(b == blocks - 1 or block_line[b + 1] != j),
            *key_range(bounds), *key_range(sums[half + j : half + j + 1]),
        ]
        rows = [jnp.where(lane1 == b, value, r) for r, value in zip(rows, values)]
    tab[...] = jnp.concatenate(rows).astype(jnp.int32)


def tables(me, lengths, enc_lengths, lines, n, line_len):
    whole, _, k = plan(lines, n)
    vmem = pl.BlockSpec(memory_space=pltpu.VMEM)
    return pl.pallas_call(
        functools.partial(tables_kernel, lines, n, line_len),
        name="tables",
        in_specs=[pl.BlockSpec(memory_space=pltpu.SMEM), vmem, vmem],
        out_specs=[vmem] * 3,
        out_shape=[
            sds((8, 128), jnp.int32), sds((8, 128), jnp.int32), sds((whole + k, 8, line_len), F32),
        ],
    )(me.reshape(1).astype(jnp.int32), lengths, enc_lengths)


def body(
    stream, encoder, cotangent, self_qkv, self_out, cross_q, cross_kv, cross_out, ffn_in, ffn_out,
    norm_gain, norm_bias, lengths, enc_lengths, ranks, cuts,
):
    n = lax.axis_size("seq")
    lines, piece = stream.shape[0], stream.shape[1]
    line_len = piece * n
    order, tab, docs = tables(lax.axis_index("seq"), lengths, enc_lengths, lines, n, line_len)
    line_of, slot_of = order[0, :lines], order[1, :lines]

    rc_in = (ranks * 32 + cuts)[line_of][:, None, :]
    cot = cotangent[line_of]
    xs, rc, es, weights = exchange_in(
        stream[line_of], rc_in, encoder[line_of], ffn_in, ffn_out.T, lines, n, line_len, lax.axis_size("dp")
    )
    rc = rc.reshape(rc.shape[0], 1, line_len)
    row = jnp.arange(8)[None, :, None]
    mk = jnp.where(row == 1, (rc // 32).astype(F32), jnp.where(row == 2, (rc % 32).astype(F32), docs))

    output, *arrays = kernels(
        lines, n, tab, xs, es, cot, mk, self_qkv, self_out, cross_q, cross_kv, cross_out, weights, norm_gain, norm_bias
    )
    encoder_grad, stream_grad, ffn, att, norms = finish(
        arrays, lines, n, line_len, lax.axis_size("dp")
    )
    return tuple(assemble(slot_of, output, encoder_grad, stream_grad, att, ffn, norms))


def solution(mesh):
    lines = P("dp", "seq", None)
    in_specs = (
        lines, lines, lines, P(), P(), P(), P(), P(), P(None, "seq"), P("seq", None), P(), P(),
        P("dp", None), P("dp", None), P("dp", "seq"), P("dp", "seq"),
    )
    out_specs = (
        lines, lines, lines, P(), P(), P(), P(), P(), P(None, "seq"), P("seq", None), P(), P(),
    )
    return jax.shard_map(body, mesh=mesh, in_specs=in_specs, out_specs=out_specs, check_vma=False)
```
